32 devices in a mesh: segment: 4 (over z), tok: 4 (over y, x), head: 2 (over core).
Axes of the slice: x: 2, y: 2, z: 4, core: 2. Of those that a mesh axis runs over, the one named last changes fastest.
Arguments:
- stream: float32 [2, 512, 2048], P(None, 'tok', 'head'), may hold values from -6 to 6
- counts: int32 [4], replicated, may hold values from 1 to 2, as said below
- norm_gain: float32 [4, 2, 2048], P('segment'), may hold values from 0.5 to 1.5
- w_qkv: bfloat16 [4, 2, 2048, 3072], P('segment', None, None, 'head'), may hold values from -0.125 to 0.125
- w_out: bfloat16 [4, 2, 1024, 2048], P('segment', None, 'head'), may hold values from -0.1875 to 0.1875
- fast_init: float32 [4, 2, 2, 3, 512, 512], P('segment', None, 'head'), may hold values from -6 to 6
Outputs:
- section_out: float32 [4, 2, 512, 2048], P('segment', None, 'tok', 'head')
- fast_final: float32 [4, 2, 2, 3, 512, 512], P('segment', None, 'head', None, 'tok')
The draws below stay inside these ranges and needn't reach their ends.
Inputs may be any that keep to these rules, and one draw needn't show every extreme that they name: `counts`: every section runs either 1 or 2 layers; some section runs 2 layers and some other section runs 1.
All inputs are finite; a program needn't handle non-finite values.
Results may differ from the reference program's by a relative error of at most 0.03.
Values sent between devices are 32-bit elements; how exact they have to be, the bound alone decides.
No kernel may reach another device: no remote copies, remote signals or barrier semaphores. Data moves between devices by JAX's collectives and lax.ppermute only.
A program may use at most 128 MiB of HBM per device.

```python
import jax
import jax.numpy as jnp
from jax import lax

D = 2048
HEADS = 2
HD = 512
FH = 512
LMAX = 2
SPANS = 2
TOKENS = 512
N_SEGMENT = 4


def draw_counts(key, part):
    pattern_key = jax.random.fold_in(key, 71)
    pattern = jax.random.randint(pattern_key, (), 1, 2 ** N_SEGMENT - 1)
    powers = 2 ** jnp.arange(N_SEGMENT, dtype=jnp.int32)
    picked = pattern // powers % 2
    layer_counts = 1 + picked * (LMAX - 1)
    return layer_counts.astype(jnp.int32)


def levels(rng, dims, shards, least, largest):
    gain, own = 1.0, jax.random.fold_in(rng, 6)
    for dim, shards_of in shards:
        heights = jnp.exp(jax.random.uniform(jax.random.fold_in(own, dim), (shards_of,), jnp.float32, least / len(shards), largest / len(shards)))
        gain = gain * jnp.repeat(heights, dims[dim] // shards_of).reshape([-1 if axis == dim else 1 for axis in range(len(dims))])
    return gain


def normal_values(stream_key, shape, width, most, pieces=(), held_as=jnp.bfloat16):
    result = width * jax.random.normal(stream_key, shape, jnp.float32)
    if pieces:
        result = result * levels(stream_key, shape, pieces, -0.22, 0.18)
    return jnp.clip(result, -most, most).astype(held_as)


def setup_inputs(seed: int = 0) -> dict:
    arg_keys = jax.random.split(jax.random.key(seed), 7)
    stream = normal_values(arg_keys[0], (SPANS, TOKENS, D), 1.0, 6.0, ((1, 4), (2, 2)), jnp.float32)
    counts = draw_counts(jax.random.fold_in(arg_keys[6], 71), 0)
    norm_gain = jnp.clip(1.0 + 0.1 * jax.random.normal(arg_keys[2], (N_SEGMENT, LMAX, D), jnp.float32), 0.5, 1.5)
    w_qkv = normal_values(arg_keys[3], (N_SEGMENT, LMAX, D, HEADS * 3 * HD), D ** -0.5, 0.125, ((0, 4), (3, 2)))
    w_out = normal_values(arg_keys[4], (N_SEGMENT, LMAX, HEADS * HD, D), (HEADS * HD) ** -0.5, 0.1875, ((0, 4), (2, 2)))
    fast_init = normal_values(arg_keys[5], (N_SEGMENT, LMAX, HEADS, 3, HD, FH), 1.0, 6.0, ((0, 4), (2, 2)), jnp.float32)
    return dict(stream=stream, counts=counts, norm_gain=norm_gain, w_qkv=w_qkv, w_out=w_out, fast_init=fast_init)


step_rate = 0.5
tiny = 1e-06

def rms_scale(values):
    return lax.rsqrt(lax.optimization_barrier(jnp.mean(values * values, axis=-1, keepdims=True)) + tiny)

def round_half(values):
    return lax.optimization_barrier(values.astype(jnp.bfloat16)).astype(jnp.float32)

def silu_slope(pre_gate):
    logistic = jax.nn.sigmoid(pre_gate)
    return logistic * (1.0 + pre_gate * (1.0 - logistic))

def contract(form, left, right):
    return jnp.einsum(form, left, right, precision=lax.Precision.HIGHEST)

def run_layer(rows_in, gain_row, qkv_layer, out_layer, fast_layer):
    token_count = rows_in.shape[0]
    widened = rows_in.astype(jnp.float32)
    normed = (widened * rms_scale(widened) * gain_row).astype(jnp.bfloat16)
    projected = round_half(jnp.dot(normed, qkv_layer, preferred_element_type=jnp.float32))
    projected = projected.reshape(token_count, HEADS, 3, HD)
    query_rows = projected[:, :, 0]
    key_rows = projected[:, :, 1]
    value_rows = projected[:, :, 2]
    head_scale = HD ** (-0.5)
    weights = round_half(fast_layer)
    w_first = weights[:, 0]
    w_third = weights[:, 1]
    w_second = weights[:, 2]
    gate_query = contract('thd,hdf->thf', query_rows, w_first) * head_scale
    lift_query = contract('thd,hdf->thf', query_rows, w_third) * head_scale
    hidden_query = round_half(jax.nn.silu(gate_query) * lift_query)
    answer = contract('thf,hdf->thd', hidden_query, w_second) * head_scale
    normed_out = round_half(answer * rms_scale(answer))
    flat_out = normed_out.reshape(token_count, HEADS * HD)
    summed = contract('tk,kd->td', flat_out, out_layer.astype(jnp.float32))
    rows_out = widened + summed
    gate_key = contract('thd,hdf->thf', key_rows, w_first) * head_scale
    lift_key = contract('thd,hdf->thf', key_rows, w_third) * head_scale
    gate_act = jax.nn.silu(gate_key)
    hidden_key = round_half(gate_act * lift_key)
    upstream = -head_scale * contract('thd,hdf->thf', value_rows, w_second)
    grad_gate = round_half(upstream * lift_key * silu_slope(gate_key))
    grad_lift = round_half(upstream * gate_act)
    grad_first = head_scale * contract('thd,thf->hdf', key_rows, grad_gate)
    grad_third = head_scale * contract('thd,thf->hdf', key_rows, grad_lift)
    grad_second = -head_scale * contract('thd,thf->hdf', value_rows, hidden_key)
    grad_total = jnp.stack([grad_first, grad_third, grad_second], axis=1)
    mean_square = lax.optimization_barrier(jnp.mean(grad_total * grad_total, axis=(2, 3), keepdims=True))
    updated = fast_layer - step_rate * grad_total * lax.rsqrt(mean_square + tiny)
    return (rows_out, updated)

def reference(stream, counts, norm_gain, w_qkv, w_out, fast_init):
    fast_states = [fast_init[index] for index in range(N_SEGMENT)]
    produced = [[] for index in range(N_SEGMENT)]
    for span_index in range(SPANS):
        rows_now = stream[span_index]
        for segment_index in range(N_SEGMENT):
            gains = norm_gain[segment_index]
            qkv_weights = w_qkv[segment_index]
            out_weights = w_out[segment_index]

            def layer_step(layer_index, state_pair):
                rows_in, fast_state = state_pair
                gain_row = lax.dynamic_index_in_dim(gains, layer_index, 0, keepdims=False)
                qkv_layer = lax.dynamic_index_in_dim(qkv_weights, layer_index, 0, keepdims=False)
                out_layer = lax.dynamic_index_in_dim(out_weights, layer_index, 0, keepdims=False)
                fast_layer = lax.dynamic_index_in_dim(fast_state, layer_index, 0, keepdims=False)
                rows_out, updated = run_layer(rows_in, gain_row, qkv_layer, out_layer, fast_layer)
                fast_state = lax.dynamic_update_index_in_dim(fast_state, updated, layer_index, 0)
                return (rows_out, fast_state)
            rows_now, fast_states[segment_index] = lax.fori_loop(0, counts[segment_index], layer_step, (rows_now, fast_states[segment_index]))
            produced[segment_index].append(rows_now)
    section_out = jnp.stack([jnp.stack(span_rows) for span_rows in produced])
    fast_final = jnp.stack(fast_states)
    return (section_out, fast_final)
```

```python
import functools

import jax
import jax.numpy as jnp
from jax import lax
from jax.experimental import pallas as pl
from jax.experimental.pallas import tpu as pltpu
from jax.sharding import PartitionSpec as P

STEP_RATE = 0.5
TINY = 1e-06
AXES = ("segment", "tok", "head")
KERNEL_VMEM = 40 * 1024 * 1024
CHUNK_TOKENS = 512

VMEM = pl.BlockSpec(memory_space=pltpu.VMEM)
SMEM = pl.BlockSpec(memory_space=pltpu.SMEM)


def dot(left, right):
    return jnp.dot(left, right, preferred_element_type=jnp.float32)


def dot_over_rows(left, right):
    return lax.dot_general(
        left, right, (((0,), (0,)), ((), ())), preferred_element_type=jnp.float32
    )


def is_active(step, spans):
    segment = lax.axis_index("segment")
    return (segment <= step) & (segment > step - spans)


def forward_kernel(step, layer, spans, last, entry, *refs):
    if layer > 0:
        counts, held, mine, theirs, gain, w_query, w_out, fast = refs[:8]
        outs = refs[8:]
    elif entry == "both":
        counts, own, other, first_own, first_other, gain, w_query, w_out, fast = refs[:9]
        outs = refs[9:]
    else:
        counts, own, other, gain, w_query, w_out, fast = refs[:7]
        outs = refs[7:]
    rows, normed = outs[:2]
    active = is_active(step, spans)
    segment = lax.axis_index("segment")
    head = lax.axis_index("head")
    run = active & (layer < counts[segment])

    @pl.when(active)
    def _():
        if layer > 0:
            rows[0] = held[0] + (mine[0] + theirs[1])
            rows[1] = held[1] + (mine[1] + theirs[0])
        elif entry == "both":
            at_first = segment == 0

            @pl.when(at_first)
            def _():
                rows[0] = first_own[...]
                rows[1] = first_other[...]

            @pl.when(jnp.logical_not(at_first))
            def _():
                rows[0] = own[...]
                rows[1] = other[...]
        else:
            rows[0] = own[...]
            rows[1] = other[...]

    @pl.when(run)
    def _():
        half = rows.shape[2]
        squares = jnp.sum(rows[0] * rows[0], axis=-1, keepdims=True)
        squares = squares + jnp.sum(rows[1] * rows[1], axis=-1, keepdims=True)
        scale = lax.rsqrt(squares / (2 * half) + TINY)
        normed[0] = (rows[0] * scale * gain[pl.ds(head, 1)]).astype(jnp.bfloat16)
        normed[1] = (rows[1] * scale * gain[pl.ds(1 - head, 1)]).astype(jnp.bfloat16)
        query = dot(normed[0], w_query[head]) + dot(normed[1], w_query[1 - head])
        query = query.astype(jnp.bfloat16)
        head_scale = query.shape[1] ** -0.5
        gate = dot(query, fast[0]) * head_scale
        lift = dot(query, fast[1]) * head_scale
        hidden = (gate * jax.nn.sigmoid(gate) * lift).astype(jnp.bfloat16)
        answer = (
            lax.dot_general(
                hidden, fast[2], (((1,), (1,)), ((), ())), preferred_element_type=jnp.float32
            )
            * head_scale
        )
        mean = jnp.mean(answer * answer, axis=-1, keepdims=True)
        answer = (answer * lax.rsqrt(mean + TINY)).astype(jnp.bfloat16)
        keep_at = pl.multiple_of(head * half, half)
        send_at = pl.multiple_of((1 - head) * half, half)
        if last:
            outs[2][...] = dot(answer, w_out[:, pl.ds(keep_at, half)])
            outs[3][...] = dot(answer, w_out[:, pl.ds(send_at, half)])
        else:
            outs[2][0] = dot(answer, w_out[:, pl.ds(keep_at, half)])
            outs[2][1] = dot(answer, w_out[:, pl.ds(send_at, half)])


def forward(step, layer, spans, last, entry, args, tokens, half):
    rows = jax.ShapeDtypeStruct((2, tokens, half), jnp.float32)
    normed = jax.ShapeDtypeStruct((2, tokens, half), jnp.bfloat16)
    part = jax.ShapeDtypeStruct((tokens, half), jnp.float32)
    return pl.pallas_call(
        functools.partial(forward_kernel, step, layer, spans, last, entry),
        out_shape=(rows, normed) + ((part, part) if last else (rows,)),
        in_specs=[SMEM] + [VMEM] * (len(args) - 1),
        out_specs=[VMEM] * (4 if last else 3),
        compiler_params=pltpu.CompilerParams(vmem_limit_bytes=KERNEL_VMEM),
        name=f"forward_s{step}_l{layer}",
    )(*args)


def key_value_kernel(step, layer, spans, counts, normed, w_key_value, out):
    head = lax.axis_index("head")
    run = is_active(step, spans) & (layer < counts[lax.axis_index("segment")])

    @pl.when(run)
    def _():
        made = dot(normed[0], w_key_value[head]) + dot(normed[1], w_key_value[1 - head])
        out[...] = made.astype(jnp.bfloat16).astype(jnp.float32)


def key_value(step, layer, spans, counts, normed, w_key_value):
    return pl.pallas_call(
        functools.partial(key_value_kernel, step, layer, spans),
        out_shape=jax.ShapeDtypeStruct((normed.shape[1], w_key_value.shape[2]), jnp.float32),
        in_specs=[SMEM, VMEM, VMEM],
        out_specs=VMEM,
        compiler_params=pltpu.CompilerParams(vmem_limit_bytes=KERNEL_VMEM),
        name=f"keyvalue_s{step}_l{layer}",
    )(counts, normed, w_key_value)


def update_kernel(step, layer, spans, n_pieces, counts, *refs):
    pieces = refs[:n_pieces]
    fast, fast_new, rounded, keys, values = refs[n_pieces:]
    run = is_active(step, spans) & (layer < counts[lax.axis_index("segment")])
    head_size = fast.shape[1]
    head_scale = head_size**-0.5

    @pl.when(run)
    def _():
        start = 0
        for piece in pieces:
            count = piece.shape[0]
            keys[start : start + count] = piece[:, :head_size].astype(jnp.bfloat16)
            values[start : start + count] = piece[:, head_size:].astype(jnp.bfloat16)
            start += count
        rounded[...] = fast[...].astype(jnp.bfloat16)
        total = keys.shape[0]
        chunk = min(total, CHUNK_TOKENS)
        sums = [0.0, 0.0, 0.0]
        for at in range(0, total, chunk):
            key_rows = keys[at : at + chunk]
            value_rows = values[at : at + chunk]
            gate = dot(key_rows, rounded[0]) * head_scale
            lift = dot(key_rows, rounded[1]) * head_scale
            up = dot(value_rows, rounded[2]) * -head_scale
            logistic = jax.nn.sigmoid(gate)
            act = gate * logistic
            hidden = (act * lift).astype(jnp.bfloat16)
            slope = logistic * (1.0 + gate * (1.0 - logistic))
            grad_gate = (up * lift * slope).astype(jnp.bfloat16)
            grad_lift = (up * act).astype(jnp.bfloat16)
            sums[0] += dot_over_rows(key_rows, grad_gate)
            sums[1] += dot_over_rows(key_rows, grad_lift)
            sums[2] += dot_over_rows(value_rows, hidden)
        for index, sign in enumerate((head_scale, head_scale, -head_scale)):
            grad = sums[index] * sign
            mean = jnp.mean(grad * grad)
            moved = fast[index] - STEP_RATE * grad * lax.rsqrt(mean + TINY)
            fast_new[index] = moved
            rounded[index] = moved.astype(jnp.bfloat16)

    @pl.when(jnp.logical_not(run))
    def _():
        fast_new[...] = fast[...]
        rounded[...] = fast[...].astype(jnp.bfloat16)


def update(step, layer, spans, counts, pieces, fast):
    total = sum(piece.shape[0] for piece in pieces)
    head_size = fast.shape[1]
    return pl.pallas_call(
        functools.partial(update_kernel, step, layer, spans, len(pieces)),
        out_shape=(
            jax.ShapeDtypeStruct(fast.shape, jnp.float32),
            jax.ShapeDtypeStruct(fast.shape, jnp.bfloat16),
        ),
        in_specs=[SMEM] + [VMEM] * (len(pieces) + 1),
        out_specs=[VMEM, VMEM],
        scratch_shapes=[pltpu.VMEM((total, head_size), jnp.bfloat16)] * 2,
        compiler_params=pltpu.CompilerParams(vmem_limit_bytes=KERNEL_VMEM),
        name=f"update_s{step}_l{layer}",
    )(counts, *pieces, fast)


def make_send(sections):
    tok_size = lax.axis_size("tok")
    head_size = lax.axis_size("head")

    def flat(segment, tok, head):
        return (segment * tok_size + tok) * head_size + head

    def send(block, move):
        route = []
        for segment in sections:
            for tok in range(tok_size):
                for head in range(head_size):
                    target = move(segment, tok, head)
                    if target is not None:
                        route.append((flat(segment, tok, head), flat(*target)))
        return lax.ppermute(block, AXES, route)

    return send


def swap_head(send, block):
    return send(block, lambda s, k, h: (s, k, 1 - h))


def gather_tokens(send, block):
    if lax.axis_size("tok") != 4:
        whole = lax.all_gather(block, "tok", axis=0, tiled=True)
        return [whole]
    cut = block.shape[0] // 2
    from_first = send(block, lambda s, k, h: (s, k ^ 1, h))
    from_second = send(block, lambda s, k, h: (s, k ^ 2, h))
    corner_top = send(from_first[:cut], lambda s, k, h: (s, k ^ 2, h))
    corner_low = send(from_second[cut:], lambda s, k, h: (s, k ^ 1, h))
    return [block, from_first, from_second, corner_top, corner_low]


def body(stream, counts, norm_gain, w_qkv, w_out, fast_init):
    segments = lax.axis_size("segment")
    segment = lax.axis_index("segment")
    spans, tokens, half = stream.shape
    slots = fast_init.shape[1]
    head_size = fast_init.shape[4]
    gains = [norm_gain[0, layer].reshape(2, half) for layer in range(slots)]
    w_query = [
        w_qkv[0, layer, :, :head_size].reshape(2, half, head_size) for layer in range(slots)
    ]
    w_key_value = [
        w_qkv[0, layer, :, head_size:].reshape(2, half, 2 * head_size) for layer in range(slots)
    ]
    w_outs = [w_out[0, layer] for layer in range(slots)]
    fasts = [fast_init[0, layer, 0] for layer in range(slots)]
    rounded = [fast.astype(jnp.bfloat16) for fast in fasts]
    my_count = lax.dynamic_index_in_dim(counts, segment, 0, keepdims=False)

    made = []
    arrived = None
    for step in range(segments + spans - 1):
        sections = [s for s in range(segments) if 0 <= step - s < spans]
        send = make_send(sections)
        entries = []
        if step > 0:
            entries += [arrived, swap_head(send, arrived)]
        if step < spans:
            entries += [stream[step], swap_head(make_send([0]), stream[step])]
        entry = "both" if len(entries) == 4 else "one"
        state = entries
        for layer in range(slots):
            last = layer == slots - 1
            args = [counts] + state + [gains[layer], w_query[layer], w_outs[layer], rounded[layer]]
            results = forward(step, layer, spans, last, entry, args, tokens, half)
            rows, normed = results[:2]
            if last:
                keep, give = results[2:]
                got = swap_head(send, give)
                grown = jnp.where(layer < my_count, rows[0] + (keep + got), rows[0])
            else:
                mine = results[2]
                theirs = swap_head(send, mine)
                state = [rows, mine, theirs]
            block = key_value(step, layer, spans, counts, normed, w_key_value[layer])
            pieces = gather_tokens(send, block)
            fasts[layer], rounded[layer] = update(
                step, layer, spans, counts, pieces, fasts[layer]
            )
        made.append(grown)
        if step < segments + spans - 2:
            arrived = send(
                grown, lambda s, k, h: (s + 1, k, h) if s + 1 < segments else None
            )
    outs = []
    for span in range(spans):
        chosen = made[span]
        for index in range(1, segments):
            chosen = jnp.where(segment == index, made[span + index], chosen)
        outs.append(chosen)
    row_share = head_size // lax.axis_size("tok")
    row_start = lax.axis_index("tok") * row_share
    own_rows = [lax.dynamic_slice_in_dim(fast, row_start, row_share, 1) for fast in fasts]
    return (jnp.stack(outs)[None], jnp.stack(own_rows)[None, :, None])


def solution(mesh):
    in_specs = (
        P(None, "tok", "head"),
        P(),
        P("segment", None, None),
        P("segment", None, None, "head"),
        P("segment", None, "head", None),
        P("segment", None, "head", None, None, None),
    )
    out_specs = (P("segment", None, "tok", "head"), P("segment", None, "head", None, "tok", None))
    return jax.shard_map(body, mesh=mesh, in_specs=in_specs, out_specs=out_specs, check_vma=False)
```

```python
import functools

import jax
import jax.numpy as jnp
from jax import lax
from jax.experimental import pallas as pl
from jax.experimental.pallas import tpu as pltpu
from jax.sharding import PartitionSpec as P

STEP_RATE = 0.5
TINY = 1e-06
AXES = ("segment", "tok", "head")
MIB = 1024 * 1024
FORWARD_VMEM = 8 * MIB
KEY_VALUE_VMEM = 4 * MIB
UPDATE_VMEM = 28 * MIB
CHUNK_TOKENS = 512

VMEM = pl.BlockSpec(memory_space=pltpu.VMEM)
SMEM = pl.BlockSpec(memory_space=pltpu.SMEM)
ANY = pl.BlockSpec(memory_space=pl.ANY)
SMALL_COST = pl.CostEstimate(flops=1024, bytes_accessed=1024, transcendentals=0)


def dot(left, right):
    return jnp.dot(left, right, preferred_element_type=jnp.float32)


def dot_over_rows(left, right):
    return lax.dot_general(
        left, right, (((0,), (0,)), ((), ())), preferred_element_type=jnp.float32
    )


def is_active(step, spans):
    segment = lax.axis_index("segment")
    return (segment <= step) & (segment > step - spans)


def forward_kernel(step, layer, spans, last, entry, n_after, *refs):
    counts, refs = refs[0], refs[1:]
    if layer > 0:
        held, mine, theirs = refs[:3]
        refs = refs[3:]
    elif entry == "both":
        own, other, first_own, first_other = refs[:4]
        refs = refs[4:]
    else:
        own, other = refs[:2]
        refs = refs[2:]
    gains, w_qkv, w_out, fast = refs[:4]
    outs = refs[4 + n_after :]
    rows, normed = outs[:2]
    segment = lax.axis_index("segment")
    head = lax.axis_index("head")
    active = is_active(step, spans)
    run = active & (layer < counts[segment])

    @pl.when(active)
    def _():
        if layer > 0:
            rows[0] = held[0] + (mine[0] + theirs[1])
            rows[1] = held[1] + (mine[1] + theirs[0])
        elif entry == "both":
            at_first = segment == 0

            @pl.when(at_first)
            def _():
                rows[0] = first_own[...]
                rows[1] = first_other[...]

            @pl.when(jnp.logical_not(at_first))
            def _():
                rows[0] = own[...]
                rows[1] = other[...]
        else:
            rows[0] = own[...]
            rows[1] = other[...]

    @pl.when(run)
    def _():
        half = rows.shape[2]
        head_size = fast.shape[-2]
        keep_at = pl.multiple_of(head * half, half)
        send_at = pl.multiple_of((1 - head) * half, half)
        squares = jnp.sum(rows[0] * rows[0], axis=-1, keepdims=True)
        squares = squares + jnp.sum(rows[1] * rows[1], axis=-1, keepdims=True)
        scale = lax.rsqrt(squares / (2 * half) + TINY)
        gain_keep = gains[0, layer : layer + 1, pl.ds(keep_at, half)]
        gain_send = gains[0, layer : layer + 1, pl.ds(send_at, half)]
        normed[0] = (rows[0] * scale * gain_keep).astype(jnp.bfloat16)
        normed[1] = (rows[1] * scale * gain_send).astype(jnp.bfloat16)
        query = dot(normed[0], w_qkv[0, layer, pl.ds(keep_at, half), :head_size])
        query += dot(normed[1], w_qkv[0, layer, pl.ds(send_at, half), :head_size])
        query = query.astype(jnp.bfloat16)
        head_scale = head_size**-0.5
        gate = dot(query, pick(fast, layer, 0).astype(jnp.bfloat16)) * head_scale
        lift = dot(query, pick(fast, layer, 1).astype(jnp.bfloat16)) * head_scale
        hidden = (gate * jax.nn.sigmoid(gate) * lift).astype(jnp.bfloat16)
        answer = (
            lax.dot_general(
                hidden,
                pick(fast, layer, 2).astype(jnp.bfloat16),
                (((1,), (1,)), ((), ())),
                preferred_element_type=jnp.float32,
            )
            * head_scale
        )
        mean = jnp.mean(answer * answer, axis=-1, keepdims=True)
        answer = (answer * lax.rsqrt(mean + TINY)).astype(jnp.bfloat16)
        kept = dot(answer, w_out[0, layer, :, pl.ds(keep_at, half)])
        given = dot(answer, w_out[0, layer, :, pl.ds(send_at, half)])
        if last:
            outs[2][...] = kept
            outs[3][...] = given
        else:
            outs[2][0] = kept
            outs[2][1] = given


def pick(fast, layer, kind):
    return fast[0, layer, 0, kind] if len(fast.shape) == 6 else fast[kind]


def forward(step, layer, spans, last, entry, args, after, tokens, half):
    rows = jax.ShapeDtypeStruct((2, tokens, half), jnp.float32)
    normed = jax.ShapeDtypeStruct((2, tokens, half), jnp.bfloat16)
    part = jax.ShapeDtypeStruct((tokens, half), jnp.float32)
    return pl.pallas_call(
        functools.partial(forward_kernel, step, layer, spans, last, entry, len(after)),
        out_shape=(rows, normed) + ((part, part) if last else (rows,)),
        in_specs=[SMEM] + [VMEM] * (len(args) - 1) + [ANY] * len(after),
        out_specs=[VMEM] * (4 if last else 3),
        cost_estimate=SMALL_COST,
        compiler_params=pltpu.CompilerParams(vmem_limit_bytes=FORWARD_VMEM),
        name=f"forward_s{step}_l{layer}",
    )(*args, *after)


def key_value_kernel(step, layer, spans, n_after, counts, normed, w_qkv, *refs):
    out = refs[n_after]
    head = lax.axis_index("head")
    run = is_active(step, spans) & (layer < counts[lax.axis_index("segment")])

    @pl.when(run)
    def _():
        half = normed.shape[2]
        keep_at = pl.multiple_of(head * half, half)
        send_at = pl.multiple_of((1 - head) * half, half)
        begin = w_qkv.shape[3] - out.shape[1]
        made = dot(normed[0], w_qkv[0, layer, pl.ds(keep_at, half), begin:])
        made += dot(normed[1], w_qkv[0, layer, pl.ds(send_at, half), begin:])
        out[...] = made.astype(jnp.bfloat16).astype(jnp.float32)


def key_value(step, layer, spans, counts, normed, w_qkv, width, after):
    return pl.pallas_call(
        functools.partial(key_value_kernel, step, layer, spans, len(after)),
        out_shape=jax.ShapeDtypeStruct((normed.shape[1], width), jnp.float32),
        in_specs=[SMEM, VMEM, VMEM] + [ANY] * len(after),
        out_specs=VMEM,
        cost_estimate=SMALL_COST,
        compiler_params=pltpu.CompilerParams(vmem_limit_bytes=KEY_VALUE_VMEM),
        name=f"keyvalue_s{step}_l{layer}",
    )(counts, normed, w_qkv, *after)


def finish_kernel(step, spans, layer, n_after, counts, rows, keep, got, *refs):
    grown = refs[n_after]
    segment = lax.axis_index("segment")
    active = is_active(step, spans)

    @pl.when(active & (layer < counts[segment]))
    def _():
        grown[...] = rows[0] + (keep[...] + got[...])

    @pl.when(active & (layer >= counts[segment]))
    def _():
        grown[...] = rows[0]


def finish(step, spans, layer, counts, rows, keep, got, after):
    return pl.pallas_call(
        functools.partial(finish_kernel, step, spans, layer, len(after)),
        out_shape=jax.ShapeDtypeStruct(keep.shape, jnp.float32),
        in_specs=[SMEM] + [VMEM] * 3 + [ANY] * len(after),
        out_specs=VMEM,
        cost_estimate=SMALL_COST,
        compiler_params=pltpu.CompilerParams(vmem_limit_bytes=KEY_VALUE_VMEM),
        name=f"finish_s{step}",
    )(counts, rows, keep, got, *after)


def place_kernel(segments, spans, *refs):
    made, out, arrivals = refs[:-2], refs[-2], refs[-1]
    for index in range(segments):

        @pl.when(lax.axis_index("segment") == index)
        def _():
            copies = [
                pltpu.make_async_copy(made[index + span], out.at[span], arrivals.at[span])
                for span in range(spans)
            ]
            for copy in copies:
                copy.start()
            for copy in copies:
                copy.wait()


def place(made, segments, spans):
    return pl.pallas_call(
        functools.partial(place_kernel, segments, spans),
        out_shape=jax.ShapeDtypeStruct((spans,) + made[0].shape, jnp.float32),
        in_specs=[ANY] * len(made),
        out_specs=ANY,
        scratch_shapes=[pltpu.SemaphoreType.DMA((spans,))],
        cost_estimate=SMALL_COST,
        compiler_params=pltpu.CompilerParams(vmem_limit_bytes=KEY_VALUE_VMEM),
        name="place",
    )(*made)


def update_kernel(layer, n_pieces, fast_all, *refs):
    pieces = refs[:n_pieces]
    fast_new, fast, keys, values, rounded, arrival = refs[n_pieces:]
    source = fast_all.at[0, layer, 0] if len(fast_all.shape) == 6 else fast_all
    fetch = pltpu.make_async_copy(source, fast, arrival)
    fetch.start()
    head_size = keys.shape[1]
    head_scale = head_size**-0.5
    begin = 0
    for piece in pieces:
        at = slice(begin, begin + piece.shape[0])
        keys[at] = piece[:, :head_size].astype(jnp.bfloat16)
        values[at] = piece[:, head_size:].astype(jnp.bfloat16)
        begin += piece.shape[0]
    fetch.wait()
    for index in range(3):
        rounded[index] = fast[index].astype(jnp.bfloat16)
    total = keys.shape[0]
    chunk = min(total, CHUNK_TOKENS)
    sums = [0.0, 0.0, 0.0]
    for begin in range(0, total, chunk):
        key_rows = keys[begin : begin + chunk]
        value_rows = values[begin : begin + chunk]
        gate = dot(key_rows, rounded[0]) * head_scale
        lift = dot(key_rows, rounded[1]) * head_scale
        up = dot(value_rows, rounded[2]) * -head_scale
        logistic = jax.nn.sigmoid(gate)
        act = gate * logistic
        hidden = (act * lift).astype(jnp.bfloat16)
        slope = logistic * (1.0 + gate * (1.0 - logistic))
        grad_gate = (up * lift * slope).astype(jnp.bfloat16)
        grad_lift = (up * act).astype(jnp.bfloat16)
        sums[0] += dot_over_rows(key_rows, grad_gate)
        sums[1] += dot_over_rows(key_rows, grad_lift)
        sums[2] += dot_over_rows(value_rows, hidden)
    tok_size = head_size // fast_new.shape[1]
    share = fast_new.shape[1]
    for index, sign in enumerate((head_scale, head_scale, -head_scale)):
        grad = sums[index] * sign
        mean = jnp.mean(grad * grad)
        rate = STEP_RATE * lax.rsqrt(mean + TINY)
        if tok_size == 1:
            fast_new[index] = fast[index] - grad * rate
        else:
            fast[index] = fast[index] - grad * rate
            begin = pl.multiple_of(lax.axis_index("tok") * share, share)
            fast_new[index] = fast[index, pl.ds(begin, share)]


def update(layer, pieces, fast, share):
    total = sum(piece.shape[0] for piece in pieces)
    shape = fast.shape[-3:]
    return pl.pallas_call(
        functools.partial(update_kernel, layer, len(pieces)),
        out_shape=jax.ShapeDtypeStruct((shape[0], share, shape[2]), jnp.float32),
        in_specs=[ANY] + [VMEM] * len(pieces),
        out_specs=VMEM,
        scratch_shapes=[
            pltpu.VMEM(shape, jnp.float32),
            pltpu.VMEM((total, shape[1]), jnp.bfloat16),
            pltpu.VMEM((total, shape[1]), jnp.bfloat16),
            pltpu.VMEM(shape, jnp.bfloat16),
            pltpu.SemaphoreType.DMA,
        ],
        cost_estimate=SMALL_COST,
        compiler_params=pltpu.CompilerParams(vmem_limit_bytes=UPDATE_VMEM),
        name=f"update_l{layer}",
    )(fast, *pieces)


def make_send(sections):
    tok_size = lax.axis_size("tok")
    head_size = lax.axis_size("head")

    def flat(segment, tok, head):
        return (segment * tok_size + tok) * head_size + head

    def send(block, move):
        route = []
        for segment in sections:
            for tok in range(tok_size):
                for head in range(head_size):
                    target = move(segment, tok, head)
                    if target is not None:
                        route.append((flat(segment, tok, head), flat(*target)))
        return lax.ppermute(block, AXES, route)

    return send


def swap_head(send, block):
    return send(block, lambda s, k, h: (s, k, 1 - h))


def gather_near(send, block):
    if lax.axis_size("tok") != 4:
        return [lax.all_gather(block, "tok", axis=0, tiled=True)]
    first = send(block, lambda s, k, h: (s, k ^ 1, h))
    second = send(block, lambda s, k, h: (s, k ^ 2, h))
    return [block, first, second]


def gather_far(send, near):
    if len(near) == 1:
        return near
    cut = near[0].shape[0] // 2
    top = send(near[1][:cut], lambda s, k, h: (s, k ^ 2, h))
    low = send(near[2][cut:], lambda s, k, h: (s, k ^ 1, h))
    return near + [top, low]


def one_layer(fast, layer):
    return fast[0, layer, 0] if len(fast.shape) == 6 else fast


def body(stream, counts, norm_gain, w_qkv, w_out, fast_init):
    segments = lax.axis_size("segment")
    segment = lax.axis_index("segment")
    spans, tokens, half = stream.shape
    slots = fast_init.shape[1]
    head_size = fast_init.shape[4]
    fasts = [fast_init for layer in range(slots)]
    steps = segments + spans - 1
    count = lax.dynamic_index_in_dim(counts, segment, 0, keepdims=False)
    row_share = head_size // lax.axis_size("tok")
    row_start = lax.axis_index("tok") * row_share

    def own_rows(fast, layer):
        return lax.dynamic_slice_in_dim(one_layer(fast, layer), row_start, row_share, 1)

    def update_branch(depth, send):
        def run(near, blocks, fasts):
            near = near + [gather_near(send, block) for block in blocks[: depth - len(near)]]
            changed = [
                update(k, gather_far(send, near[k]), fasts[k], head_size) for k in range(depth)
            ]
            return changed + [one_layer(fasts[k], k) for k in range(depth, slots)]

        return run

    def final_branch(depth, send):
        def run(near, blocks, fasts):
            if depth > 0:
                near = near + [gather_near(send, block) for block in blocks[: depth - 1]]
            changed = [
                update(k, gather_far(send, near[k]), fasts[k], row_share) for k in range(depth)
            ]
            return changed + [own_rows(fasts[k], k) for k in range(depth, slots)]

        return run

    grown_all = []
    own = stream[0]
    for step in range(steps):
        send = make_send([s for s in range(segments) if 0 <= step - s < spans])
        final = step == steps - 1
        active = (segment <= step) & (segment > step - spans)
        depth = jnp.where(active, count, 0)
        state = [own, swap_head(send, own)]
        blocks = []
        near = []
        for layer in range(slots):
            last = layer == slots - 1
            args = [counts] + state + [norm_gain, w_qkv, w_out, fasts[layer]]
            made = forward(
                step, layer, spans, last, "one", args, blocks[-1:], tokens, half
            )
            rows, normed = made[:2]
            got = swap_head(send, made[3] if last else made[2])
            state = [rows, made[2], got]
            blocks.append(
                key_value(step, layer, spans, counts, normed, w_qkv, 2 * head_size, [])
            )
            if final and layer == 0:
                near.append(gather_near(send, blocks[0]))
        grown = finish(step, spans, slots - 1, counts, *state, blocks[-1:])
        grown_all.append(grown)
        if final:
            branches = [final_branch(k, send) for k in range(slots + 1)]
            rows = lax.switch(depth, branches, near, blocks[1:], fasts)
            break
        arrived = send(grown, lambda s, k, h: (s + 1, k, h) if s + 1 < segments else None)
        branches = [update_branch(k, send) for k in range(slots + 1)]
        fasts = lax.switch(depth, branches, [], blocks, fasts)
        own, fasts = lax.optimization_barrier((arrived, fasts))
        if step + 1 < spans:
            own = jnp.where(segment == 0, stream[step + 1], own)
    results = place(grown_all, segments, spans)
    return (results[None], jnp.stack(rows)[None, :, None])


def solution(mesh):
    in_specs = (
        P(None, "tok", "head"),
        P(),
        P("segment", None, None),
        P("segment", None, None, "head"),
        P("segment", None, "head", None),
        P("segment", None, "head", None, None, None),
    )
    out_specs = (P("segment", None, "tok", "head"), P("segment", None, "head", None, "tok", None))
    return jax.shard_map(body, mesh=mesh, in_specs=in_specs, out_specs=out_specs, check_vma=False)
```

```python
import functools

import jax
import jax.numpy as jnp
from jax import lax
from jax.experimental import pallas as pl
from jax.experimental.pallas import tpu as pltpu
from jax.sharding import PartitionSpec as P

STEP_RATE = 0.5
TINY = 1e-06
AXES = ("segment", "tok", "head")
MIB = 1024 * 1024
FORWARD_VMEM = 48 * MIB
KEY_VALUE_VMEM = 4 * MIB
UPDATE_VMEM = 28 * MIB
CHUNK_TOKENS = 512

VMEM = pl.BlockSpec(memory_space=pltpu.VMEM)
SMEM = pl.BlockSpec(memory_space=pltpu.SMEM)
ANY = pl.BlockSpec(memory_space=pl.ANY)
HBM = pl.BlockSpec(memory_space=pltpu.HBM)
SMALL_COST = pl.CostEstimate(flops=1024, bytes_accessed=1024, transcendentals=0)


def dot(left, right):
    return jnp.dot(left, right, preferred_element_type=jnp.float32)


def dot_over_rows(left, right):
    return lax.dot_general(
        left, right, (((0,), (0,)), ((), ())), preferred_element_type=jnp.float32
    )


def is_active(step, spans):
    segment = lax.axis_index("segment")
    return (segment <= step) & (segment > step - spans)


def fetch(source, target, arrival):
    copy = pltpu.make_async_copy(source, target, arrival)
    copy.start()
    return copy


def forward_kernel(step, layer, spans, last, n_after, *refs):
    counts, refs = refs[0], refs[1:]
    n_enter = 3 if layer > 0 else 2
    entering, refs = refs[:n_enter], refs[n_enter:]
    gains, w_qkv, w_out, fast = refs[:4]
    outs, scratch = refs[4 + n_after : -4], refs[-4:]
    w_query, w_mix, fast_here, arrivals = scratch
    rows, normed = outs[:2]
    head = lax.axis_index("head")
    active = is_active(step, spans)
    run = active & (layer < counts[lax.axis_index("segment")])
    half = rows.shape[2]
    head_size = w_mix.shape[0]

    def assemble():
        if layer == 0:
            rows[0] = entering[0][...]
            rows[1] = entering[1][...]
        else:
            held, mine, theirs = entering
            rows[0] = held[0] + (mine[0] + theirs[1])
            rows[1] = held[1] + (mine[1] + theirs[0])

    @pl.when(run)
    def _():
        query_copy = fetch(w_qkv.at[0, layer, :, pl.ds(0, head_size)], w_query, arrivals.at[0])
        fast_from = fast.at[0, layer, 0] if len(fast.shape) == 6 else fast
        fast_copies = [
            fetch(fast_from.at[kind], fast_here.at[kind], arrivals.at[1 + kind])
            for kind in range(3)
        ]
        mix_copy = fetch(w_out.at[0, layer], w_mix, arrivals.at[4])
        assemble()
        keep_at = pl.multiple_of(head * half, half)
        send_at = pl.multiple_of((1 - head) * half, half)
        squares = jnp.sum(rows[0] * rows[0], axis=-1, keepdims=True)
        squares = squares + jnp.sum(rows[1] * rows[1], axis=-1, keepdims=True)
        scale = lax.rsqrt(squares / (2 * half) + TINY)
        gain_keep = gains[0, layer : layer + 1, pl.ds(keep_at, half)]
        gain_send = gains[0, layer : layer + 1, pl.ds(send_at, half)]
        normed[0] = (rows[0] * scale * gain_keep).astype(jnp.bfloat16)
        normed[1] = (rows[1] * scale * gain_send).astype(jnp.bfloat16)
        query_copy.wait()
        query = dot(normed[0], w_query[pl.ds(keep_at, half)])
        query += dot(normed[1], w_query[pl.ds(send_at, half)])
        query = query.astype(jnp.bfloat16)
        head_scale = head_size**-0.5
        fast_copies[0].wait()
        gate = dot(query, fast_here[0].astype(jnp.bfloat16)) * head_scale
        fast_copies[1].wait()
        lift = dot(query, fast_here[1].astype(jnp.bfloat16)) * head_scale
        hidden = (gate * jax.nn.sigmoid(gate) * lift).astype(jnp.bfloat16)
        fast_copies[2].wait()
        answer = (
            lax.dot_general(
                hidden,
                fast_here[2].astype(jnp.bfloat16),
                (((1,), (1,)), ((), ())),
                preferred_element_type=jnp.float32,
            )
            * head_scale
        )
        mean = jnp.mean(answer * answer, axis=-1, keepdims=True)
        answer = (answer * lax.rsqrt(mean + TINY)).astype(jnp.bfloat16)
        mix_copy.wait()
        kept = dot(answer, w_mix[:, pl.ds(keep_at, half)])
        given = dot(answer, w_mix[:, pl.ds(send_at, half)])
        if last:
            outs[2][...] = kept
            outs[3][...] = given
        else:
            outs[2][0] = kept
            outs[2][1] = given

    @pl.when(active & jnp.logical_not(run))
    def _():
        assemble()


def forward(step, layer, spans, last, entering, weights, fast, after):
    counts, gains, w_qkv, w_out = weights
    tokens, half = entering[0].shape[-2:]
    head_size = w_out.shape[2]
    rows = jax.ShapeDtypeStruct((2, tokens, half), jnp.float32)
    normed = jax.ShapeDtypeStruct((2, tokens, half), jnp.bfloat16)
    part = jax.ShapeDtypeStruct((tokens, half), jnp.float32)
    return pl.pallas_call(
        functools.partial(forward_kernel, step, layer, spans, last, len(after)),
        out_shape=(rows, normed) + ((part, part) if last else (rows,)),
        in_specs=[SMEM] + [VMEM] * (len(entering) + 1) + [HBM] * 3 + [ANY] * len(after),
        out_specs=[VMEM] * (4 if last else 3),
        scratch_shapes=[
            pltpu.VMEM((2 * half, head_size), jnp.bfloat16),
            pltpu.VMEM((head_size, 2 * half), jnp.bfloat16),
            pltpu.VMEM(fast.shape[-3:], jnp.float32),
            pltpu.SemaphoreType.DMA((5,)),
        ],
        cost_estimate=SMALL_COST,
        compiler_params=pltpu.CompilerParams(vmem_limit_bytes=FORWARD_VMEM),
        name=f"forward_s{step}_l{layer}",
    )(counts, *entering, gains, w_qkv, w_out, fast, *after)


def key_value_kernel(step, layer, spans, counts, normed, w_qkv, out, held, arrivals):
    head = lax.axis_index("head")
    run = is_active(step, spans) & (layer < counts[lax.axis_index("segment")])

    @pl.when(run)
    def _():
        half = normed.shape[2]
        width = out.shape[1]
        begin = w_qkv.shape[3] - width
        pieces = arrivals.shape[0]
        depth = 2 * half // pieces
        source = w_qkv.at[0, layer, :, pl.ds(begin, width)]
        copies = []
        for index in range(pieces):
            side = head if index * depth < half else 1 - head
            at = pl.multiple_of(side * half + index * depth % half, depth)
            copies.append(
                fetch(source.at[pl.ds(at, depth)], held.at[index], arrivals.at[index])
            )
        made = 0.0
        for index in range(pieces):
            copies[index].wait()
            at = index * depth % half
            made += dot(normed[index * depth // half, :, at : at + depth], held[index])
        out[...] = made.astype(jnp.bfloat16).astype(jnp.float32)


def key_value(step, layer, spans, counts, normed, w_qkv, width):
    pieces = 4
    return pl.pallas_call(
        functools.partial(key_value_kernel, step, layer, spans),
        out_shape=jax.ShapeDtypeStruct((normed.shape[1], width), jnp.float32),
        in_specs=[SMEM, VMEM, HBM],
        out_specs=VMEM,
        scratch_shapes=[
            pltpu.VMEM((pieces, w_qkv.shape[2] // pieces, width), jnp.bfloat16),
            pltpu.SemaphoreType.DMA((pieces,)),
        ],
        cost_estimate=SMALL_COST,
        compiler_params=pltpu.CompilerParams(vmem_limit_bytes=FORWARD_VMEM),
        name=f"keyvalue_s{step}_l{layer}",
    )(counts, normed, w_qkv)


def finish_kernel(step, spans, layer, n_after, counts, rows, keep, got, *refs):
    grown = refs[n_after]
    segment = lax.axis_index("segment")
    active = is_active(step, spans)

    @pl.when(active & (layer < counts[segment]))
    def _():
        grown[...] = rows[0] + (keep[...] + got[...])

    @pl.when(active & (layer >= counts[segment]))
    def _():
        grown[...] = rows[0]


def finish(step, spans, layer, counts, rows, keep, got, after):
    return pl.pallas_call(
        functools.partial(finish_kernel, step, spans, layer, len(after)),
        out_shape=jax.ShapeDtypeStruct(keep.shape, jnp.float32),
        in_specs=[SMEM] + [VMEM] * 3 + [ANY] * len(after),
        out_specs=VMEM,
        cost_estimate=SMALL_COST,
        compiler_params=pltpu.CompilerParams(vmem_limit_bytes=KEY_VALUE_VMEM),
        name=f"finish_s{step}",
    )(counts, rows, keep, got, *after)


def place_kernel(segments, spans, *refs):
    made, out, arrivals = refs[:-2], refs[-2], refs[-1]
    for index in range(segments):

        @pl.when(lax.axis_index("segment") == index)
        def _():
            copies = [
                pltpu.make_async_copy(made[index + span], out.at[span], arrivals.at[span])
                for span in range(spans)
            ]
            for copy in copies:
                copy.start()
            for copy in copies:
                copy.wait()


def place(made, segments, spans):
    return pl.pallas_call(
        functools.partial(place_kernel, segments, spans),
        out_shape=jax.ShapeDtypeStruct((spans,) + made[0].shape, jnp.float32),
        in_specs=[ANY] * len(made),
        out_specs=ANY,
        scratch_shapes=[pltpu.SemaphoreType.DMA((spans,))],
        cost_estimate=SMALL_COST,
        compiler_params=pltpu.CompilerParams(vmem_limit_bytes=KEY_VALUE_VMEM),
        name="place",
    )(*made)


def update_kernel(layer, n_pieces, fast_all, *refs):
    pieces = refs[:n_pieces]
    fast_new, fast, keys, values, rounded, arrivals, leavings = refs[n_pieces:]
    source = fast_all.at[0, layer, 0] if len(fast_all.shape) == 6 else fast_all
    copies = [fetch(source.at[kind], fast.at[kind], arrivals.at[kind]) for kind in range(3)]
    head_size = keys.shape[1]
    head_scale = head_size**-0.5
    begin = 0
    for piece in pieces:
        at = slice(begin, begin + piece.shape[0])
        keys[at] = piece[:, :head_size].astype(jnp.bfloat16)
        values[at] = piece[:, head_size:].astype(jnp.bfloat16)
        begin += piece.shape[0]
    for kind in range(3):
        copies[kind].wait()
        rounded[kind] = fast[kind].astype(jnp.bfloat16)
    total = keys.shape[0]
    chunk = min(total, CHUNK_TOKENS)
    sums = [0.0, 0.0, 0.0]
    for begin in range(0, total, chunk):
        key_rows = keys[begin : begin + chunk]
        value_rows = values[begin : begin + chunk]
        gate = dot(key_rows, rounded[0]) * head_scale
        lift = dot(key_rows, rounded[1]) * head_scale
        up = dot(value_rows, rounded[2]) * -head_scale
        logistic = jax.nn.sigmoid(gate)
        act = gate * logistic
        hidden = (act * lift).astype(jnp.bfloat16)
        slope = logistic * (1.0 + gate * (1.0 - logistic))
        grad_gate = (up * lift * slope).astype(jnp.bfloat16)
        grad_lift = (up * act).astype(jnp.bfloat16)
        sums[0] += dot_over_rows(key_rows, grad_gate)
        sums[1] += dot_over_rows(key_rows, grad_lift)
        sums[2] += dot_over_rows(value_rows, hidden)
    share = fast_new.shape[1]
    begin = 0
    if share < head_size:
        begin = pl.multiple_of(lax.axis_index("tok") * share, share)
    out_copies = []
    for kind, sign in enumerate((head_scale, head_scale, -head_scale)):
        grad = sums[kind] * sign
        mean = jnp.mean(grad * grad)
        rate = STEP_RATE * lax.rsqrt(mean + TINY)
        fast[kind] = fast[kind] - grad * rate
        out_copies.append(
            fetch(fast.at[kind, pl.ds(begin, share)], fast_new.at[kind], leavings.at[kind])
        )
    for copy in out_copies:
        copy.wait()


def update(layer, pieces, fast, share):
    total = sum(piece.shape[0] for piece in pieces)
    shape = fast.shape[-3:]
    return pl.pallas_call(
        functools.partial(update_kernel, layer, len(pieces)),
        out_shape=jax.ShapeDtypeStruct((shape[0], share, shape[2]), jnp.float32),
        in_specs=[HBM] + [VMEM] * len(pieces),
        out_specs=HBM,
        scratch_shapes=[
            pltpu.VMEM(shape, jnp.float32),
            pltpu.VMEM((total, shape[1]), jnp.bfloat16),
            pltpu.VMEM((total, shape[1]), jnp.bfloat16),
            pltpu.VMEM(shape, jnp.bfloat16),
            pltpu.SemaphoreType.DMA((3,)),
            pltpu.SemaphoreType.DMA((3,)),
        ],
        cost_estimate=SMALL_COST,
        compiler_params=pltpu.CompilerParams(vmem_limit_bytes=UPDATE_VMEM),
        name=f"update_l{layer}",
    )(fast, *pieces)


def make_send(sections):
    tok_size = lax.axis_size("tok")
    head_size = lax.axis_size("head")

    def flat(segment, tok, head):
        return (segment * tok_size + tok) * head_size + head

    def send(block, move):
        route = []
        for segment in sections:
            for tok in range(tok_size):
                for head in range(head_size):
                    target = move(segment, tok, head)
                    if target is not None:
                        route.append((flat(segment, tok, head), flat(*target)))
        return lax.ppermute(block, AXES, route)

    return send


def swap_head(send, block):
    return send(block, lambda s, k, h: (s, k, 1 - h))


def gather_near(send, block):
    if lax.axis_size("tok") != 4:
        return [lax.all_gather(block, "tok", axis=0, tiled=True)]
    first = send(block, lambda s, k, h: (s, k ^ 1, h))
    second = send(block, lambda s, k, h: (s, k ^ 2, h))
    return [block, first, second]


def gather_far(send, near):
    if len(near) == 1:
        return near
    cut = near[0].shape[0] // 2
    top = send(near[1][:cut], lambda s, k, h: (s, k ^ 2, h))
    low = send(near[2][cut:], lambda s, k, h: (s, k ^ 1, h))
    return near + [top, low]


def one_layer(fast, layer):
    return fast[0, layer, 0] if len(fast.shape) == 6 else fast


def body(stream, counts, norm_gain, w_qkv, w_out, fast_init):
    segments = lax.axis_size("segment")
    segment = lax.axis_index("segment")
    spans = stream.shape[0]
    slots = fast_init.shape[1]
    head_size = fast_init.shape[4]
    fasts = [fast_init for layer in range(slots)]
    steps = segments + spans - 1
    count = lax.dynamic_index_in_dim(counts, segment, 0, keepdims=False)
    row_share = head_size // lax.axis_size("tok")
    row_start = lax.axis_index("tok") * row_share

    def own_rows(fast, layer):
        return lax.dynamic_slice_in_dim(one_layer(fast, layer), row_start, row_share, 1)

    def update_branch(depth, send):
        def run(near, blocks, fasts):
            near = near + [gather_near(send, block) for block in blocks[: depth - len(near)]]
            changed = [
                update(k, gather_far(send, near[k]), fasts[k], head_size) for k in range(depth)
            ]
            return changed + [one_layer(fasts[k], k) for k in range(depth, slots)]

        return run

    def final_branch(depth, send):
        def run(near, blocks, fasts):
            if depth > 0:
                near = near + [gather_near(send, block) for block in blocks[: depth - 1]]
            changed = [
                update(k, gather_far(send, near[k]), fasts[k], row_share) for k in range(depth)
            ]
            return changed + [own_rows(fasts[k], k) for k in range(depth, slots)]

        return run

    grown_all = []
    weights = [counts, norm_gain, w_qkv, w_out]
    own = stream[0]
    for step in range(steps):
        send = make_send([s for s in range(segments) if 0 <= step - s < spans])
        final = step == steps - 1
        active = (segment <= step) & (segment > step - spans)
        depth = jnp.where(active, count, 0)
        state = [own, swap_head(send, own)]
        blocks = []
        near = []
        for layer in range(slots):
            last = layer == slots - 1
            made = forward(
                step, layer, spans, last, state, weights, fasts[layer], blocks[-1:]
            )
            rows, normed = made[:2]
            got = swap_head(send, made[3] if last else made[2])
            state = [rows, made[2], got]
            blocks.append(key_value(step, layer, spans, counts, normed, w_qkv, 2 * head_size))
            if final and layer == 0:
                near.append(gather_near(send, blocks[0]))
        grown = finish(step, spans, slots - 1, counts, *state, blocks[-1:])
        grown_all.append(grown)
        if final:
            branches = [final_branch(k, send) for k in range(slots + 1)]
            rows = lax.switch(depth, branches, near, blocks[1:], fasts)
            break
        arrived = send(grown, lambda s, k, h: (s + 1, k, h) if s + 1 < segments else None)
        branches = [update_branch(k, send) for k in range(slots + 1)]
        fasts = lax.switch(depth, branches, [], blocks, fasts)
        own, fasts = lax.optimization_barrier((arrived, fasts))
        if step + 1 < spans:
            own = jnp.where(segment == 0, stream[step + 1], own)
    results = place(grown_all, segments, spans)
    return (results[None], jnp.stack(rows)[None, :, None])


def solution(mesh):
    in_specs = (
        P(None, "tok", "head"),
        P(),
        P("segment", None, None),
        P("segment", None, None, "head"),
        P("segment", None, "head", None),
        P("segment", None, "head", None, None, None),
    )
    out_specs = (P("segment", None, "tok", "head"), P("segment", None, "head", None, "tok", None))
    return jax.shard_map(body, mesh=mesh, in_specs=in_specs, out_specs=out_specs, check_vma=False)
```

```python
import functools

import jax
import jax.numpy as jnp
from jax import lax
from jax.experimental import pallas as pl
from jax.experimental.pallas import tpu as pltpu
from jax.sharding import PartitionSpec as P

STEP_RATE = 0.5
TINY = 1e-06
AXES = ("segment", "tok", "head")
MIB = 1024 * 1024
FORWARD_VMEM = 48 * MIB
KEY_VALUE_VMEM = 4 * MIB
UPDATE_VMEM = 28 * MIB
CHUNK_TOKENS = 512

VMEM = pl.BlockSpec(memory_space=pltpu.VMEM)
SMEM = pl.BlockSpec(memory_space=pltpu.SMEM)
ANY = pl.BlockSpec(memory_space=pl.ANY)
HBM = pl.BlockSpec(memory_space=pltpu.HBM)
SMALL_COST = pl.CostEstimate(flops=1024, bytes_accessed=1024, transcendentals=0)


def dot(left, right):
    return jnp.dot(left, right, preferred_element_type=jnp.float32)


def dot_over_rows(left, right):
    return lax.dot_general(
        left, right, (((0,), (0,)), ((), ())), preferred_element_type=jnp.float32
    )


def is_active(step, spans):
    segment = lax.axis_index("segment")
    return (segment <= step) & (segment > step - spans)


def fetch(source, target, arrival):
    copy = pltpu.make_async_copy(source, target, arrival)
    copy.start()
    return copy


def forward_kernel(step, layer, spans, last, n_after, *refs):
    counts, refs = refs[0], refs[1:]
    n_enter = 3 if layer > 0 else 2
    entering, refs = refs[:n_enter], refs[n_enter:]
    gains, w_qkv, w_out, fast = refs[:4]
    outs, scratch = refs[4 + n_after : -4], refs[-4:]
    w_query, w_mix, fast_here, arrivals = scratch
    rows, normed = outs[:2]
    head = lax.axis_index("head")
    active = is_active(step, spans)
    run = active & (layer < counts[lax.axis_index("segment")])
    half = rows.shape[2]
    head_size = w_mix.shape[0]

    def assemble():
        if layer == 0:
            rows[0] = entering[0][...]
            rows[1] = entering[1][...]
        else:
            held, mine, theirs = entering
            rows[0] = held[0] + (mine[0] + theirs[1])
            rows[1] = held[1] + (mine[1] + theirs[0])

    @pl.when(run)
    def _():
        query_copy = fetch(w_qkv.at[0, layer, :, pl.ds(0, head_size)], w_query, arrivals.at[0])
        fast_from = fast.at[0, layer, 0] if len(fast.shape) == 6 else fast
        fast_copies = [
            fetch(fast_from.at[kind], fast_here.at[kind], arrivals.at[1 + kind])
            for kind in range(3)
        ]
        mix_copy = fetch(w_out.at[0, layer], w_mix, arrivals.at[4])
        assemble()
        keep_at = pl.multiple_of(head * half, half)
        send_at = pl.multiple_of((1 - head) * half, half)
        squares = jnp.sum(rows[0] * rows[0], axis=-1, keepdims=True)
        squares = squares + jnp.sum(rows[1] * rows[1], axis=-1, keepdims=True)
        scale = lax.rsqrt(squares / (2 * half) + TINY)
        gain_keep = gains[0, layer : layer + 1, pl.ds(keep_at, half)]
        gain_send = gains[0, layer : layer + 1, pl.ds(send_at, half)]
        normed[0] = (rows[0] * scale * gain_keep).astype(jnp.bfloat16)
        normed[1] = (rows[1] * scale * gain_send).astype(jnp.bfloat16)
        query_copy.wait()
        query = dot(normed[0], w_query[pl.ds(keep_at, half)])
        query += dot(normed[1], w_query[pl.ds(send_at, half)])
        query = query.astype(jnp.bfloat16)
        head_scale = head_size**-0.5
        fast_copies[0].wait()
        gate = dot(query, fast_here[0].astype(jnp.bfloat16)) * head_scale
        fast_copies[1].wait()
        lift = dot(query, fast_here[1].astype(jnp.bfloat16)) * head_scale
        hidden = (gate * jax.nn.sigmoid(gate) * lift).astype(jnp.bfloat16)
        fast_copies[2].wait()
        answer = (
            lax.dot_general(
                hidden,
                fast_here[2].astype(jnp.bfloat16),
                (((1,), (1,)), ((), ())),
                preferred_element_type=jnp.float32,
            )
            * head_scale
        )
        mean = jnp.mean(answer * answer, axis=-1, keepdims=True)
        answer = (answer * lax.rsqrt(mean + TINY)).astype(jnp.bfloat16)
        mix_copy.wait()
        kept = dot(answer, w_mix[:, pl.ds(keep_at, half)])
        given = dot(answer, w_mix[:, pl.ds(send_at, half)])
        if last:
            outs[2][...] = kept
            outs[3][...] = given
        else:
            outs[2][0] = kept
            outs[2][1] = given

    @pl.when(active & jnp.logical_not(run))
    def _():
        assemble()


def forward(step, layer, spans, last, entering, weights, fast, after):
    counts, gains, w_qkv, w_out = weights
    tokens, half = entering[0].shape[-2:]
    head_size = w_out.shape[2]
    rows = jax.ShapeDtypeStruct((2, tokens, half), jnp.float32)
    normed = jax.ShapeDtypeStruct((2, tokens, half), jnp.bfloat16)
    part = jax.ShapeDtypeStruct((tokens, half), jnp.float32)
    return pl.pallas_call(
        functools.partial(forward_kernel, step, layer, spans, last, len(after)),
        out_shape=(rows, normed) + ((part, part) if last else (rows,)),
        in_specs=[SMEM] + [VMEM] * (len(entering) + 1) + [HBM] * 3 + [ANY] * len(after),
        out_specs=[VMEM] * (4 if last else 3),
        scratch_shapes=[
            pltpu.VMEM((2 * half, head_size), jnp.bfloat16),
            pltpu.VMEM((head_size, 2 * half), jnp.bfloat16),
            pltpu.VMEM(fast.shape[-3:], jnp.float32),
            pltpu.SemaphoreType.DMA((5,)),
        ],
        cost_estimate=SMALL_COST,
        compiler_params=pltpu.CompilerParams(vmem_limit_bytes=FORWARD_VMEM),
        name=f"forward_s{step}_l{layer}",
    )(counts, *entering, gains, w_qkv, w_out, fast, *after)


def key_value_kernel(step, layer, spans, counts, normed, w_qkv, out, held, arrivals):
    head = lax.axis_index("head")
    run = is_active(step, spans) & (layer < counts[lax.axis_index("segment")])

    @pl.when(run)
    def _():
        half = normed.shape[2]
        width = out.shape[1]
        begin = w_qkv.shape[3] - width
        pieces = arrivals.shape[0]
        depth = 2 * half // pieces
        source = w_qkv.at[0, layer, :, pl.ds(begin, width)]
        copies = []
        for index in range(pieces):
            side = head if index * depth < half else 1 - head
            at = pl.multiple_of(side * half + index * depth % half, depth)
            copies.append(
                fetch(source.at[pl.ds(at, depth)], held.at[index], arrivals.at[index])
            )
        made = 0.0
        for index in range(pieces):
            copies[index].wait()
            at = index * depth % half
            made += dot(normed[index * depth // half, :, at : at + depth], held[index])
        out[...] = made.astype(jnp.bfloat16).astype(jnp.float32)


def key_value(step, layer, spans, counts, normed, w_qkv, width):
    pieces = 4
    return pl.pallas_call(
        functools.partial(key_value_kernel, step, layer, spans),
        out_shape=jax.ShapeDtypeStruct((normed.shape[1], width), jnp.float32),
        in_specs=[SMEM, VMEM, HBM],
        out_specs=VMEM,
        scratch_shapes=[
            pltpu.VMEM((pieces, w_qkv.shape[2] // pieces, width), jnp.bfloat16),
            pltpu.SemaphoreType.DMA((pieces,)),
        ],
        cost_estimate=SMALL_COST,
        compiler_params=pltpu.CompilerParams(vmem_limit_bytes=FORWARD_VMEM),
        name=f"keyvalue_s{step}_l{layer}",
    )(counts, normed, w_qkv)


def early_kernel(layer, counts, *refs):
    entering, refs = refs[:-5], refs[-5:]
    gains, w_qkv, out, held, arrivals = refs
    segment = lax.axis_index("segment")
    head = lax.axis_index("head")

    @pl.when((segment == lax.axis_size("segment") - 1) & (layer < counts[segment]))
    def _():
        width = out.shape[1]
        pieces = arrivals.shape[0]
        half = w_qkv.shape[2] // 2
        depth = 2 * half // pieces
        source = w_qkv.at[0, layer, :, pl.ds(w_qkv.shape[3] - width, width)]
        copies = []
        for index in range(pieces):
            side = head if index * depth < half else 1 - head
            at = pl.multiple_of(side * half + index * depth % half, depth)
            copies.append(
                fetch(source.at[pl.ds(at, depth)], held.at[index], arrivals.at[index])
            )
        if len(entering) == 2:
            rows = [entering[0][...], entering[1][...]]
        else:
            before, mine, theirs = entering
            rows = [before[0] + (mine[0] + theirs[1]), before[1] + (mine[1] + theirs[0])]
        squares = jnp.sum(rows[0] * rows[0], axis=-1, keepdims=True)
        squares = squares + jnp.sum(rows[1] * rows[1], axis=-1, keepdims=True)
        scale = lax.rsqrt(squares / (2 * half) + TINY)
        normed = []
        for side, part in ((head, rows[0]), (1 - head, rows[1])):
            at = pl.multiple_of(side * half, half)
            gain = gains[0, layer : layer + 1, pl.ds(at, half)]
            normed.append((part * scale * gain).astype(jnp.bfloat16))
        made = 0.0
        for index in range(pieces):
            copies[index].wait()
            at = index * depth % half
            made += dot(normed[index * depth // half][:, at : at + depth], held[index])
        out[...] = made.astype(jnp.bfloat16).astype(jnp.float32)


def early_key_value(layer, entering, weights, width):
    counts, gains, w_qkv, _ = weights
    pieces = 4
    return pl.pallas_call(
        functools.partial(early_kernel, layer),
        out_shape=jax.ShapeDtypeStruct((entering[0].shape[-2], width), jnp.float32),
        in_specs=[SMEM] + [VMEM] * (len(entering) + 1) + [HBM],
        out_specs=VMEM,
        scratch_shapes=[
            pltpu.VMEM((pieces, w_qkv.shape[2] // pieces, width), jnp.bfloat16),
            pltpu.SemaphoreType.DMA((pieces,)),
        ],
        cost_estimate=SMALL_COST,
        compiler_params=pltpu.CompilerParams(vmem_limit_bytes=FORWARD_VMEM),
        name=f"early_l{layer}",
    )(counts, *entering, gains, w_qkv)


def finish_kernel(step, spans, layer, n_after, counts, rows, keep, got, *refs):
    grown = refs[n_after]
    segment = lax.axis_index("segment")
    active = is_active(step, spans)

    @pl.when(active & (layer < counts[segment]))
    def _():
        grown[...] = rows[0] + (keep[...] + got[...])

    @pl.when(active & (layer >= counts[segment]))
    def _():
        grown[...] = rows[0]


def finish(step, spans, layer, counts, rows, keep, got, after):
    return pl.pallas_call(
        functools.partial(finish_kernel, step, spans, layer, len(after)),
        out_shape=jax.ShapeDtypeStruct(keep.shape, jnp.float32),
        in_specs=[SMEM] + [VMEM] * 3 + [ANY] * len(after),
        out_specs=VMEM,
        cost_estimate=SMALL_COST,
        compiler_params=pltpu.CompilerParams(vmem_limit_bytes=KEY_VALUE_VMEM),
        name=f"finish_s{step}",
    )(counts, rows, keep, got, *after)


def join_kernel(rows, mine, theirs, grown):
    grown[...] = rows[0] + (mine[0] + theirs[1])


def join(rows, mine, theirs):
    return pl.pallas_call(
        join_kernel,
        out_shape=jax.ShapeDtypeStruct(rows.shape[1:], jnp.float32),
        in_specs=[VMEM] * 3,
        out_specs=VMEM,
        cost_estimate=SMALL_COST,
        compiler_params=pltpu.CompilerParams(vmem_limit_bytes=KEY_VALUE_VMEM),
        name="join",
    )(rows, mine, theirs)


def deliver_kernel(segments, spans, slots, *refs):
    fasts, refs = refs[:slots], refs[slots:]
    made, (out, own, arrivals, leavings) = refs[:-4], refs[-4:]
    share = own.shape[2]
    begin = pl.multiple_of(lax.axis_index("tok") * share, share)
    row_copies = [
        fetch(fasts[layer].at[:, pl.ds(begin, share)], own.at[layer], leavings.at[layer])
        for layer in range(slots)
    ]
    for index in range(segments):

        @pl.when(lax.axis_index("segment") == index)
        def _():
            copies = [
                fetch(made[index + span], out.at[span], arrivals.at[span])
                for span in range(spans)
            ]
            for copy in copies:
                copy.wait()

    for copy in row_copies:
        copy.wait()


def deliver(fasts, made, segments, spans, share):
    kinds, _, width = fasts[0].shape
    return pl.pallas_call(
        functools.partial(deliver_kernel, segments, spans, len(fasts)),
        out_shape=(
            jax.ShapeDtypeStruct((spans,) + made[0].shape, jnp.float32),
            jax.ShapeDtypeStruct((len(fasts), kinds, share, width), jnp.float32),
        ),
        in_specs=[ANY] * (len(fasts) + len(made)),
        out_specs=(ANY, ANY),
        scratch_shapes=[
            pltpu.SemaphoreType.DMA((spans,)),
            pltpu.SemaphoreType.DMA((len(fasts),)),
        ],
        cost_estimate=SMALL_COST,
        compiler_params=pltpu.CompilerParams(vmem_limit_bytes=KEY_VALUE_VMEM),
        name="deliver",
    )(*fasts, *made)


def update_kernel(layer, n_pieces, fast_all, *refs):
    pieces = refs[:n_pieces]
    fast_new, fast, keys, values, rounded, arrivals, leavings = refs[n_pieces:]
    source = fast_all.at[0, layer, 0] if len(fast_all.shape) == 6 else fast_all
    copies = [fetch(source.at[kind], fast.at[kind], arrivals.at[kind]) for kind in range(3)]
    head_size = keys.shape[1]
    head_scale = head_size**-0.5
    begin = 0
    for piece in pieces:
        at = slice(begin, begin + piece.shape[0])
        keys[at] = piece[:, :head_size].astype(jnp.bfloat16)
        values[at] = piece[:, head_size:].astype(jnp.bfloat16)
        begin += piece.shape[0]
    for kind in range(3):
        copies[kind].wait()
        rounded[kind] = fast[kind].astype(jnp.bfloat16)
    total = keys.shape[0]
    chunk = min(total, CHUNK_TOKENS)
    sums = [0.0, 0.0, 0.0]
    for begin in range(0, total, chunk):
        key_rows = keys[begin : begin + chunk]
        value_rows = values[begin : begin + chunk]
        gate = dot(key_rows, rounded[0]) * head_scale
        lift = dot(key_rows, rounded[1]) * head_scale
        up = dot(value_rows, rounded[2]) * -head_scale
        logistic = jax.nn.sigmoid(gate)
        act = gate * logistic
        hidden = (act * lift).astype(jnp.bfloat16)
        slope = logistic * (1.0 + gate * (1.0 - logistic))
        grad_gate = (up * lift * slope).astype(jnp.bfloat16)
        grad_lift = (up * act).astype(jnp.bfloat16)
        sums[0] += dot_over_rows(key_rows, grad_gate)
        sums[1] += dot_over_rows(key_rows, grad_lift)
        sums[2] += dot_over_rows(value_rows, hidden)
    out_copies = []
    for kind, sign in enumerate((head_scale, head_scale, -head_scale)):
        grad = sums[kind] * sign
        mean = jnp.mean(grad * grad)
        rate = STEP_RATE * lax.rsqrt(mean + TINY)
        fast[kind] = fast[kind] - grad * rate
        out_copies.append(fetch(fast.at[kind], fast_new.at[kind], leavings.at[kind]))
    for copy in out_copies:
        copy.wait()


def update(layer, pieces, fast):
    total = sum(piece.shape[0] for piece in pieces)
    shape = fast.shape[-3:]
    return pl.pallas_call(
        functools.partial(update_kernel, layer, len(pieces)),
        out_shape=jax.ShapeDtypeStruct(shape, jnp.float32),
        in_specs=[HBM] + [VMEM] * len(pieces),
        out_specs=HBM,
        scratch_shapes=[
            pltpu.VMEM(shape, jnp.float32),
            pltpu.VMEM((total, shape[1]), jnp.bfloat16),
            pltpu.VMEM((total, shape[1]), jnp.bfloat16),
            pltpu.VMEM(shape, jnp.bfloat16),
            pltpu.SemaphoreType.DMA((3,)),
            pltpu.SemaphoreType.DMA((3,)),
        ],
        cost_estimate=SMALL_COST,
        compiler_params=pltpu.CompilerParams(vmem_limit_bytes=UPDATE_VMEM),
        input_output_aliases={0: 0} if len(fast.shape) == 3 else {},
        name=f"update_l{layer}",
    )(fast, *pieces)


def make_send(sections):
    tok_size = lax.axis_size("tok")
    head_size = lax.axis_size("head")

    def flat(segment, tok, head):
        return (segment * tok_size + tok) * head_size + head

    def send(block, move):
        route = []
        for segment in sections:
            for tok in range(tok_size):
                for head in range(head_size):
                    target = move(segment, tok, head)
                    if target is not None:
                        route.append((flat(segment, tok, head), flat(*target)))
        return lax.ppermute(block, AXES, route)

    return send


def swap_head(send, block):
    return send(block, lambda s, k, h: (s, k, 1 - h))


def gather_near(send, block):
    if lax.axis_size("tok") != 4:
        return [lax.all_gather(block, "tok", axis=0, tiled=True)]
    first = send(block, lambda s, k, h: (s, k ^ 1, h))
    second = send(block, lambda s, k, h: (s, k ^ 2, h))
    return [block, first, second]


def gather_far(send, near):
    if len(near) == 1:
        return near
    cut = near[0].shape[0] // 2
    top = send(near[1][:cut], lambda s, k, h: (s, k ^ 2, h))
    low = send(near[2][cut:], lambda s, k, h: (s, k ^ 1, h))
    return near + [top, low]


def one_layer(fast, layer):
    return fast[0, layer, 0] if len(fast.shape) == 6 else fast


def body(stream, counts, norm_gain, w_qkv, w_out, fast_init):
    segments = lax.axis_size("segment")
    segment = lax.axis_index("segment")
    spans = stream.shape[0]
    slots = fast_init.shape[1]
    head_size = fast_init.shape[4]
    width = 2 * head_size
    fasts = [fast_init for layer in range(slots)]
    weights = [counts, norm_gain, w_qkv, w_out]
    steps = segments + spans - 1
    count = lax.dynamic_index_in_dim(counts, segment, 0, keepdims=False)

    def update_branch(depth, send):
        def run(blocks, fasts):
            near = [gather_near(send, block) for block in blocks[:depth]]
            changed = [update(k, gather_far(send, near[k]), fasts[k]) for k in range(depth)]
            return changed + [one_layer(fasts[k], k) for k in range(depth, slots)]

        return run

    def last_branch(depth, send):
        def run(own, fasts, weights):
            if depth == 0:
                return jnp.zeros_like(own), fasts
            state = [own, swap_head(send, own)]
            near = []
            for layer in range(depth):
                last = layer > 0 and layer == depth - 1
                block = early_key_value(layer, state, weights, width)
                near.append(gather_near(send, block))
                after = near[0][1:] if depth == 1 else [block]
                made = forward(
                    steps - 1, layer, spans, last, state, weights, fasts[layer], after
                )
                state = [made[0], made[2], swap_head(send, made[3] if last else made[2])]
            if depth == 1:
                grown = join(*state)
            else:
                grown = finish(steps - 1, spans, depth - 1, weights[0], *state, [])
            changed = [update(k, gather_far(send, near[k]), fasts[k]) for k in range(depth)]
            return grown, changed + fasts[depth:]

        return run

    grown_all = []
    own = stream[0]
    for step in range(steps - 1):
        send = make_send([s for s in range(segments) if 0 <= step - s < spans])
        active = (segment <= step) & (segment > step - spans)
        depth = jnp.where(active, count, 0)
        state = [own, swap_head(send, own)]
        blocks = []
        for layer in range(slots):
            last = layer == slots - 1
            made = forward(
                step, layer, spans, last, state, weights, fasts[layer], blocks[-1:]
            )
            rows, normed = made[:2]
            got = swap_head(send, made[3] if last else made[2])
            state = [rows, made[2], got]
            blocks.append(key_value(step, layer, spans, counts, normed, w_qkv, width))
        grown = finish(step, spans, slots - 1, counts, *state, blocks[-1:])
        grown_all.append(grown)
        arrived = send(grown, lambda s, k, h: (s + 1, k, h) if s + 1 < segments else None)
        branches = [update_branch(k, send) for k in range(slots + 1)]
        fasts = lax.switch(depth, branches, blocks, fasts)
        own, fasts = lax.optimization_barrier((arrived, fasts))
        if step + 1 < spans:
            own = jnp.where(segment == 0, stream[step + 1], own)

    send = make_send([segments - 1])
    depth = jnp.where(segment == segments - 1, count, 0)
    branches = [last_branch(k, send) for k in range(slots + 1)]
    grown, fasts = lax.switch(depth, branches, own, fasts, weights)
    grown_all.append(grown)
    row_share = head_size // lax.axis_size("tok")
    results, rows = deliver(fasts, grown_all, segments, spans, row_share)
    return (results[None], rows[None, :, None])


def solution(mesh):
    in_specs = (
        P(None, "tok", "head"),
        P(),
        P("segment", None, None),
        P("segment", None, None, "head"),
        P("segment", None, "head", None),
        P("segment", None, "head", None, None, None),
    )
    out_specs = (P("segment", None, "tok", "head"), P("segment", None, "head", None, "tok", None))
    return jax.shard_map(body, mesh=mesh, in_specs=in_specs, out_specs=out_specs, check_vma=False)
```

```python
import functools

import jax
import jax.numpy as jnp
from jax import lax
from jax.experimental import pallas as pl
from jax.experimental.pallas import tpu as pltpu
from jax.sharding import PartitionSpec as P

STEP_RATE = 0.5
TINY = 1e-06
AXES = ("segment", "tok", "head")
MIB = 1024 * 1024
FORWARD_VMEM = 48 * MIB
KEY_VALUE_VMEM = 4 * MIB
UPDATE_VMEM = 28 * MIB
CHUNK_TOKENS = 512

VMEM = pl.BlockSpec(memory_space=pltpu.VMEM)
SMEM = pl.BlockSpec(memory_space=pltpu.SMEM)
ANY = pl.BlockSpec(memory_space=pl.ANY)
HBM = pl.BlockSpec(memory_space=pltpu.HBM)
SMALL_COST = pl.CostEstimate(flops=1024, bytes_accessed=1024, transcendentals=0)


def dot(left, right):
    return jnp.dot(left, right, preferred_element_type=jnp.float32)


def dot_over_rows(left, right):
    return lax.dot_general(
        left, right, (((0,), (0,)), ((), ())), preferred_element_type=jnp.float32
    )


def is_active(step, spans):
    segment = lax.axis_index("segment")
    return (segment <= step) & (segment > step - spans)


def fetch(source, target, arrival):
    copy = pltpu.make_async_copy(source, target, arrival)
    copy.start()
    return copy


def forward_kernel(step, layer, spans, last, n_after, *refs):
    counts, refs = refs[0], refs[1:]
    n_enter = 3 if layer > 0 else 2
    entering, refs = refs[:n_enter], refs[n_enter:]
    gains, w_qkv, w_out, fast = refs[:4]
    outs, scratch = refs[4 + n_after : -4], refs[-4:]
    w_query, w_mix, fast_here, arrivals = scratch
    rows, normed = outs[:2]
    head = lax.axis_index("head")
    active = is_active(step, spans)
    run = active & (layer < counts[lax.axis_index("segment")])
    half = rows.shape[2]
    head_size = w_mix.shape[0]

    def assemble():
        if layer == 0:
            rows[0] = entering[0][...]
            rows[1] = entering[1][...]
        else:
            held, mine, theirs = entering
            rows[0] = held[0] + (mine[0] + theirs[1])
            rows[1] = held[1] + (mine[1] + theirs[0])

    @pl.when(run)
    def _():
        query_copy = fetch(w_qkv.at[0, layer, :, pl.ds(0, head_size)], w_query, arrivals.at[0])
        fast_from = fast.at[0, layer, 0] if len(fast.shape) == 6 else fast
        fast_copies = [
            fetch(fast_from.at[kind], fast_here.at[kind], arrivals.at[1 + kind])
            for kind in range(3)
        ]
        mix_copy = fetch(w_out.at[0, layer], w_mix, arrivals.at[4])
        assemble()
        keep_at = pl.multiple_of(head * half, half)
        send_at = pl.multiple_of((1 - head) * half, half)
        squares = jnp.sum(rows[0] * rows[0], axis=-1, keepdims=True)
        squares = squares + jnp.sum(rows[1] * rows[1], axis=-1, keepdims=True)
        scale = lax.rsqrt(squares / (2 * half) + TINY)
        gain_keep = gains[0, layer : layer + 1, pl.ds(keep_at, half)]
        gain_send = gains[0, layer : layer + 1, pl.ds(send_at, half)]
        normed[0] = (rows[0] * scale * gain_keep).astype(jnp.bfloat16)
        normed[1] = (rows[1] * scale * gain_send).astype(jnp.bfloat16)
        query_copy.wait()
        query = dot(normed[0], w_query[pl.ds(keep_at, half)])
        query += dot(normed[1], w_query[pl.ds(send_at, half)])
        query = query.astype(jnp.bfloat16)
        head_scale = head_size**-0.5
        fast_copies[0].wait()
        gate = dot(query, fast_here[0].astype(jnp.bfloat16)) * head_scale
        fast_copies[1].wait()
        lift = dot(query, fast_here[1].astype(jnp.bfloat16)) * head_scale
        hidden = (gate * jax.nn.sigmoid(gate) * lift).astype(jnp.bfloat16)
        fast_copies[2].wait()
        answer = (
            lax.dot_general(
                hidden,
                fast_here[2].astype(jnp.bfloat16),
                (((1,), (1,)), ((), ())),
                preferred_element_type=jnp.float32,
            )
            * head_scale
        )
        mean = jnp.mean(answer * answer, axis=-1, keepdims=True)
        answer = (answer * lax.rsqrt(mean + TINY)).astype(jnp.bfloat16)
        mix_copy.wait()
        kept = dot(answer, w_mix[:, pl.ds(keep_at, half)])
        given = dot(answer, w_mix[:, pl.ds(send_at, half)])
        if last:
            outs[2][...] = kept
            outs[3][...] = given
        else:
            outs[2][0] = kept
            outs[2][1] = given

    @pl.when(active & jnp.logical_not(run))
    def _():
        assemble()


def forward(step, layer, spans, last, entering, weights, fast, after):
    counts, gains, w_qkv, w_out = weights
    tokens, half = entering[0].shape[-2:]
    head_size = w_out.shape[2]
    rows = jax.ShapeDtypeStruct((2, tokens, half), jnp.float32)
    normed = jax.ShapeDtypeStruct((2, tokens, half), jnp.bfloat16)
    part = jax.ShapeDtypeStruct((tokens, half), jnp.float32)
    return pl.pallas_call(
        functools.partial(forward_kernel, step, layer, spans, last, len(after)),
        out_shape=(rows, normed) + ((part, part) if last else (rows,)),
        in_specs=[SMEM] + [VMEM] * (len(entering) + 1) + [HBM] * 3 + [ANY] * len(after),
        out_specs=[VMEM] * (4 if last else 3),
        scratch_shapes=[
            pltpu.VMEM((2 * half, head_size), jnp.bfloat16),
            pltpu.VMEM((head_size, 2 * half), jnp.bfloat16),
            pltpu.VMEM(fast.shape[-3:], jnp.float32),
            pltpu.SemaphoreType.DMA((5,)),
        ],
        cost_estimate=SMALL_COST,
        compiler_params=pltpu.CompilerParams(vmem_limit_bytes=FORWARD_VMEM),
        name=f"forward_s{step}_l{layer}",
    )(counts, *entering, gains, w_qkv, w_out, fast, *after)


def key_value_kernel(step, layer, spans, counts, normed, w_qkv, out, held, arrivals):
    head = lax.axis_index("head")
    run = is_active(step, spans) & (layer < counts[lax.axis_index("segment")])

    @pl.when(run)
    def _():
        half = normed.shape[2]
        width = out.shape[1]
        begin = w_qkv.shape[3] - width
        pieces = arrivals.shape[0]
        depth = 2 * half // pieces
        source = w_qkv.at[0, layer, :, pl.ds(begin, width)]
        copies = []
        for index in range(pieces):
            side = head if index * depth < half else 1 - head
            at = pl.multiple_of(side * half + index * depth % half, depth)
            copies.append(
                fetch(source.at[pl.ds(at, depth)], held.at[index], arrivals.at[index])
            )
        made = 0.0
        for index in range(pieces):
            copies[index].wait()
            at = index * depth % half
            made += dot(normed[index * depth // half, :, at : at + depth], held[index])
        out[...] = made.astype(jnp.bfloat16).astype(jnp.float32)


def key_value(step, layer, spans, counts, normed, w_qkv, width):
    pieces = 4
    return pl.pallas_call(
        functools.partial(key_value_kernel, step, layer, spans),
        out_shape=jax.ShapeDtypeStruct((normed.shape[1], width), jnp.float32),
        in_specs=[SMEM, VMEM, HBM],
        out_specs=VMEM,
        scratch_shapes=[
            pltpu.VMEM((pieces, w_qkv.shape[2] // pieces, width), jnp.bfloat16),
            pltpu.SemaphoreType.DMA((pieces,)),
        ],
        cost_estimate=SMALL_COST,
        compiler_params=pltpu.CompilerParams(vmem_limit_bytes=FORWARD_VMEM),
        name=f"keyvalue_s{step}_l{layer}",
    )(counts, normed, w_qkv)


def early_kernel(layer, counts, *refs):
    entering, refs = refs[:-5], refs[-5:]
    gains, w_qkv, out, held, arrivals = refs
    segment = lax.axis_index("segment")
    head = lax.axis_index("head")

    @pl.when((segment == lax.axis_size("segment") - 1) & (layer < counts[segment]))
    def _():
        width = out.shape[1]
        pieces = arrivals.shape[0]
        half = w_qkv.shape[2] // 2
        depth = 2 * half // pieces
        source = w_qkv.at[0, layer, :, pl.ds(w_qkv.shape[3] - width, width)]
        copies = []
        for index in range(pieces):
            side = head if index * depth < half else 1 - head
            at = pl.multiple_of(side * half + index * depth % half, depth)
            copies.append(
                fetch(source.at[pl.ds(at, depth)], held.at[index], arrivals.at[index])
            )
        if len(entering) == 2:
            rows = [entering[0][...], entering[1][...]]
        else:
            before, mine, theirs = entering
            rows = [before[0] + (mine[0] + theirs[1]), before[1] + (mine[1] + theirs[0])]
        squares = jnp.sum(rows[0] * rows[0], axis=-1, keepdims=True)
        squares = squares + jnp.sum(rows[1] * rows[1], axis=-1, keepdims=True)
        scale = lax.rsqrt(squares / (2 * half) + TINY)
        normed = []
        for side, part in ((head, rows[0]), (1 - head, rows[1])):
            at = pl.multiple_of(side * half, half)
            gain = gains[0, layer : layer + 1, pl.ds(at, half)]
            normed.append((part * scale * gain).astype(jnp.bfloat16))
        made = 0.0
        for index in range(pieces):
            copies[index].wait()
            at = index * depth % half
            made += dot(normed[index * depth // half][:, at : at + depth], held[index])
        out[...] = made.astype(jnp.bfloat16).astype(jnp.float32)


def early_key_value(layer, entering, weights, width):
    counts, gains, w_qkv, _ = weights
    pieces = 4
    return pl.pallas_call(
        functools.partial(early_kernel, layer),
        out_shape=jax.ShapeDtypeStruct((entering[0].shape[-2], width), jnp.float32),
        in_specs=[SMEM] + [VMEM] * (len(entering) + 1) + [HBM],
        out_specs=VMEM,
        scratch_shapes=[
            pltpu.VMEM((pieces, w_qkv.shape[2] // pieces, width), jnp.bfloat16),
            pltpu.SemaphoreType.DMA((pieces,)),
        ],
        cost_estimate=SMALL_COST,
        compiler_params=pltpu.CompilerParams(vmem_limit_bytes=FORWARD_VMEM),
        name=f"early_l{layer}",
    )(counts, *entering, gains, w_qkv)


def finish_kernel(step, spans, layer, n_after, counts, rows, keep, got, *refs):
    grown = refs[n_after]
    segment = lax.axis_index("segment")
    active = is_active(step, spans)

    @pl.when(active & (layer < counts[segment]))
    def _():
        grown[...] = rows[0] + (keep[...] + got[...])

    @pl.when(active & (layer >= counts[segment]))
    def _():
        grown[...] = rows[0]


def finish(step, spans, layer, counts, rows, keep, got, after):
    return pl.pallas_call(
        functools.partial(finish_kernel, step, spans, layer, len(after)),
        out_shape=jax.ShapeDtypeStruct(keep.shape, jnp.float32),
        in_specs=[SMEM] + [VMEM] * 3 + [ANY] * len(after),
        out_specs=VMEM,
        cost_estimate=SMALL_COST,
        compiler_params=pltpu.CompilerParams(vmem_limit_bytes=KEY_VALUE_VMEM),
        name=f"finish_s{step}",
    )(counts, rows, keep, got, *after)


def join_kernel(n_after, rows, mine, theirs, *refs):
    refs[n_after][...] = rows[0] + (mine[0] + theirs[1])


def join(rows, mine, theirs, after):
    return pl.pallas_call(
        functools.partial(join_kernel, len(after)),
        out_shape=jax.ShapeDtypeStruct(rows.shape[1:], jnp.float32),
        in_specs=[VMEM] * 3 + [ANY] * len(after),
        out_specs=VMEM,
        cost_estimate=SMALL_COST,
        compiler_params=pltpu.CompilerParams(vmem_limit_bytes=KEY_VALUE_VMEM),
        name="join",
    )(rows, mine, theirs, *after)


def deliver_kernel(segments, spans, slots, *refs):
    fasts, refs = refs[:slots], refs[slots:]
    made, (out, own, out_held, own_held, arrivals, leavings) = refs[:-6], refs[-6:]
    share = own.shape[2]
    begin = pl.multiple_of(lax.axis_index("tok") * share, share)
    pairs = [(own_held.at[layer], own.at[layer]) for layer in range(slots)]
    pairs += [(out_held.at[span], out.at[span]) for span in range(spans)]
    for layer in range(slots):
        fetch(fasts[layer].at[:, pl.ds(begin, share)], own_held.at[layer], arrivals.at[layer])
    for span in range(spans):
        for index in range(segments):

            @pl.when(lax.axis_index("segment") == index)
            def _():
                fetch(made[index + span], out_held.at[span], arrivals.at[slots + span])

    copies = []
    for index, (held, target) in enumerate(pairs):
        pltpu.make_async_copy(held, held, arrivals.at[index]).wait()
        copies.append(fetch(held, target, leavings.at[index]))
    for copy in copies:
        copy.wait()


def deliver(fasts, made, segments, spans, share):
    kinds, _, width = fasts[0].shape
    out = (spans,) + made[0].shape
    own = (len(fasts), kinds, share, width)
    return pl.pallas_call(
        functools.partial(deliver_kernel, segments, spans, len(fasts)),
        out_shape=(
            jax.ShapeDtypeStruct(out, jnp.float32),
            jax.ShapeDtypeStruct(own, jnp.float32),
        ),
        in_specs=[ANY] * (len(fasts) + len(made)),
        out_specs=(ANY, ANY),
        scratch_shapes=[
            pltpu.VMEM(out, jnp.float32),
            pltpu.VMEM(own, jnp.float32),
            pltpu.SemaphoreType.DMA((len(fasts) + spans,)),
            pltpu.SemaphoreType.DMA((len(fasts) + spans,)),
        ],
        cost_estimate=SMALL_COST,
        compiler_params=pltpu.CompilerParams(vmem_limit_bytes=FORWARD_VMEM),
        name="deliver",
    )(*fasts, *made)


def update_kernel(layer, n_pieces, fast_all, *refs):
    pieces = refs[:n_pieces]
    fast_new, fast, keys, values, rounded, arrivals, leavings = refs[n_pieces:]
    source = fast_all.at[0, layer, 0] if len(fast_all.shape) == 6 else fast_all
    copies = [fetch(source.at[kind], fast.at[kind], arrivals.at[kind]) for kind in range(3)]
    head_size = keys.shape[1]
    head_scale = head_size**-0.5
    begin = 0
    for piece in pieces:
        at = slice(begin, begin + piece.shape[0])
        keys[at] = piece[:, :head_size].astype(jnp.bfloat16)
        values[at] = piece[:, head_size:].astype(jnp.bfloat16)
        begin += piece.shape[0]
    for kind in range(3):
        copies[kind].wait()
        rounded[kind] = fast[kind].astype(jnp.bfloat16)
    total = keys.shape[0]
    chunk = min(total, CHUNK_TOKENS)
    sums = [0.0, 0.0, 0.0]
    for begin in range(0, total, chunk):
        key_rows = keys[begin : begin + chunk]
        value_rows = values[begin : begin + chunk]
        gate = dot(key_rows, rounded[0]) * head_scale
        lift = dot(key_rows, rounded[1]) * head_scale
        up = dot(value_rows, rounded[2]) * -head_scale
        logistic = jax.nn.sigmoid(gate)
        act = gate * logistic
        hidden = (act * lift).astype(jnp.bfloat16)
        slope = logistic * (1.0 + gate * (1.0 - logistic))
        grad_gate = (up * lift * slope).astype(jnp.bfloat16)
        grad_lift = (up * act).astype(jnp.bfloat16)
        sums[0] += dot_over_rows(key_rows, grad_gate)
        sums[1] += dot_over_rows(key_rows, grad_lift)
        sums[2] += dot_over_rows(value_rows, hidden)
    out_copies = []
    for kind, sign in enumerate((head_scale, head_scale, -head_scale)):
        grad = sums[kind] * sign
        mean = jnp.mean(grad * grad)
        rate = STEP_RATE * lax.rsqrt(mean + TINY)
        fast[kind] = fast[kind] - grad * rate
        out_copies.append(fetch(fast.at[kind], fast_new.at[kind], leavings.at[kind]))
    for copy in out_copies:
        copy.wait()


def update(layer, pieces, fast):
    total = sum(piece.shape[0] for piece in pieces)
    shape = fast.shape[-3:]
    return pl.pallas_call(
        functools.partial(update_kernel, layer, len(pieces)),
        out_shape=jax.ShapeDtypeStruct(shape, jnp.float32),
        in_specs=[HBM] + [VMEM] * len(pieces),
        out_specs=HBM,
        scratch_shapes=[
            pltpu.VMEM(shape, jnp.float32),
            pltpu.VMEM((total, shape[1]), jnp.bfloat16),
            pltpu.VMEM((total, shape[1]), jnp.bfloat16),
            pltpu.VMEM(shape, jnp.bfloat16),
            pltpu.SemaphoreType.DMA((3,)),
            pltpu.SemaphoreType.DMA((3,)),
        ],
        cost_estimate=SMALL_COST,
        compiler_params=pltpu.CompilerParams(vmem_limit_bytes=UPDATE_VMEM),
        input_output_aliases={0: 0} if len(fast.shape) == 3 else {},
        name=f"update_l{layer}",
    )(fast, *pieces)


def make_send(sections):
    tok_size = lax.axis_size("tok")
    head_size = lax.axis_size("head")

    def flat(segment, tok, head):
        return (segment * tok_size + tok) * head_size + head

    def send(block, move):
        route = []
        for segment in sections:
            for tok in range(tok_size):
                for head in range(head_size):
                    target = move(segment, tok, head)
                    if target is not None:
                        route.append((flat(segment, tok, head), flat(*target)))
        return lax.ppermute(block, AXES, route)

    return send


def swap_head(send, block):
    return send(block, lambda s, k, h: (s, k, 1 - h))


def gather_near(send, block):
    if lax.axis_size("tok") != 4:
        return [lax.all_gather(block, "tok", axis=0, tiled=True)]
    first = send(block, lambda s, k, h: (s, k ^ 1, h))
    second = send(block, lambda s, k, h: (s, k ^ 2, h))
    return [block, first, second]


def gather_far(send, near):
    if len(near) == 1:
        return near
    cut = near[0].shape[0] // 2
    top = send(near[1][:cut], lambda s, k, h: (s, k ^ 2, h))
    low = send(near[2][cut:], lambda s, k, h: (s, k ^ 1, h))
    return near + [top, low]


def one_layer(fast, layer):
    return fast[0, layer, 0] if len(fast.shape) == 6 else fast


def body(stream, counts, norm_gain, w_qkv, w_out, fast_init):
    segments = lax.axis_size("segment")
    segment = lax.axis_index("segment")
    spans = stream.shape[0]
    slots = fast_init.shape[1]
    head_size = fast_init.shape[4]
    width = 2 * head_size
    fasts = [fast_init for layer in range(slots)]
    weights = [counts, norm_gain, w_qkv, w_out]
    steps = segments + spans - 1
    count = lax.dynamic_index_in_dim(counts, segment, 0, keepdims=False)

    def update_branch(depth, send):
        def run(blocks, fasts):
            near = [gather_near(send, block) for block in blocks[:depth]]
            changed = [update(k, gather_far(send, near[k]), fasts[k]) for k in range(depth)]
            return changed + [one_layer(fasts[k], k) for k in range(depth, slots)]

        return run

    def last_branch(depth, send):
        def run(own, fasts, weights):
            if depth == 0:
                return jnp.zeros_like(own), fasts
            state = [own, swap_head(send, own)]
            near = []
            for layer in range(depth):
                last = layer > 0 and layer == depth - 1
                block = early_key_value(layer, state, weights, width)
                near.append(gather_near(send, block))
                made = forward(
                    steps - 1, layer, spans, last, state, weights, fasts[layer], [block]
                )
                state = [made[0], made[2], swap_head(send, made[3] if last else made[2])]
            changed = [update(k, gather_far(send, near[k]), fasts[k]) for k in range(depth)]
            if depth == 1:
                grown = join(*state, changed[-1:])
            else:
                grown = finish(
                    steps - 1, spans, depth - 1, weights[0], *state, changed[-1:]
                )
            return grown, changed + fasts[depth:]

        return run

    grown_all = []
    own = stream[0]
    for step in range(steps - 1):
        send = make_send([s for s in range(segments) if 0 <= step - s < spans])
        active = (segment <= step) & (segment > step - spans)
        depth = jnp.where(active, count, 0)
        state = [own, swap_head(send, own)]
        blocks = []
        for layer in range(slots):
            last = layer == slots - 1
            made = forward(
                step, layer, spans, last, state, weights, fasts[layer], blocks[-1:]
            )
            rows, normed = made[:2]
            got = swap_head(send, made[3] if last else made[2])
            state = [rows, made[2], got]
            blocks.append(key_value(step, layer, spans, counts, normed, w_qkv, width))
        grown = finish(step, spans, slots - 1, counts, *state, blocks[-1:])
        grown_all.append(grown)
        arrived = send(grown, lambda s, k, h: (s + 1, k, h) if s + 1 < segments else None)
        branches = [update_branch(k, send) for k in range(slots + 1)]
        fasts = lax.switch(depth, branches, blocks, fasts)
        own, fasts = lax.optimization_barrier((arrived, fasts))
        if step + 1 < spans:
            own = jnp.where(segment == 0, stream[step + 1], own)

    send = make_send([segments - 1])
    depth = jnp.where(segment == segments - 1, count, 0)
    branches = [last_branch(k, send) for k in range(slots + 1)]
    grown, fasts = lax.switch(depth, branches, own, fasts, weights)
    grown_all.append(grown)
    row_share = head_size // lax.axis_size("tok")
    results, rows = deliver(fasts, grown_all, segments, spans, row_share)
    return (results[None], rows[None, :, None])


def solution(mesh):
    in_specs = (
        P(None, "tok", "head"),
        P(),
        P("segment", None, None),
        P("segment", None, None, "head"),
        P("segment", None, "head", None),
        P("segment", None, "head", None, None, None),
    )
    out_specs = (P("segment", None, "tok", "head"), P("segment", None, "head", None, "tok", None))
    return jax.shard_map(body, mesh=mesh, in_specs=in_specs, out_specs=out_specs, check_vma=False)
```

```python
import functools

import jax
import jax.numpy as jnp
from jax import lax
from jax.experimental import pallas as pl
from jax.experimental.pallas import tpu as pltpu
from jax.sharding import PartitionSpec as P

STEP_RATE = 0.5
TINY = 1e-06
AXES = ("segment", "tok", "head")
MIB = 1024 * 1024
FORWARD_VMEM = 48 * MIB
KEY_VALUE_VMEM = 4 * MIB
UPDATE_VMEM = 28 * MIB
CHUNK_TOKENS = 512

VMEM = pl.BlockSpec(memory_space=pltpu.VMEM)
SMEM = pl.BlockSpec(memory_space=pltpu.SMEM)
ANY = pl.BlockSpec(memory_space=pl.ANY)
HBM = pl.BlockSpec(memory_space=pltpu.HBM)
LARGE_COST = pl.CostEstimate(flops=2**34, bytes_accessed=2**27, transcendentals=0)
SMALL_COST = pl.CostEstimate(flops=1024, bytes_accessed=1024, transcendentals=0)


def dot(left, right):
    return jnp.dot(left, right, preferred_element_type=jnp.float32)


def dot_over_rows(left, right):
    return lax.dot_general(
        left, right, (((0,), (0,)), ((), ())), preferred_element_type=jnp.float32
    )


def is_active(step, spans):
    segment = lax.axis_index("segment")
    return (segment <= step) & (segment > step - spans)


def fetch(source, target, arrival):
    copy = pltpu.make_async_copy(source, target, arrival)
    copy.start()
    return copy


def forward_kernel(step, layer, spans, last, n_after, *refs):
    counts, refs = refs[0], refs[1:]
    n_enter = 3 if layer > 0 else 2
    entering, refs = refs[:n_enter], refs[n_enter:]
    gains, w_qkv, w_out, fast = refs[:4]
    outs, scratch = refs[4 + n_after : -4], refs[-4:]
    w_query, w_mix, fast_here, arrivals = scratch
    rows, normed = outs[:2]
    head = lax.axis_index("head")
    active = is_active(step, spans)
    run = active & (layer < counts[lax.axis_index("segment")])
    half = rows.shape[2]
    head_size = w_mix.shape[0]

    def assemble():
        if layer == 0:
            rows[0] = entering[0][...]
            rows[1] = entering[1][...]
        else:
            held, mine, theirs = entering
            rows[0] = held[0] + (mine[0] + theirs[1])
            rows[1] = held[1] + (mine[1] + theirs[0])

    @pl.when(run)
    def _():
        query_copy = fetch(w_qkv.at[0, layer, :, pl.ds(0, head_size)], w_query, arrivals.at[0])
        fast_from = fast.at[0, layer, 0] if len(fast.shape) == 6 else fast
        fast_copies = [
            fetch(fast_from.at[kind], fast_here.at[kind], arrivals.at[1 + kind])
            for kind in range(3)
        ]
        mix_copy = fetch(w_out.at[0, layer], w_mix, arrivals.at[4])
        assemble()
        keep_at = pl.multiple_of(head * half, half)
        send_at = pl.multiple_of((1 - head) * half, half)
        squares = jnp.sum(rows[0] * rows[0], axis=-1, keepdims=True)
        squares = squares + jnp.sum(rows[1] * rows[1], axis=-1, keepdims=True)
        scale = lax.rsqrt(squares / (2 * half) + TINY)
        gain_keep = gains[0, layer : layer + 1, pl.ds(keep_at, half)]
        gain_send = gains[0, layer : layer + 1, pl.ds(send_at, half)]
        normed[0] = (rows[0] * scale * gain_keep).astype(jnp.bfloat16)
        normed[1] = (rows[1] * scale * gain_send).astype(jnp.bfloat16)
        query_copy.wait()
        query = dot(normed[0], w_query[pl.ds(keep_at, half)])
        query += dot(normed[1], w_query[pl.ds(send_at, half)])
        query = query.astype(jnp.bfloat16)
        head_scale = head_size**-0.5
        fast_copies[0].wait()
        gate = dot(query, fast_here[0].astype(jnp.bfloat16)) * head_scale
        fast_copies[1].wait()
        lift = dot(query, fast_here[1].astype(jnp.bfloat16)) * head_scale
        hidden = (gate * jax.nn.sigmoid(gate) * lift).astype(jnp.bfloat16)
        fast_copies[2].wait()
        answer = (
            lax.dot_general(
                hidden,
                fast_here[2].astype(jnp.bfloat16),
                (((1,), (1,)), ((), ())),
                preferred_element_type=jnp.float32,
            )
            * head_scale
        )
        mean = jnp.mean(answer * answer, axis=-1, keepdims=True)
        answer = (answer * lax.rsqrt(mean + TINY)).astype(jnp.bfloat16)
        mix_copy.wait()
        kept = dot(answer, w_mix[:, pl.ds(keep_at, half)])
        given = dot(answer, w_mix[:, pl.ds(send_at, half)])
        if last:
            outs[2][...] = kept
            outs[3][...] = given
        else:
            outs[2][0] = kept
            outs[2][1] = given

    @pl.when(active & jnp.logical_not(run))
    def _():
        assemble()


def forward(step, layer, spans, last, entering, weights, fast, after):
    counts, gains, w_qkv, w_out = weights
    tokens, half = entering[0].shape[-2:]
    head_size = w_out.shape[2]
    rows = jax.ShapeDtypeStruct((2, tokens, half), jnp.float32)
    normed = jax.ShapeDtypeStruct((2, tokens, half), jnp.bfloat16)
    part = jax.ShapeDtypeStruct((tokens, half), jnp.float32)
    return pl.pallas_call(
        functools.partial(forward_kernel, step, layer, spans, last, len(after)),
        out_shape=(rows, normed) + ((part, part) if last else (rows,)),
        in_specs=[SMEM] + [VMEM] * (len(entering) + 1) + [HBM] * 3 + [ANY] * len(after),
        out_specs=[VMEM] * (4 if last else 3),
        scratch_shapes=[
            pltpu.VMEM((2 * half, head_size), jnp.bfloat16),
            pltpu.VMEM((head_size, 2 * half), jnp.bfloat16),
            pltpu.VMEM(fast.shape[-3:], jnp.float32),
            pltpu.SemaphoreType.DMA((5,)),
        ],
        cost_estimate=SMALL_COST,
        compiler_params=pltpu.CompilerParams(vmem_limit_bytes=FORWARD_VMEM),
        name=f"forward_s{step}_l{layer}",
    )(counts, *entering, gains, w_qkv, w_out, fast, *after)


def key_value_kernel(step, layer, spans, counts, normed, w_qkv, out, held, arrivals):
    head = lax.axis_index("head")
    run = is_active(step, spans) & (layer < counts[lax.axis_index("segment")])

    @pl.when(run)
    def _():
        half = normed.shape[2]
        width = out.shape[1]
        begin = w_qkv.shape[3] - width
        pieces = arrivals.shape[0]
        depth = 2 * half // pieces
        source = w_qkv.at[0, layer, :, pl.ds(begin, width)]
        copies = []
        for index in range(pieces):
            side = head if index * depth < half else 1 - head
            at = pl.multiple_of(side * half + index * depth % half, depth)
            copies.append(
                fetch(source.at[pl.ds(at, depth)], held.at[index], arrivals.at[index])
            )
        made = 0.0
        for index in range(pieces):
            copies[index].wait()
            at = index * depth % half
            made += dot(normed[index * depth // half, :, at : at + depth], held[index])
        out[...] = made.astype(jnp.bfloat16).astype(jnp.float32)


def key_value(step, layer, spans, counts, normed, w_qkv, width):
    pieces = 4
    return pl.pallas_call(
        functools.partial(key_value_kernel, step, layer, spans),
        out_shape=jax.ShapeDtypeStruct((normed.shape[1], width), jnp.float32),
        in_specs=[SMEM, VMEM, HBM],
        out_specs=VMEM,
        scratch_shapes=[
            pltpu.VMEM((pieces, w_qkv.shape[2] // pieces, width), jnp.bfloat16),
            pltpu.SemaphoreType.DMA((pieces,)),
        ],
        cost_estimate=SMALL_COST,
        compiler_params=pltpu.CompilerParams(vmem_limit_bytes=FORWARD_VMEM),
        name=f"keyvalue_s{step}_l{layer}",
    )(counts, normed, w_qkv)


def early_kernel(layer, counts, *refs):
    entering, refs = refs[:-5], refs[-5:]
    gains, w_qkv, out, held, arrivals = refs
    segment = lax.axis_index("segment")
    head = lax.axis_index("head")

    @pl.when((segment == lax.axis_size("segment") - 1) & (layer < counts[segment]))
    def _():
        width = out.shape[1]
        pieces = arrivals.shape[0]
        half = w_qkv.shape[2] // 2
        depth = 2 * half // pieces
        source = w_qkv.at[0, layer, :, pl.ds(w_qkv.shape[3] - width, width)]
        copies = []
        for index in range(pieces):
            side = head if index * depth < half else 1 - head
            at = pl.multiple_of(side * half + index * depth % half, depth)
            copies.append(
                fetch(source.at[pl.ds(at, depth)], held.at[index], arrivals.at[index])
            )
        if len(entering) == 2:
            rows = [entering[0][...], entering[1][...]]
        else:
            before, mine, theirs = entering
            rows = [before[0] + (mine[0] + theirs[1]), before[1] + (mine[1] + theirs[0])]
        squares = jnp.sum(rows[0] * rows[0], axis=-1, keepdims=True)
        squares = squares + jnp.sum(rows[1] * rows[1], axis=-1, keepdims=True)
        scale = lax.rsqrt(squares / (2 * half) + TINY)
        normed = []
        for side, part in ((head, rows[0]), (1 - head, rows[1])):
            at = pl.multiple_of(side * half, half)
            gain = gains[0, layer : layer + 1, pl.ds(at, half)]
            normed.append((part * scale * gain).astype(jnp.bfloat16))
        made = 0.0
        for index in range(pieces):
            copies[index].wait()
            at = index * depth % half
            made += dot(normed[index * depth // half][:, at : at + depth], held[index])
        out[...] = made.astype(jnp.bfloat16).astype(jnp.float32)


def early_key_value(layer, entering, weights, width):
    counts, gains, w_qkv, _ = weights
    pieces = 4
    return pl.pallas_call(
        functools.partial(early_kernel, layer),
        out_shape=jax.ShapeDtypeStruct((entering[0].shape[-2], width), jnp.float32),
        in_specs=[SMEM] + [VMEM] * (len(entering) + 1) + [HBM],
        out_specs=VMEM,
        scratch_shapes=[
            pltpu.VMEM((pieces, w_qkv.shape[2] // pieces, width), jnp.bfloat16),
            pltpu.SemaphoreType.DMA((pieces,)),
        ],
        cost_estimate=SMALL_COST,
        compiler_params=pltpu.CompilerParams(vmem_limit_bytes=FORWARD_VMEM),
        name=f"early_l{layer}",
    )(counts, *entering, gains, w_qkv)


def finish_kernel(step, spans, layer, n_after, counts, rows, keep, got, *refs):
    grown = refs[n_after]
    segment = lax.axis_index("segment")
    active = is_active(step, spans)

    @pl.when(active & (layer < counts[segment]))
    def _():
        grown[...] = rows[0] + (keep[...] + got[...])

    @pl.when(active & (layer >= counts[segment]))
    def _():
        grown[...] = rows[0]


def finish(step, spans, layer, counts, rows, keep, got, after):
    return pl.pallas_call(
        functools.partial(finish_kernel, step, spans, layer, len(after)),
        out_shape=jax.ShapeDtypeStruct(keep.shape, jnp.float32),
        in_specs=[SMEM] + [VMEM] * 3 + [ANY] * len(after),
        out_specs=VMEM,
        cost_estimate=SMALL_COST,
        compiler_params=pltpu.CompilerParams(vmem_limit_bytes=KEY_VALUE_VMEM),
        name=f"finish_s{step}",
    )(counts, rows, keep, got, *after)


def join_kernel(n_after, rows, mine, theirs, *refs):
    refs[n_after][...] = rows[0] + (mine[0] + theirs[1])


def join(rows, mine, theirs, after):
    return pl.pallas_call(
        functools.partial(join_kernel, len(after)),
        out_shape=jax.ShapeDtypeStruct(rows.shape[1:], jnp.float32),
        in_specs=[VMEM] * 3 + [ANY] * len(after),
        out_specs=VMEM,
        cost_estimate=SMALL_COST,
        compiler_params=pltpu.CompilerParams(vmem_limit_bytes=KEY_VALUE_VMEM),
        name="join",
    )(rows, mine, theirs, *after)


def deliver_kernel(segments, spans, slots, *refs):
    fasts, refs = refs[:slots], refs[slots:]
    made, (out, own, out_held, own_held, arrivals, leavings) = refs[:-6], refs[-6:]
    share = own.shape[2]
    begin = pl.multiple_of(lax.axis_index("tok") * share, share)
    pairs = [(own_held.at[layer], own.at[layer]) for layer in range(slots)]
    pairs += [(out_held.at[span], out.at[span]) for span in range(spans)]
    for layer in range(slots):
        fetch(fasts[layer].at[:, pl.ds(begin, share)], own_held.at[layer], arrivals.at[layer])
    for span in range(spans):
        for index in range(segments):

            @pl.when(lax.axis_index("segment") == index)
            def _():
                fetch(made[index + span], out_held.at[span], arrivals.at[slots + span])

    copies = []
    for index, (held, target) in enumerate(pairs):
        pltpu.make_async_copy(held, held, arrivals.at[index]).wait()
        copies.append(fetch(held, target, leavings.at[index]))
    for copy in copies:
        copy.wait()


def deliver(fasts, made, segments, spans, share):
    kinds, _, width = fasts[0].shape
    out = (spans,) + made[0].shape
    own = (len(fasts), kinds, share, width)
    return pl.pallas_call(
        functools.partial(deliver_kernel, segments, spans, len(fasts)),
        out_shape=(
            jax.ShapeDtypeStruct(out, jnp.float32),
            jax.ShapeDtypeStruct(own, jnp.float32),
        ),
        in_specs=[ANY] * (len(fasts) + len(made)),
        out_specs=(ANY, ANY),
        scratch_shapes=[
            pltpu.VMEM(out, jnp.float32),
            pltpu.VMEM(own, jnp.float32),
            pltpu.SemaphoreType.DMA((len(fasts) + spans,)),
            pltpu.SemaphoreType.DMA((len(fasts) + spans,)),
        ],
        cost_estimate=SMALL_COST,
        compiler_params=pltpu.CompilerParams(vmem_limit_bytes=FORWARD_VMEM),
        name="deliver",
    )(*fasts, *made)


def update_kernel(layer, n_pieces, fast_all, *refs):
    pieces = refs[:n_pieces]
    fast_new, fast, keys, values, rounded, arrivals, leavings = refs[n_pieces:]
    source = fast_all.at[0, layer, 0] if len(fast_all.shape) == 6 else fast_all
    copies = [fetch(source.at[kind], fast.at[kind], arrivals.at[kind]) for kind in range(3)]
    head_size = keys.shape[1]
    head_scale = head_size**-0.5
    begin = 0
    for piece in pieces:
        at = slice(begin, begin + piece.shape[0])
        keys[at] = piece[:, :head_size].astype(jnp.bfloat16)
        values[at] = piece[:, head_size:].astype(jnp.bfloat16)
        begin += piece.shape[0]
    for kind in range(3):
        copies[kind].wait()
        rounded[kind] = fast[kind].astype(jnp.bfloat16)
    total = keys.shape[0]
    chunk = min(total, CHUNK_TOKENS)
    made = ([], [], [])
    for begin in range(0, total, chunk):
        key_rows = keys[begin : begin + chunk]
        value_rows = values[begin : begin + chunk]
        gate = dot(key_rows, rounded[0]) * head_scale
        lift = dot(key_rows, rounded[1]) * head_scale
        logistic = jax.nn.sigmoid(gate)
        act = gate * logistic
        made[2].append((value_rows, (act * lift).astype(jnp.bfloat16)))
        up = dot(value_rows, rounded[2]) * -head_scale
        made[1].append((key_rows, (up * act).astype(jnp.bfloat16)))
        slope = logistic * (1.0 + gate * (1.0 - logistic))
        made[0].append((key_rows, (up * lift * slope).astype(jnp.bfloat16)))
    out_copies = []
    for kind, sign in ((2, -head_scale), (1, head_scale), (0, head_scale)):
        grad = sum(dot_over_rows(left, right) for left, right in made[kind]) * sign
        mean = jnp.mean(grad * grad)
        rate = STEP_RATE * lax.rsqrt(mean + TINY)
        fast[kind] = fast[kind] - grad * rate
        out_copies.append(fetch(fast.at[kind], fast_new.at[kind], leavings.at[kind]))
    for copy in out_copies:
        copy.wait()


def update(layer, pieces, fast):
    total = sum(piece.shape[0] for piece in pieces)
    shape = fast.shape[-3:]
    return pl.pallas_call(
        functools.partial(update_kernel, layer, len(pieces)),
        out_shape=jax.ShapeDtypeStruct(shape, jnp.float32),
        in_specs=[HBM] + [VMEM] * len(pieces),
        out_specs=HBM,
        scratch_shapes=[
            pltpu.VMEM(shape, jnp.float32),
            pltpu.VMEM((total, shape[1]), jnp.bfloat16),
            pltpu.VMEM((total, shape[1]), jnp.bfloat16),
            pltpu.VMEM(shape, jnp.bfloat16),
            pltpu.SemaphoreType.DMA((3,)),
            pltpu.SemaphoreType.DMA((3,)),
        ],
        cost_estimate=LARGE_COST,
        compiler_params=pltpu.CompilerParams(vmem_limit_bytes=UPDATE_VMEM),
        input_output_aliases={0: 0} if len(fast.shape) == 3 else {},
        name=f"update_l{layer}",
    )(fast, *pieces)


def make_send(sections):
    tok_size = lax.axis_size("tok")
    head_size = lax.axis_size("head")

    def flat(segment, tok, head):
        return (segment * tok_size + tok) * head_size + head

    def send(block, move):
        route = []
        for segment in sections:
            for tok in range(tok_size):
                for head in range(head_size):
                    target = move(segment, tok, head)
                    if target is not None:
                        route.append((flat(segment, tok, head), flat(*target)))
        return lax.ppermute(block, AXES, route)

    return send


def swap_head(send, block):
    return send(block, lambda s, k, h: (s, k, 1 - h))


def gather_near(send, block):
    if lax.axis_size("tok") != 4:
        return [lax.all_gather(block, "tok", axis=0, tiled=True)]
    first = send(block, lambda s, k, h: (s, k ^ 1, h))
    second = send(block, lambda s, k, h: (s, k ^ 2, h))
    return [block, first, second]


def gather_far(send, near):
    if len(near) == 1:
        return near
    cut = near[0].shape[0] // 2
    top = send(near[1][:cut], lambda s, k, h: (s, k ^ 2, h))
    low = send(near[2][cut:], lambda s, k, h: (s, k ^ 1, h))
    return near + [top, low]


def one_layer(fast, layer):
    return fast[0, layer, 0] if len(fast.shape) == 6 else fast


def body(stream, counts, norm_gain, w_qkv, w_out, fast_init):
    segments = lax.axis_size("segment")
    segment = lax.axis_index("segment")
    spans = stream.shape[0]
    slots = fast_init.shape[1]
    head_size = fast_init.shape[4]
    width = 2 * head_size
    fasts = [fast_init for layer in range(slots)]
    weights = [counts, norm_gain, w_qkv, w_out]
    steps = segments + spans - 1
    count = lax.dynamic_index_in_dim(counts, segment, 0, keepdims=False)

    def update_branch(step, depth, send):
        def run(block, norms, fasts):
            blocks = [block]
            for layer in range(1, depth):
                blocks.append(
                    key_value(step, layer, spans, counts, norms[layer - 1], w_qkv, width)
                )
            near = [gather_near(send, block) for block in blocks[:depth]]
            changed = [update(k, gather_far(send, near[k]), fasts[k]) for k in range(depth)]
            return changed + [one_layer(fasts[k], k) for k in range(depth, slots)]

        return run

    def last_branch(depth, send):
        def run(own, fasts, weights):
            if depth == 0:
                return jnp.zeros_like(own), fasts
            state = [own, swap_head(send, own)]
            near = []
            for layer in range(depth):
                last = layer > 0 and layer == depth - 1
                block = early_key_value(layer, state, weights, width)
                near.append(gather_near(send, block))
                made = forward(
                    steps - 1, layer, spans, last, state, weights, fasts[layer], [block]
                )
                state = [made[0], made[2], swap_head(send, made[3] if last else made[2])]
            changed = [update(k, gather_far(send, near[k]), fasts[k]) for k in range(depth)]
            if depth == 1:
                grown = join(*state, changed[-1:])
            else:
                grown = finish(
                    steps - 1, spans, depth - 1, weights[0], *state, changed[-1:]
                )
            return grown, changed + fasts[depth:]

        return run

    grown_all = []
    own = stream[0]
    for step in range(steps - 1):
        send = make_send([s for s in range(segments) if 0 <= step - s < spans])
        active = (segment <= step) & (segment > step - spans)
        depth = jnp.where(active, count, 0)
        state = [own, swap_head(send, own)]
        blocks = []
        norms = []
        for layer in range(slots):
            last = layer == slots - 1
            made = forward(step, layer, spans, last, state, weights, fasts[layer], blocks)
            rows, normed = made[:2]
            got = swap_head(send, made[3] if last else made[2])
            state = [rows, made[2], got]
            if layer == 0:
                blocks.append(key_value(step, layer, spans, counts, normed, w_qkv, width))
            else:
                norms.append(normed)
        grown = finish(step, spans, slots - 1, counts, *state, blocks)
        grown_all.append(grown)
        arrived = send(grown, lambda s, k, h: (s + 1, k, h) if s + 1 < segments else None)
        branches = [update_branch(step, k, send) for k in range(slots + 1)]
        fasts = lax.switch(depth, branches, blocks[0], norms, fasts)
        own, fasts = lax.optimization_barrier((arrived, fasts))
        if step + 1 < spans:
            own = jnp.where(segment == 0, stream[step + 1], own)

    send = make_send([segments - 1])
    depth = jnp.where(segment == segments - 1, count, 0)
    branches = [last_branch(k, send) for k in range(slots + 1)]
    grown, fasts = lax.switch(depth, branches, own, fasts, weights)
    grown_all.append(grown)
    row_share = head_size // lax.axis_size("tok")
    results, rows = deliver(fasts, grown_all, segments, spans, row_share)
    return (results[None], rows[None, :, None])


def solution(mesh):
    in_specs = (
        P(None, "tok", "head"),
        P(),
        P("segment", None, None),
        P("segment", None, None, "head"),
        P("segment", None, "head", None),
        P("segment", None, "head", None, None, None),
    )
    out_specs = (P("segment", None, "tok", "head"), P("segment", None, "head", None, "tok", None))
    return jax.shard_map(body, mesh=mesh, in_specs=in_specs, out_specs=out_specs, check_vma=False)
```

```python
import functools

import jax
import jax.numpy as jnp
from jax import lax
from jax.experimental import pallas as pl
from jax.experimental.pallas import tpu as pltpu
from jax.sharding import PartitionSpec as P

STEP_RATE = 0.5
TINY = 1e-06
AXES = ("segment", "tok", "head")
MIB = 1024 * 1024
FORWARD_VMEM = 48 * MIB
KEY_VALUE_VMEM = 4 * MIB
UPDATE_VMEM = 28 * MIB
CHUNK_TOKENS = 512

VMEM = pl.BlockSpec(memory_space=pltpu.VMEM)
SMEM = pl.BlockSpec(memory_space=pltpu.SMEM)
ANY = pl.BlockSpec(memory_space=pl.ANY)
HBM = pl.BlockSpec(memory_space=pltpu.HBM)
LARGE_COST = pl.CostEstimate(flops=2**34, bytes_accessed=2**27, transcendentals=0)
SMALL_COST = pl.CostEstimate(flops=1024, bytes_accessed=1024, transcendentals=0)


def dot(left, right):
    return jnp.dot(left, right, preferred_element_type=jnp.float32)


def dot_over_rows(left, right):
    return lax.dot_general(
        left, right, (((0,), (0,)), ((), ())), preferred_element_type=jnp.float32
    )


def is_active(step, spans):
    segment = lax.axis_index("segment")
    return (segment <= step) & (segment > step - spans)


def fetch(source, target, arrival):
    copy = pltpu.make_async_copy(source, target, arrival)
    copy.start()
    return copy


def forward_kernel(step, layer, spans, last, n_after, *refs):
    counts, refs = refs[0], refs[1:]
    n_enter = 3 if layer > 0 else 2
    entering, refs = refs[:n_enter], refs[n_enter:]
    gains, w_qkv, w_out, fast = refs[:4]
    outs, scratch = refs[4 + n_after : -4], refs[-4:]
    w_query, w_mix, fast_here, arrivals = scratch
    rows, normed = outs[:2]
    head = lax.axis_index("head")
    active = is_active(step, spans)
    run = active & (layer < counts[lax.axis_index("segment")])
    half = rows.shape[2]
    head_size = w_mix.shape[0]

    def assemble():
        if layer == 0:
            rows[0] = entering[0][...]
            rows[1] = entering[1][...]
        else:
            held, mine, theirs = entering
            rows[0] = held[0] + (mine[0] + theirs[1])
            rows[1] = held[1] + (mine[1] + theirs[0])

    @pl.when(run)
    def _():
        query_copy = fetch(w_qkv.at[0, layer, :, pl.ds(0, head_size)], w_query, arrivals.at[0])
        fast_from = fast.at[0, layer, 0] if len(fast.shape) == 6 else fast
        fast_copies = [
            fetch(fast_from.at[kind], fast_here.at[kind], arrivals.at[1 + kind])
            for kind in range(3)
        ]
        assemble()
        keep_at = pl.multiple_of(head * half, half)
        send_at = pl.multiple_of((1 - head) * half, half)
        squares = jnp.sum(rows[0] * rows[0], axis=-1, keepdims=True)
        squares = squares + jnp.sum(rows[1] * rows[1], axis=-1, keepdims=True)
        scale = lax.rsqrt(squares / (2 * half) + TINY)
        gain_keep = gains[0, layer : layer + 1, pl.ds(keep_at, half)]
        gain_send = gains[0, layer : layer + 1, pl.ds(send_at, half)]
        normed[0] = (rows[0] * scale * gain_keep).astype(jnp.bfloat16)
        normed[1] = (rows[1] * scale * gain_send).astype(jnp.bfloat16)
        query_copy.wait()
        mix_copy = fetch(w_out.at[0, layer], w_mix, arrivals.at[4])
        query = dot(normed[0], w_query[pl.ds(keep_at, half)])
        query += dot(normed[1], w_query[pl.ds(send_at, half)])
        query = query.astype(jnp.bfloat16)
        head_scale = head_size**-0.5
        fast_copies[0].wait()
        gate = dot(query, fast_here[0].astype(jnp.bfloat16)) * head_scale
        fast_copies[1].wait()
        lift = dot(query, fast_here[1].astype(jnp.bfloat16)) * head_scale
        hidden = (gate * jax.nn.sigmoid(gate) * lift).astype(jnp.bfloat16)
        fast_copies[2].wait()
        answer = (
            lax.dot_general(
                hidden,
                fast_here[2].astype(jnp.bfloat16),
                (((1,), (1,)), ((), ())),
                preferred_element_type=jnp.float32,
            )
            * head_scale
        )
        mean = jnp.mean(answer * answer, axis=-1, keepdims=True)
        answer = (answer * lax.rsqrt(mean + TINY)).astype(jnp.bfloat16)
        mix_copy.wait()
        kept = dot(answer, w_mix[:, pl.ds(keep_at, half)])
        given = dot(answer, w_mix[:, pl.ds(send_at, half)])
        if last:
            outs[2][...] = kept
            outs[3][...] = given
        else:
            outs[2][0] = kept
            outs[2][1] = given

    @pl.when(active & jnp.logical_not(run))
    def _():
        assemble()


def forward(step, layer, spans, last, entering, weights, fast, after):
    counts, gains, w_qkv, w_out = weights
    tokens, half = entering[0].shape[-2:]
    head_size = w_out.shape[2]
    rows = jax.ShapeDtypeStruct((2, tokens, half), jnp.float32)
    normed = jax.ShapeDtypeStruct((2, tokens, half), jnp.bfloat16)
    part = jax.ShapeDtypeStruct((tokens, half), jnp.float32)
    return pl.pallas_call(
        functools.partial(forward_kernel, step, layer, spans, last, len(after)),
        out_shape=(rows, normed) + ((part, part) if last else (rows,)),
        in_specs=[SMEM] + [VMEM] * (len(entering) + 1) + [HBM] * 3 + [ANY] * len(after),
        out_specs=[VMEM] * (4 if last else 3),
        scratch_shapes=[
            pltpu.VMEM((2 * half, head_size), jnp.bfloat16),
            pltpu.VMEM((head_size, 2 * half), jnp.bfloat16),
            pltpu.VMEM(fast.shape[-3:], jnp.float32),
            pltpu.SemaphoreType.DMA((5,)),
        ],
        cost_estimate=SMALL_COST,
        compiler_params=pltpu.CompilerParams(vmem_limit_bytes=FORWARD_VMEM),
        name=f"forward_s{step}_l{layer}",
    )(counts, *entering, gains, w_qkv, w_out, fast, *after)


def key_value_kernel(step, layer, spans, counts, normed, w_qkv, out, held, arrivals):
    head = lax.axis_index("head")
    run = is_active(step, spans) & (layer < counts[lax.axis_index("segment")])

    @pl.when(run)
    def _():
        half = normed.shape[2]
        width = out.shape[1]
        begin = w_qkv.shape[3] - width
        pieces = arrivals.shape[0]
        depth = 2 * half // pieces
        source = w_qkv.at[0, layer, :, pl.ds(begin, width)]
        copies = []
        for index in range(pieces):
            side = head if index * depth < half else 1 - head
            at = pl.multiple_of(side * half + index * depth % half, depth)
            copies.append(
                fetch(source.at[pl.ds(at, depth)], held.at[index], arrivals.at[index])
            )
        made = 0.0
        for index in range(pieces):
            copies[index].wait()
            at = index * depth % half
            made += dot(normed[index * depth // half, :, at : at + depth], held[index])
        out[...] = made.astype(jnp.bfloat16).astype(jnp.float32)


def key_value(step, layer, spans, counts, normed, w_qkv, width):
    pieces = 4
    return pl.pallas_call(
        functools.partial(key_value_kernel, step, layer, spans),
        out_shape=jax.ShapeDtypeStruct((normed.shape[1], width), jnp.float32),
        in_specs=[SMEM, VMEM, HBM],
        out_specs=VMEM,
        scratch_shapes=[
            pltpu.VMEM((pieces, w_qkv.shape[2] // pieces, width), jnp.bfloat16),
            pltpu.SemaphoreType.DMA((pieces,)),
        ],
        cost_estimate=SMALL_COST,
        compiler_params=pltpu.CompilerParams(vmem_limit_bytes=FORWARD_VMEM),
        name=f"keyvalue_s{step}_l{layer}",
    )(counts, normed, w_qkv)


def early_kernel(layer, counts, *refs):
    entering, refs = refs[:-5], refs[-5:]
    gains, w_qkv, out, held, arrivals = refs
    segment = lax.axis_index("segment")
    head = lax.axis_index("head")

    @pl.when((segment == lax.axis_size("segment") - 1) & (layer < counts[segment]))
    def _():
        width = out.shape[1]
        pieces = arrivals.shape[0]
        half = w_qkv.shape[2] // 2
        depth = 2 * half // pieces
        source = w_qkv.at[0, layer, :, pl.ds(w_qkv.shape[3] - width, width)]
        copies = []
        for index in range(pieces):
            side = head if index * depth < half else 1 - head
            at = pl.multiple_of(side * half + index * depth % half, depth)
            copies.append(
                fetch(source.at[pl.ds(at, depth)], held.at[index], arrivals.at[index])
            )
        if len(entering) == 2:
            rows = [entering[0][...], entering[1][...]]
        else:
            before, mine, theirs = entering
            rows = [before[0] + (mine[0] + theirs[1]), before[1] + (mine[1] + theirs[0])]
        squares = jnp.sum(rows[0] * rows[0], axis=-1, keepdims=True)
        squares = squares + jnp.sum(rows[1] * rows[1], axis=-1, keepdims=True)
        scale = lax.rsqrt(squares / (2 * half) + TINY)
        normed = []
        for side, part in ((head, rows[0]), (1 - head, rows[1])):
            at = pl.multiple_of(side * half, half)
            gain = gains[0, layer : layer + 1, pl.ds(at, half)]
            normed.append((part * scale * gain).astype(jnp.bfloat16))
        made = 0.0
        for index in range(pieces):
            copies[index].wait()
            at = index * depth % half
            made += dot(normed[index * depth // half][:, at : at + depth], held[index])
        out[...] = made.astype(jnp.bfloat16).astype(jnp.float32)


def early_key_value(layer, entering, weights, width):
    counts, gains, w_qkv, _ = weights
    pieces = 4
    return pl.pallas_call(
        functools.partial(early_kernel, layer),
        out_shape=jax.ShapeDtypeStruct((entering[0].shape[-2], width), jnp.float32),
        in_specs=[SMEM] + [VMEM] * (len(entering) + 1) + [HBM],
        out_specs=VMEM,
        scratch_shapes=[
            pltpu.VMEM((pieces, w_qkv.shape[2] // pieces, width), jnp.bfloat16),
            pltpu.SemaphoreType.DMA((pieces,)),
        ],
        cost_estimate=SMALL_COST,
        compiler_params=pltpu.CompilerParams(vmem_limit_bytes=FORWARD_VMEM),
        name=f"early_l{layer}",
    )(counts, *entering, gains, w_qkv)


def finish_kernel(step, spans, layer, n_after, counts, rows, keep, got, *refs):
    grown = refs[n_after]
    segment = lax.axis_index("segment")
    active = is_active(step, spans)

    @pl.when(active & (layer < counts[segment]))
    def _():
        grown[...] = rows[0] + (keep[...] + got[...])

    @pl.when(active & (layer >= counts[segment]))
    def _():
        grown[...] = rows[0]


def finish(step, spans, layer, counts, rows, keep, got, after):
    return pl.pallas_call(
        functools.partial(finish_kernel, step, spans, layer, len(after)),
        out_shape=jax.ShapeDtypeStruct(keep.shape, jnp.float32),
        in_specs=[SMEM] + [VMEM] * 3 + [ANY] * len(after),
        out_specs=VMEM,
        cost_estimate=SMALL_COST,
        compiler_params=pltpu.CompilerParams(vmem_limit_bytes=KEY_VALUE_VMEM),
        name=f"finish_s{step}",
    )(counts, rows, keep, got, *after)


def join_kernel(n_after, rows, mine, theirs, *refs):
    refs[n_after][...] = rows[0] + (mine[0] + theirs[1])


def join(rows, mine, theirs, after):
    return pl.pallas_call(
        functools.partial(join_kernel, len(after)),
        out_shape=jax.ShapeDtypeStruct(rows.shape[1:], jnp.float32),
        in_specs=[VMEM] * 3 + [ANY] * len(after),
        out_specs=VMEM,
        cost_estimate=SMALL_COST,
        compiler_params=pltpu.CompilerParams(vmem_limit_bytes=KEY_VALUE_VMEM),
        name="join",
    )(rows, mine, theirs, *after)


def deliver_kernel(segments, spans, slots, *refs):
    fasts, refs = refs[:slots], refs[slots:]
    made, (out, own, out_held, own_held, arrivals, leavings) = refs[:-6], refs[-6:]
    share = own.shape[2]
    begin = pl.multiple_of(lax.axis_index("tok") * share, share)
    pairs = [(own_held.at[layer], own.at[layer]) for layer in range(slots)]
    pairs += [(out_held.at[span], out.at[span]) for span in range(spans)]
    for layer in range(slots):
        fetch(fasts[layer].at[:, pl.ds(begin, share)], own_held.at[layer], arrivals.at[layer])
    for span in range(spans):
        for index in range(segments):

            @pl.when(lax.axis_index("segment") == index)
            def _():
                fetch(made[index + span], out_held.at[span], arrivals.at[slots + span])

    copies = []
    for index, (held, target) in enumerate(pairs):
        pltpu.make_async_copy(held, held, arrivals.at[index]).wait()
        copies.append(fetch(held, target, leavings.at[index]))
    for copy in copies:
        copy.wait()


def deliver(fasts, made, segments, spans, share):
    kinds, _, width = fasts[0].shape
    out = (spans,) + made[0].shape
    own = (len(fasts), kinds, share, width)
    return pl.pallas_call(
        functools.partial(deliver_kernel, segments, spans, len(fasts)),
        out_shape=(
            jax.ShapeDtypeStruct(out, jnp.float32),
            jax.ShapeDtypeStruct(own, jnp.float32),
        ),
        in_specs=[ANY] * (len(fasts) + len(made)),
        out_specs=(ANY, ANY),
        scratch_shapes=[
            pltpu.VMEM(out, jnp.float32),
            pltpu.VMEM(own, jnp.float32),
            pltpu.SemaphoreType.DMA((len(fasts) + spans,)),
            pltpu.SemaphoreType.DMA((len(fasts) + spans,)),
        ],
        cost_estimate=SMALL_COST,
        compiler_params=pltpu.CompilerParams(vmem_limit_bytes=FORWARD_VMEM),
        name="deliver",
    )(*fasts, *made)


def update_kernel(layer, n_pieces, fast_all, *refs):
    pieces = refs[:n_pieces]
    fast_new, fast, keys, values, rounded, arrivals, leavings = refs[n_pieces:]
    source = fast_all.at[0, layer, 0] if len(fast_all.shape) == 6 else fast_all
    copies = [fetch(source.at[kind], fast.at[kind], arrivals.at[kind]) for kind in range(3)]
    head_size = keys.shape[1]
    head_scale = head_size**-0.5
    begin = 0
    for piece in pieces:
        at = slice(begin, begin + piece.shape[0])
        keys[at] = piece[:, :head_size].astype(jnp.bfloat16)
        values[at] = piece[:, head_size:].astype(jnp.bfloat16)
        begin += piece.shape[0]
    for kind in range(3):
        copies[kind].wait()
        rounded[kind] = fast[kind].astype(jnp.bfloat16)
    total = keys.shape[0]
    chunk = min(total, CHUNK_TOKENS)
    made = ([], [], [])
    for begin in range(0, total, chunk):
        key_rows = keys[begin : begin + chunk]
        value_rows = values[begin : begin + chunk]
        gate = dot(key_rows, rounded[0]) * head_scale
        lift = dot(key_rows, rounded[1]) * head_scale
        logistic = jax.nn.sigmoid(gate)
        act = gate * logistic
        made[2].append((value_rows, (act * lift).astype(jnp.bfloat16)))
        up = dot(value_rows, rounded[2]) * -head_scale
        made[1].append((key_rows, (up * act).astype(jnp.bfloat16)))
        slope = logistic * (1.0 + gate * (1.0 - logistic))
        made[0].append((key_rows, (up * lift * slope).astype(jnp.bfloat16)))
    sums = [sum(dot_over_rows(left, right) for left, right in pairs) for pairs in made]
    out_copies = []
    for kind, sign in enumerate((head_scale, head_scale, -head_scale)):
        grad = sums[kind] * sign
        mean = jnp.mean(grad * grad)
        rate = STEP_RATE * lax.rsqrt(mean + TINY)
        fast[kind] = fast[kind] - grad * rate
        out_copies.append(fetch(fast.at[kind], fast_new.at[kind], leavings.at[kind]))
    for copy in out_copies:
        copy.wait()


def update(layer, pieces, fast):
    total = sum(piece.shape[0] for piece in pieces)
    shape = fast.shape[-3:]
    return pl.pallas_call(
        functools.partial(update_kernel, layer, len(pieces)),
        out_shape=jax.ShapeDtypeStruct(shape, jnp.float32),
        in_specs=[HBM] + [VMEM] * len(pieces),
        out_specs=HBM,
        scratch_shapes=[
            pltpu.VMEM(shape, jnp.float32),
            pltpu.VMEM((total, shape[1]), jnp.bfloat16),
            pltpu.VMEM((total, shape[1]), jnp.bfloat16),
            pltpu.VMEM(shape, jnp.bfloat16),
            pltpu.SemaphoreType.DMA((3,)),
            pltpu.SemaphoreType.DMA((3,)),
        ],
        cost_estimate=LARGE_COST,
        compiler_params=pltpu.CompilerParams(vmem_limit_bytes=UPDATE_VMEM),
        input_output_aliases={0: 0} if len(fast.shape) == 3 else {},
        name=f"update_l{layer}",
    )(fast, *pieces)


def make_send(sections):
    tok_size = lax.axis_size("tok")
    head_size = lax.axis_size("head")

    def flat(segment, tok, head):
        return (segment * tok_size + tok) * head_size + head

    def send(block, move):
        route = []
        for segment in sections:
            for tok in range(tok_size):
                for head in range(head_size):
                    target = move(segment, tok, head)
                    if target is not None:
                        route.append((flat(segment, tok, head), flat(*target)))
        return lax.ppermute(block, AXES, route)

    return send


def swap_head(send, block):
    return send(block, lambda s, k, h: (s, k, 1 - h))


def gather_near(send, block):
    if lax.axis_size("tok") != 4:
        return [lax.all_gather(block, "tok", axis=0, tiled=True)]
    first = send(block, lambda s, k, h: (s, k ^ 1, h))
    second = send(block, lambda s, k, h: (s, k ^ 2, h))
    return [block, first, second]


def gather_far(send, near):
    if len(near) == 1:
        return near
    cut = near[0].shape[0] // 2
    top = send(near[1][:cut], lambda s, k, h: (s, k ^ 2, h))
    low = send(near[2][cut:], lambda s, k, h: (s, k ^ 1, h))
    return near + [top, low]


def one_layer(fast, layer):
    return fast[0, layer, 0] if len(fast.shape) == 6 else fast


def body(stream, counts, norm_gain, w_qkv, w_out, fast_init):
    segments = lax.axis_size("segment")
    segment = lax.axis_index("segment")
    spans = stream.shape[0]
    slots = fast_init.shape[1]
    head_size = fast_init.shape[4]
    width = 2 * head_size
    fasts = [fast_init for layer in range(slots)]
    weights = [counts, norm_gain, w_qkv, w_out]
    steps = segments + spans - 1
    count = lax.dynamic_index_in_dim(counts, segment, 0, keepdims=False)

    def update_branch(step, depth, send):
        def run(block, norms, fasts):
            blocks = [block]
            for layer in range(1, depth):
                blocks.append(
                    key_value(step, layer, spans, counts, norms[layer - 1], w_qkv, width)
                )
            near = [gather_near(send, block) for block in blocks[:depth]]
            changed = [update(k, gather_far(send, near[k]), fasts[k]) for k in range(depth)]
            return changed + [one_layer(fasts[k], k) for k in range(depth, slots)]

        return run

    def last_branch(depth, send):
        def run(own, fasts, weights):
            if depth == 0:
                return jnp.zeros_like(own), fasts
            state = [own, swap_head(send, own)]
            near = []
            for layer in range(depth):
                last = layer > 0 and layer == depth - 1
                block = early_key_value(layer, state, weights, width)
                near.append(gather_near(send, block))
                made = forward(
                    steps - 1, layer, spans, last, state, weights, fasts[layer], [block]
                )
                rows = made[0]
                if layer > 0 and len(near[layer]) > 1:
                    *tied, rows = lax.optimization_barrier((*near[layer][1:], rows))
                    near[layer] = near[layer][:1] + tied
                state = [rows, made[2], swap_head(send, made[3] if last else made[2])]
            changed = [update(k, gather_far(send, near[k]), fasts[k]) for k in range(depth)]
            if depth == 1:
                grown = join(*state, changed[-1:])
            else:
                grown = finish(
                    steps - 1, spans, depth - 1, weights[0], *state, changed[-1:]
                )
            return grown, changed + fasts[depth:]

        return run

    grown_all = []
    own = stream[0]
    for step in range(steps - 1):
        send = make_send([s for s in range(segments) if 0 <= step - s < spans])
        active = (segment <= step) & (segment > step - spans)
        depth = jnp.where(active, count, 0)
        state = [own, swap_head(send, own)]
        blocks = []
        norms = []
        for layer in range(slots):
            last = layer == slots - 1
            made = forward(step, layer, spans, last, state, weights, fasts[layer], blocks)
            rows, normed = made[:2]
            got = swap_head(send, made[3] if last else made[2])
            state = [rows, made[2], got]
            if layer == 0:
                blocks.append(key_value(step, layer, spans, counts, normed, w_qkv, width))
            else:
                norms.append(normed)
        grown = finish(step, spans, slots - 1, counts, *state, blocks)
        grown_all.append(grown)
        arrived = send(grown, lambda s, k, h: (s + 1, k, h) if s + 1 < segments else None)
        branches = [update_branch(step, k, send) for k in range(slots + 1)]
        fasts = lax.switch(depth, branches, blocks[0], norms, fasts)
        own, fasts = lax.optimization_barrier((arrived, fasts))
        if step + 1 < spans:
            own = jnp.where(segment == 0, stream[step + 1], own)

    send = make_send([segments - 1])
    depth = jnp.where(segment == segments - 1, count, 0)
    branches = [last_branch(k, send) for k in range(slots + 1)]
    grown, fasts = lax.switch(depth, branches, own, fasts, weights)
    grown_all.append(grown)
    row_share = head_size // lax.axis_size("tok")
    results, rows = deliver(fasts, grown_all, segments, spans, row_share)
    return (results[None], rows[None, :, None])


def solution(mesh):
    in_specs = (
        P(None, "tok", "head"),
        P(),
        P("segment", None, None),
        P("segment", None, None, "head"),
        P("segment", None, "head", None),
        P("segment", None, "head", None, None, None),
    )
    out_specs = (P("segment", None, "tok", "head"), P("segment", None, "head", None, "tok", None))
    return jax.shard_map(body, mesh=mesh, in_specs=in_specs, out_specs=out_specs, check_vma=False)
```

```python
import functools

import jax
import jax.numpy as jnp
from jax import lax
from jax.experimental import pallas as pl
from jax.experimental.pallas import tpu as pltpu
from jax.sharding import PartitionSpec as P

STEP_RATE = 0.5
TINY = 1e-06
AXES = ("segment", "tok", "head")
MIB = 1024 * 1024
FORWARD_VMEM = 48 * MIB
KEY_VALUE_VMEM = 4 * MIB
UPDATE_VMEM = 28 * MIB
CHUNK_TOKENS = 512

VMEM = pl.BlockSpec(memory_space=pltpu.VMEM)
SMEM = pl.BlockSpec(memory_space=pltpu.SMEM)
ANY = pl.BlockSpec(memory_space=pl.ANY)
HBM = pl.BlockSpec(memory_space=pltpu.HBM)
LARGE_COST = pl.CostEstimate(flops=2**34, bytes_accessed=2**27, transcendentals=0)
SMALL_COST = pl.CostEstimate(flops=1024, bytes_accessed=1024, transcendentals=0)


def dot(left, right):
    return jnp.dot(left, right, preferred_element_type=jnp.float32)


def dot_over_rows(left, right):
    return lax.dot_general(
        left, right, (((0,), (0,)), ((), ())), preferred_element_type=jnp.float32
    )


def is_active(step, spans):
    segment = lax.axis_index("segment")
    return (segment <= step) & (segment > step - spans)


def fetch(source, target, arrival):
    copy = pltpu.make_async_copy(source, target, arrival)
    copy.start()
    return copy


def forward_kernel(step, layer, spans, last, n_after, *refs):
    counts, refs = refs[0], refs[1:]
    n_enter = 3 if layer > 0 else 2
    entering, refs = refs[:n_enter], refs[n_enter:]
    gains, w_qkv, w_out, fast = refs[:4]
    outs, scratch = refs[4 + n_after : -4], refs[-4:]
    w_query, w_mix, fast_here, arrivals = scratch
    rows, normed = outs[:2]
    head = lax.axis_index("head")
    active = is_active(step, spans)
    run = active & (layer < counts[lax.axis_index("segment")])
    half = rows.shape[2]
    head_size = w_mix.shape[0]

    def assemble():
        if layer == 0:
            rows[0] = entering[0][...]
            rows[1] = entering[1][...]
        else:
            held, mine, theirs = entering
            rows[0] = held[0] + (mine[0] + theirs[1])
            rows[1] = held[1] + (mine[1] + theirs[0])

    @pl.when(run)
    def _():
        query_copy = fetch(w_qkv.at[0, layer, :, pl.ds(0, head_size)], w_query, arrivals.at[0])
        fast_from = fast.at[0, layer, 0] if len(fast.shape) == 6 else fast
        fast_copies = [
            fetch(fast_from.at[kind], fast_here.at[kind], arrivals.at[1 + kind])
            for kind in range(3)
        ]
        mix_copy = fetch(w_out.at[0, layer], w_mix, arrivals.at[4])
        assemble()
        keep_at = pl.multiple_of(head * half, half)
        send_at = pl.multiple_of((1 - head) * half, half)
        squares = jnp.sum(rows[0] * rows[0], axis=-1, keepdims=True)
        squares = squares + jnp.sum(rows[1] * rows[1], axis=-1, keepdims=True)
        scale = lax.rsqrt(squares / (2 * half) + TINY)
        gain_keep = gains[0, layer : layer + 1, pl.ds(keep_at, half)]
        gain_send = gains[0, layer : layer + 1, pl.ds(send_at, half)]
        normed[0] = (rows[0] * scale * gain_keep).astype(jnp.bfloat16)
        normed[1] = (rows[1] * scale * gain_send).astype(jnp.bfloat16)
        query_copy.wait()
        query = dot(normed[0], w_query[pl.ds(keep_at, half)])
        query += dot(normed[1], w_query[pl.ds(send_at, half)])
        query = query.astype(jnp.bfloat16)
        head_scale = head_size**-0.5
        fast_copies[0].wait()
        gate = dot(query, fast_here[0].astype(jnp.bfloat16)) * head_scale
        fast_copies[1].wait()
        lift = dot(query, fast_here[1].astype(jnp.bfloat16)) * head_scale
        hidden = (gate * jax.nn.sigmoid(gate) * lift).astype(jnp.bfloat16)
        fast_copies[2].wait()
        answer = (
            lax.dot_general(
                hidden,
                fast_here[2].astype(jnp.bfloat16),
                (((1,), (1,)), ((), ())),
                preferred_element_type=jnp.float32,
            )
            * head_scale
        )
        mean = jnp.mean(answer * answer, axis=-1, keepdims=True)
        answer = (answer * lax.rsqrt(mean + TINY)).astype(jnp.bfloat16)
        mix_copy.wait()
        kept = dot(answer, w_mix[:, pl.ds(keep_at, half)])
        given = dot(answer, w_mix[:, pl.ds(send_at, half)])
        if last:
            outs[2][...] = kept
            outs[3][...] = given
        else:
            outs[2][0] = kept
            outs[2][1] = given

    @pl.when(active & jnp.logical_not(run))
    def _():
        assemble()


def forward(step, layer, spans, last, entering, weights, fast, after):
    counts, gains, w_qkv, w_out = weights
    tokens, half = entering[0].shape[-2:]
    head_size = w_out.shape[2]
    rows = jax.ShapeDtypeStruct((2, tokens, half), jnp.float32)
    normed = jax.ShapeDtypeStruct((2, tokens, half), jnp.bfloat16)
    part = jax.ShapeDtypeStruct((tokens, half), jnp.float32)
    return pl.pallas_call(
        functools.partial(forward_kernel, step, layer, spans, last, len(after)),
        out_shape=(rows, normed) + ((part, part) if last else (rows,)),
        in_specs=[SMEM] + [VMEM] * (len(entering) + 1) + [HBM] * 3 + [ANY] * len(after),
        out_specs=[VMEM] * (4 if last else 3),
        scratch_shapes=[
            pltpu.VMEM((2 * half, head_size), jnp.bfloat16),
            pltpu.VMEM((head_size, 2 * half), jnp.bfloat16),
            pltpu.VMEM(fast.shape[-3:], fast.dtype),
            pltpu.SemaphoreType.DMA((5,)),
        ],
        cost_estimate=SMALL_COST,
        compiler_params=pltpu.CompilerParams(vmem_limit_bytes=FORWARD_VMEM),
        name=f"forward_s{step}_l{layer}",
    )(counts, *entering, gains, w_qkv, w_out, fast, *after)


def key_value_kernel(step, layer, spans, counts, normed, w_qkv, out, held, arrivals):
    head = lax.axis_index("head")
    run = is_active(step, spans) & (layer < counts[lax.axis_index("segment")])

    @pl.when(run)
    def _():
        half = normed.shape[2]
        width = out.shape[1]
        begin = w_qkv.shape[3] - width
        pieces = arrivals.shape[0]
        depth = 2 * half // pieces
        source = w_qkv.at[0, layer, :, pl.ds(begin, width)]
        copies = []
        for index in range(pieces):
            side = head if index * depth < half else 1 - head
            at = pl.multiple_of(side * half + index * depth % half, depth)
            copies.append(
                fetch(source.at[pl.ds(at, depth)], held.at[index], arrivals.at[index])
            )
        made = 0.0
        for index in range(pieces):
            copies[index].wait()
            at = index * depth % half
            made += dot(normed[index * depth // half, :, at : at + depth], held[index])
        out[...] = made.astype(jnp.bfloat16).astype(jnp.float32)


def key_value(step, layer, spans, counts, normed, w_qkv, width):
    pieces = 4
    return pl.pallas_call(
        functools.partial(key_value_kernel, step, layer, spans),
        out_shape=jax.ShapeDtypeStruct((normed.shape[1], width), jnp.float32),
        in_specs=[SMEM, VMEM, HBM],
        out_specs=VMEM,
        scratch_shapes=[
            pltpu.VMEM((pieces, w_qkv.shape[2] // pieces, width), jnp.bfloat16),
            pltpu.SemaphoreType.DMA((pieces,)),
        ],
        cost_estimate=SMALL_COST,
        compiler_params=pltpu.CompilerParams(vmem_limit_bytes=FORWARD_VMEM),
        name=f"keyvalue_s{step}_l{layer}",
    )(counts, normed, w_qkv)


def early_kernel(layer, counts, *refs):
    entering, refs = refs[:-5], refs[-5:]
    gains, w_qkv, out, held, arrivals = refs
    segment = lax.axis_index("segment")
    head = lax.axis_index("head")

    @pl.when((segment == lax.axis_size("segment") - 1) & (layer < counts[segment]))
    def _():
        width = out.shape[1]
        pieces = arrivals.shape[0]
        half = w_qkv.shape[2] // 2
        depth = 2 * half // pieces
        source = w_qkv.at[0, layer, :, pl.ds(w_qkv.shape[3] - width, width)]
        copies = []
        for index in range(pieces):
            side = head if index * depth < half else 1 - head
            at = pl.multiple_of(side * half + index * depth % half, depth)
            copies.append(
                fetch(source.at[pl.ds(at, depth)], held.at[index], arrivals.at[index])
            )
        if len(entering) == 2:
            rows = [entering[0][...], entering[1][...]]
        else:
            before, mine, theirs = entering
            rows = [before[0] + (mine[0] + theirs[1]), before[1] + (mine[1] + theirs[0])]
        squares = jnp.sum(rows[0] * rows[0], axis=-1, keepdims=True)
        squares = squares + jnp.sum(rows[1] * rows[1], axis=-1, keepdims=True)
        scale = lax.rsqrt(squares / (2 * half) + TINY)
        normed = []
        for side, part in ((head, rows[0]), (1 - head, rows[1])):
            at = pl.multiple_of(side * half, half)
            gain = gains[0, layer : layer + 1, pl.ds(at, half)]
            normed.append((part * scale * gain).astype(jnp.bfloat16))
        made = 0.0
        for index in range(pieces):
            copies[index].wait()
            at = index * depth % half
            made += dot(normed[index * depth // half][:, at : at + depth], held[index])
        out[...] = made.astype(jnp.bfloat16).astype(jnp.float32)


def early_key_value(layer, entering, weights, width):
    counts, gains, w_qkv, _ = weights
    pieces = 4
    return pl.pallas_call(
        functools.partial(early_kernel, layer),
        out_shape=jax.ShapeDtypeStruct((entering[0].shape[-2], width), jnp.float32),
        in_specs=[SMEM] + [VMEM] * (len(entering) + 1) + [HBM],
        out_specs=VMEM,
        scratch_shapes=[
            pltpu.VMEM((pieces, w_qkv.shape[2] // pieces, width), jnp.bfloat16),
            pltpu.SemaphoreType.DMA((pieces,)),
        ],
        cost_estimate=SMALL_COST,
        compiler_params=pltpu.CompilerParams(vmem_limit_bytes=FORWARD_VMEM),
        name=f"early_l{layer}",
    )(counts, *entering, gains, w_qkv)


def finish_kernel(step, spans, layer, n_after, counts, rows, keep, got, *refs):
    grown = refs[n_after]
    segment = lax.axis_index("segment")
    active = is_active(step, spans)

    @pl.when(active & (layer < counts[segment]))
    def _():
        grown[...] = rows[0] + (keep[...] + got[...])

    @pl.when(active & (layer >= counts[segment]))
    def _():
        grown[...] = rows[0]


def finish(step, spans, layer, counts, rows, keep, got, after):
    return pl.pallas_call(
        functools.partial(finish_kernel, step, spans, layer, len(after)),
        out_shape=jax.ShapeDtypeStruct(keep.shape, jnp.float32),
        in_specs=[SMEM] + [VMEM] * 3 + [ANY] * len(after),
        out_specs=VMEM,
        cost_estimate=SMALL_COST,
        compiler_params=pltpu.CompilerParams(vmem_limit_bytes=KEY_VALUE_VMEM),
        name=f"finish_s{step}",
    )(counts, rows, keep, got, *after)


def join_kernel(n_after, rows, mine, theirs, *refs):
    refs[n_after][...] = rows[0] + (mine[0] + theirs[1])


def join(rows, mine, theirs, after):
    return pl.pallas_call(
        functools.partial(join_kernel, len(after)),
        out_shape=jax.ShapeDtypeStruct(rows.shape[1:], jnp.float32),
        in_specs=[VMEM] * 3 + [ANY] * len(after),
        out_specs=VMEM,
        cost_estimate=SMALL_COST,
        compiler_params=pltpu.CompilerParams(vmem_limit_bytes=KEY_VALUE_VMEM),
        name="join",
    )(rows, mine, theirs, *after)


def deliver_kernel(segments, spans, slots, *refs):
    fasts, refs = refs[:slots], refs[slots:]
    made, (out, own, out_held, own_held, arrivals, leavings) = refs[:-6], refs[-6:]
    share = own.shape[2]
    begin = pl.multiple_of(lax.axis_index("tok") * share, share)
    pairs = [(own_held.at[layer], own.at[layer]) for layer in range(slots)]
    pairs += [(out_held.at[span], out.at[span]) for span in range(spans)]
    for layer in range(slots):
        fetch(fasts[layer].at[:, pl.ds(begin, share)], own_held.at[layer], arrivals.at[layer])
    for span in range(spans):
        for index in range(segments):

            @pl.when(lax.axis_index("segment") == index)
            def _():
                fetch(made[index + span], out_held.at[span], arrivals.at[slots + span])

    copies = []
    for index, (held, target) in enumerate(pairs):
        pltpu.make_async_copy(held, held, arrivals.at[index]).wait()
        copies.append(fetch(held, target, leavings.at[index]))
    for copy in copies:
        copy.wait()


def deliver(fasts, made, segments, spans, share):
    kinds, _, width = fasts[0].shape
    out = (spans,) + made[0].shape
    own = (len(fasts), kinds, share, width)
    return pl.pallas_call(
        functools.partial(deliver_kernel, segments, spans, len(fasts)),
        out_shape=(
            jax.ShapeDtypeStruct(out, jnp.float32),
            jax.ShapeDtypeStruct(own, jnp.float32),
        ),
        in_specs=[ANY] * (len(fasts) + len(made)),
        out_specs=(ANY, ANY),
        scratch_shapes=[
            pltpu.VMEM(out, jnp.float32),
            pltpu.VMEM(own, jnp.float32),
            pltpu.SemaphoreType.DMA((len(fasts) + spans,)),
            pltpu.SemaphoreType.DMA((len(fasts) + spans,)),
        ],
        cost_estimate=SMALL_COST,
        compiler_params=pltpu.CompilerParams(vmem_limit_bytes=FORWARD_VMEM),
        name="deliver",
    )(*fasts, *made)


def update_kernel(layer, n_fast, n_pieces, n_out, *refs):
    sources, refs = refs[:n_fast], refs[n_fast:]
    pieces, refs = refs[:n_pieces], refs[n_pieces:]
    targets, (fast, keys, values, rounded, arrivals, leavings) = refs[:n_out], refs[n_out:]
    kinds = range(fast.shape[0])
    source = sources[0].at[0, layer, 0] if len(sources[0].shape) == 6 else sources[0]
    if n_fast > 1:
        short = [
            fetch(sources[1].at[kind], rounded.at[kind], arrivals.at[1, kind]) for kind in kinds
        ]
    full = [fetch(source.at[kind], fast.at[kind], arrivals.at[0, kind]) for kind in kinds]
    head_size = keys.shape[1]
    head_scale = head_size**-0.5
    begin = 0
    for piece in pieces:
        at = slice(begin, begin + piece.shape[0])
        keys[at] = piece[:, :head_size].astype(jnp.bfloat16)
        values[at] = piece[:, head_size:].astype(jnp.bfloat16)
        begin += piece.shape[0]

    def ready(kind):
        if n_fast > 1:
            short[kind].wait()
        else:
            full[kind].wait()
            rounded[kind] = fast[kind].astype(jnp.bfloat16)

    total = keys.shape[0]
    chunk = min(total, CHUNK_TOKENS)
    made = ([], [], [])
    for begin in range(0, total, chunk):
        key_rows = keys[begin : begin + chunk]
        value_rows = values[begin : begin + chunk]
        if begin == 0:
            ready(0)
        gate = dot(key_rows, rounded[0]) * head_scale
        if begin == 0:
            ready(1)
        lift = dot(key_rows, rounded[1]) * head_scale
        if begin == 0:
            ready(2)
        up = dot(value_rows, rounded[2]) * -head_scale
        logistic = jax.nn.sigmoid(gate)
        act = gate * logistic
        made[2].append((value_rows, (act * lift).astype(jnp.bfloat16)))
        made[1].append((key_rows, (up * act).astype(jnp.bfloat16)))
        slope = logistic * (1.0 + gate * (1.0 - logistic))
        made[0].append((key_rows, (up * lift * slope).astype(jnp.bfloat16)))
    sums = [sum(dot_over_rows(left, right) for left, right in pairs) for pairs in made]
    if n_fast > 1:
        for kind in kinds:
            full[kind].wait()
    out_copies = []
    for kind, sign in enumerate((head_scale, head_scale, -head_scale)):
        grad = sums[kind] * sign
        mean = jnp.mean(grad * grad)
        rate = STEP_RATE * lax.rsqrt(mean + TINY)
        moved = fast[kind] - grad * rate
        fast[kind] = moved
        out_copies.append(fetch(fast.at[kind], targets[0].at[kind], leavings.at[0, kind]))
        if n_out > 1:
            rounded[kind] = moved.astype(jnp.bfloat16)
            out_copies.append(
                fetch(rounded.at[kind], targets[1].at[kind], leavings.at[1, kind])
            )
    for copy in out_copies:
        copy.wait()


def update(layer, pieces, fast, final=False):
    sources = list(fast) if isinstance(fast, (tuple, list)) else [fast]
    total = sum(piece.shape[0] for piece in pieces)
    shape = sources[0].shape[-3:]
    outs = [jax.ShapeDtypeStruct(shape, jnp.float32)]
    if not final:
        outs.append(jax.ShapeDtypeStruct(shape, jnp.bfloat16))
    in_place = range(min(len(sources), len(outs))) if len(sources) > 1 else ()
    made = pl.pallas_call(
        functools.partial(update_kernel, layer, len(sources), len(pieces), len(outs)),
        out_shape=outs,
        in_specs=[HBM] * len(sources) + [VMEM] * len(pieces),
        out_specs=[HBM] * len(outs),
        scratch_shapes=[
            pltpu.VMEM(shape, jnp.float32),
            pltpu.VMEM((total, shape[1]), jnp.bfloat16),
            pltpu.VMEM((total, shape[1]), jnp.bfloat16),
            pltpu.VMEM(shape, jnp.bfloat16),
            pltpu.SemaphoreType.DMA((2, shape[0])),
            pltpu.SemaphoreType.DMA((2, shape[0])),
        ],
        cost_estimate=LARGE_COST,
        compiler_params=pltpu.CompilerParams(vmem_limit_bytes=UPDATE_VMEM),
        input_output_aliases={index: index for index in in_place},
        name=f"update_l{layer}",
    )(*sources, *pieces)
    return made[0] if final else tuple(made)


def make_send(sections):
    tok_size = lax.axis_size("tok")
    head_size = lax.axis_size("head")

    def flat(segment, tok, head):
        return (segment * tok_size + tok) * head_size + head

    def send(block, move):
        route = []
        for segment in sections:
            for tok in range(tok_size):
                for head in range(head_size):
                    target = move(segment, tok, head)
                    if target is not None:
                        route.append((flat(segment, tok, head), flat(*target)))
        return lax.ppermute(block, AXES, route)

    return send


def swap_head(send, block):
    return send(block, lambda s, k, h: (s, k, 1 - h))


def gather_near(send, block):
    if lax.axis_size("tok") != 4:
        return [lax.all_gather(block, "tok", axis=0, tiled=True)]
    first = send(block, lambda s, k, h: (s, k ^ 1, h))
    second = send(block, lambda s, k, h: (s, k ^ 2, h))
    return [block, first, second]


def gather_far(send, near):
    if len(near) == 1:
        return near
    cut = near[0].shape[0] // 2
    top = send(near[1][:cut], lambda s, k, h: (s, k ^ 2, h))
    low = send(near[2][cut:], lambda s, k, h: (s, k ^ 1, h))
    return near + [top, low]


def both_forms(fast, layer):
    if isinstance(fast, (tuple, list)):
        return tuple(fast)
    return fast[0, layer, 0], fast[0, layer, 0].astype(jnp.bfloat16)


def to_multiply(fast):
    return fast[1] if isinstance(fast, (tuple, list)) else fast


def body(stream, counts, norm_gain, w_qkv, w_out, fast_init):
    segments = lax.axis_size("segment")
    segment = lax.axis_index("segment")
    spans = stream.shape[0]
    slots = fast_init.shape[1]
    head_size = fast_init.shape[4]
    width = 2 * head_size
    fasts = [fast_init for layer in range(slots)]
    weights = [counts, norm_gain, w_qkv, w_out]
    steps = segments + spans - 1
    count = lax.dynamic_index_in_dim(counts, segment, 0, keepdims=False)

    def update_branch(step, depth, send):
        def run(block, norms, fasts):
            blocks = [block]
            for layer in range(1, depth):
                blocks.append(
                    key_value(step, layer, spans, counts, norms[layer - 1], w_qkv, width)
                )
            near = [gather_near(send, block) for block in blocks[:depth]]
            changed = [update(k, gather_far(send, near[k]), fasts[k]) for k in range(depth)]
            return changed + [both_forms(fasts[k], k) for k in range(depth, slots)]

        return run

    def last_branch(depth, send):
        def run(own, fasts, weights):
            if depth == 0:
                return jnp.zeros_like(own), [fast[0] for fast in fasts]
            state = [own, swap_head(send, own)]
            near = []
            for layer in range(depth):
                last = layer > 0 and layer == depth - 1
                block = early_key_value(layer, state, weights, width)
                near.append(gather_near(send, block))
                made = forward(
                    steps - 1, layer, spans, last, state, weights, to_multiply(fasts[layer]), [block]
                )
                rows = made[0]
                if layer > 0 and len(near[layer]) > 1:
                    *tied, rows = lax.optimization_barrier((*near[layer][1:], rows))
                    near[layer] = near[layer][:1] + tied
                state = [rows, made[2], swap_head(send, made[3] if last else made[2])]
            changed = [
                update(k, gather_far(send, near[k]), fasts[k], True) for k in range(depth)
            ]
            if depth == 1:
                grown = join(*state, changed[-1:])
            else:
                grown = finish(
                    steps - 1, spans, depth - 1, weights[0], *state, changed[-1:]
                )
            return grown, changed + [fast[0] for fast in fasts[depth:]]

        return run

    grown_all = []
    own = stream[0]
    for step in range(steps - 1):
        send = make_send([s for s in range(segments) if 0 <= step - s < spans])
        active = (segment <= step) & (segment > step - spans)
        depth = jnp.where(active, count, 0)
        state = [own, swap_head(send, own)]
        blocks = []
        norms = []
        for layer in range(slots):
            last = layer == slots - 1
            made = forward(
                step, layer, spans, last, state, weights, to_multiply(fasts[layer]), blocks
            )
            rows, normed = made[:2]
            got = swap_head(send, made[3] if last else made[2])
            state = [rows, made[2], got]
            if layer == 0:
                blocks.append(key_value(step, layer, spans, counts, normed, w_qkv, width))
            else:
                norms.append(normed)
        grown = finish(step, spans, slots - 1, counts, *state, blocks)
        grown_all.append(grown)
        arrived = send(grown, lambda s, k, h: (s + 1, k, h) if s + 1 < segments else None)
        branches = [update_branch(step, k, send) for k in range(slots + 1)]
        fasts = lax.switch(depth, branches, blocks[0], norms, fasts)
        own, fasts = lax.optimization_barrier((arrived, fasts))
        if step + 1 < spans:
            own = jnp.where(segment == 0, stream[step + 1], own)

    send = make_send([segments - 1])
    depth = jnp.where(segment == segments - 1, count, 0)
    branches = [last_branch(k, send) for k in range(slots + 1)]
    grown, fasts = lax.switch(depth, branches, own, fasts, weights)
    grown_all.append(grown)
    row_share = head_size // lax.axis_size("tok")
    results, rows = deliver(fasts, grown_all, segments, spans, row_share)
    return (results[None], rows[None, :, None])


def solution(mesh):
    in_specs = (
        P(None, "tok", "head"),
        P(),
        P("segment", None, None),
        P("segment", None, None, "head"),
        P("segment", None, "head", None),
        P("segment", None, "head", None, None, None),
    )
    out_specs = (P("segment", None, "tok", "head"), P("segment", None, "head", None, "tok", None))
    return jax.shard_map(body, mesh=mesh, in_specs=in_specs, out_specs=out_specs, check_vma=False)
```

```python
import functools

import jax
import jax.numpy as jnp
from jax import lax
from jax.experimental import pallas as pl
from jax.experimental.pallas import tpu as pltpu
from jax.sharding import PartitionSpec as P

STEP_RATE = 0.5
TINY = 1e-06
AXES = ("segment", "tok", "head")
MIB = 1024 * 1024
FORWARD_VMEM = 48 * MIB
KEY_VALUE_VMEM = 4 * MIB
UPDATE_VMEM = 28 * MIB
CHUNK_TOKENS = 512

VMEM = pl.BlockSpec(memory_space=pltpu.VMEM)
SMEM = pl.BlockSpec(memory_space=pltpu.SMEM)
ANY = pl.BlockSpec(memory_space=pl.ANY)
HBM = pl.BlockSpec(memory_space=pltpu.HBM)
LARGE_COST = pl.CostEstimate(flops=2**34, bytes_accessed=2**27, transcendentals=0)
SMALL_COST = pl.CostEstimate(flops=1024, bytes_accessed=1024, transcendentals=0)


def dot(left, right):
    return jnp.dot(left, right, preferred_element_type=jnp.float32)


def dot_over_rows(left, right):
    return lax.dot_general(
        left, right, (((0,), (0,)), ((), ())), preferred_element_type=jnp.float32
    )


def is_active(step, spans):
    segment = lax.axis_index("segment")
    return (segment <= step) & (segment > step - spans)


def fetch(source, target, arrival):
    copy = pltpu.make_async_copy(source, target, arrival)
    copy.start()
    return copy


def forward_kernel(step, layer, spans, last, n_after, *refs):
    counts, refs = refs[0], refs[1:]
    n_enter = 3 if layer > 0 else 2
    entering, refs = refs[:n_enter], refs[n_enter:]
    gains, w_qkv, w_out, fast = refs[:4]
    outs, scratch = refs[4 + n_after : -4], refs[-4:]
    w_query, w_mix, fast_here, arrivals = scratch
    rows, normed = outs[:2]
    head = lax.axis_index("head")
    active = is_active(step, spans)
    run = active & (layer < counts[lax.axis_index("segment")])
    half = rows.shape[2]
    head_size = w_mix.shape[0]

    def assemble():
        if layer == 0:
            rows[0] = entering[0][...]
            rows[1] = entering[1][...]
        else:
            held, mine, theirs = entering
            rows[0] = held[0] + (mine[0] + theirs[1])
            rows[1] = held[1] + (mine[1] + theirs[0])

    @pl.when(run)
    def _():
        query_copy = fetch(w_qkv.at[0, layer, :, pl.ds(0, head_size)], w_query, arrivals.at[0])
        fast_from = fast.at[0, layer, 0] if len(fast.shape) == 6 else fast
        fast_copies = [
            fetch(fast_from.at[kind], fast_here.at[kind], arrivals.at[1 + kind])
            for kind in range(3)
        ]
        mix_copy = fetch(w_out.at[0, layer], w_mix, arrivals.at[4])
        assemble()
        keep_at = pl.multiple_of(head * half, half)
        send_at = pl.multiple_of((1 - head) * half, half)
        squares = jnp.sum(rows[0] * rows[0], axis=-1, keepdims=True)
        squares = squares + jnp.sum(rows[1] * rows[1], axis=-1, keepdims=True)
        scale = lax.rsqrt(squares / (2 * half) + TINY)
        gain_keep = gains[0, layer : layer + 1, pl.ds(keep_at, half)]
        gain_send = gains[0, layer : layer + 1, pl.ds(send_at, half)]
        normed[0] = (rows[0] * scale * gain_keep).astype(jnp.bfloat16)
        normed[1] = (rows[1] * scale * gain_send).astype(jnp.bfloat16)
        query_copy.wait()
        query = dot(normed[0], w_query[pl.ds(keep_at, half)])
        query += dot(normed[1], w_query[pl.ds(send_at, half)])
        query = query.astype(jnp.bfloat16)
        head_scale = head_size**-0.5
        fast_copies[0].wait()
        gate = dot(query, fast_here[0].astype(jnp.bfloat16)) * head_scale
        fast_copies[1].wait()
        lift = dot(query, fast_here[1].astype(jnp.bfloat16)) * head_scale
        hidden = (gate * jax.nn.sigmoid(gate) * lift).astype(jnp.bfloat16)
        fast_copies[2].wait()
        answer = (
            lax.dot_general(
                hidden,
                fast_here[2].astype(jnp.bfloat16),
                (((1,), (1,)), ((), ())),
                preferred_element_type=jnp.float32,
            )
            * head_scale
        )
        mean = jnp.mean(answer * answer, axis=-1, keepdims=True)
        answer = (answer * lax.rsqrt(mean + TINY)).astype(jnp.bfloat16)
        mix_copy.wait()
        kept = dot(answer, w_mix[:, pl.ds(keep_at, half)])
        given = dot(answer, w_mix[:, pl.ds(send_at, half)])
        if last:
            outs[2][...] = kept
            outs[3][...] = given
        else:
            outs[2][0] = kept
            outs[2][1] = given

    @pl.when(active & jnp.logical_not(run))
    def _():
        assemble()


def forward(step, layer, spans, last, entering, weights, fast, after):
    counts, gains, w_qkv, w_out = weights
    tokens, half = entering[0].shape[-2:]
    head_size = w_out.shape[2]
    rows = jax.ShapeDtypeStruct((2, tokens, half), jnp.float32)
    normed = jax.ShapeDtypeStruct((2, tokens, half), jnp.bfloat16)
    part = jax.ShapeDtypeStruct((tokens, half), jnp.float32)
    return pl.pallas_call(
        functools.partial(forward_kernel, step, layer, spans, last, len(after)),
        out_shape=(rows, normed) + ((part, part) if last else (rows,)),
        in_specs=[SMEM] + [VMEM] * (len(entering) + 1) + [HBM] * 3 + [ANY] * len(after),
        out_specs=[VMEM] * (4 if last else 3),
        scratch_shapes=[
            pltpu.VMEM((2 * half, head_size), jnp.bfloat16),
            pltpu.VMEM((head_size, 2 * half), jnp.bfloat16),
            pltpu.VMEM(fast.shape[-3:], jnp.float32),
            pltpu.SemaphoreType.DMA((5,)),
        ],
        cost_estimate=SMALL_COST,
        compiler_params=pltpu.CompilerParams(vmem_limit_bytes=FORWARD_VMEM),
        name=f"forward_s{step}_l{layer}",
    )(counts, *entering, gains, w_qkv, w_out, fast, *after)


def key_value_kernel(step, layer, spans, counts, normed, w_qkv, out, held, arrivals):
    head = lax.axis_index("head")
    run = is_active(step, spans) & (layer < counts[lax.axis_index("segment")])

    @pl.when(run)
    def _():
        half = normed.shape[2]
        width = out.shape[1]
        begin = w_qkv.shape[3] - width
        pieces = arrivals.shape[0]
        depth = 2 * half // pieces
        source = w_qkv.at[0, layer, :, pl.ds(begin, width)]
        copies = []
        for index in range(pieces):
            side = head if index * depth < half else 1 - head
            at = pl.multiple_of(side * half + index * depth % half, depth)
            copies.append(
                fetch(source.at[pl.ds(at, depth)], held.at[index], arrivals.at[index])
            )
        made = 0.0
        for index in range(pieces):
            copies[index].wait()
            at = index * depth % half
            made += dot(normed[index * depth // half, :, at : at + depth], held[index])
        out[...] = made.astype(jnp.bfloat16).astype(jnp.float32)


def key_value(step, layer, spans, counts, normed, w_qkv, width):
    pieces = 4
    return pl.pallas_call(
        functools.partial(key_value_kernel, step, layer, spans),
        out_shape=jax.ShapeDtypeStruct((normed.shape[1], width), jnp.float32),
        in_specs=[SMEM, VMEM, HBM],
        out_specs=VMEM,
        scratch_shapes=[
            pltpu.VMEM((pieces, w_qkv.shape[2] // pieces, width), jnp.bfloat16),
            pltpu.SemaphoreType.DMA((pieces,)),
        ],
        cost_estimate=SMALL_COST,
        compiler_params=pltpu.CompilerParams(vmem_limit_bytes=FORWARD_VMEM),
        name=f"keyvalue_s{step}_l{layer}",
    )(counts, normed, w_qkv)


def early_kernel(layer, counts, *refs):
    entering, refs = refs[:-5], refs[-5:]
    gains, w_qkv, out, held, arrivals = refs
    segment = lax.axis_index("segment")
    head = lax.axis_index("head")

    @pl.when((segment == lax.axis_size("segment") - 1) & (layer < counts[segment]))
    def _():
        width = out.shape[1]
        pieces = arrivals.shape[0]
        half = w_qkv.shape[2] // 2
        depth = 2 * half // pieces
        source = w_qkv.at[0, layer, :, pl.ds(w_qkv.shape[3] - width, width)]
        copies = []
        for index in range(pieces):
            side = head if index * depth < half else 1 - head
            at = pl.multiple_of(side * half + index * depth % half, depth)
            copies.append(
                fetch(source.at[pl.ds(at, depth)], held.at[index], arrivals.at[index])
            )
        if len(entering) == 2:
            rows = [entering[0][...], entering[1][...]]
        else:
            before, mine, theirs = entering
            rows = [before[0] + (mine[0] + theirs[1]), before[1] + (mine[1] + theirs[0])]
        squares = jnp.sum(rows[0] * rows[0], axis=-1, keepdims=True)
        squares = squares + jnp.sum(rows[1] * rows[1], axis=-1, keepdims=True)
        scale = lax.rsqrt(squares / (2 * half) + TINY)
        normed = []
        for side, part in ((head, rows[0]), (1 - head, rows[1])):
            at = pl.multiple_of(side * half, half)
            gain = gains[0, layer : layer + 1, pl.ds(at, half)]
            normed.append((part * scale * gain).astype(jnp.bfloat16))
        made = 0.0
        for index in range(pieces):
            copies[index].wait()
            at = index * depth % half
            made += dot(normed[index * depth // half][:, at : at + depth], held[index])
        out[...] = made.astype(jnp.bfloat16).astype(jnp.float32)


def early_key_value(layer, entering, weights, width):
    counts, gains, w_qkv, _ = weights
    pieces = 4
    return pl.pallas_call(
        functools.partial(early_kernel, layer),
        out_shape=jax.ShapeDtypeStruct((entering[0].shape[-2], width), jnp.float32),
        in_specs=[SMEM] + [VMEM] * (len(entering) + 1) + [HBM],
        out_specs=VMEM,
        scratch_shapes=[
            pltpu.VMEM((pieces, w_qkv.shape[2] // pieces, width), jnp.bfloat16),
            pltpu.SemaphoreType.DMA((pieces,)),
        ],
        cost_estimate=SMALL_COST,
        compiler_params=pltpu.CompilerParams(vmem_limit_bytes=FORWARD_VMEM),
        name=f"early_l{layer}",
    )(counts, *entering, gains, w_qkv)


def finish_kernel(step, spans, layer, n_after, counts, rows, keep, got, *refs):
    grown = refs[n_after]
    segment = lax.axis_index("segment")
    active = is_active(step, spans)

    @pl.when(active & (layer < counts[segment]))
    def _():
        grown[...] = rows[0] + (keep[...] + got[...])

    @pl.when(active & (layer >= counts[segment]))
    def _():
        grown[...] = rows[0]


def finish(step, spans, layer, counts, rows, keep, got, after):
    return pl.pallas_call(
        functools.partial(finish_kernel, step, spans, layer, len(after)),
        out_shape=jax.ShapeDtypeStruct(keep.shape, jnp.float32),
        in_specs=[SMEM] + [VMEM] * 3 + [ANY] * len(after),
        out_specs=VMEM,
        cost_estimate=SMALL_COST,
        compiler_params=pltpu.CompilerParams(vmem_limit_bytes=KEY_VALUE_VMEM),
        name=f"finish_s{step}",
    )(counts, rows, keep, got, *after)


def join_kernel(n_after, rows, mine, theirs, *refs):
    refs[n_after][...] = rows[0] + (mine[0] + theirs[1])


def join(rows, mine, theirs, after):
    return pl.pallas_call(
        functools.partial(join_kernel, len(after)),
        out_shape=jax.ShapeDtypeStruct(rows.shape[1:], jnp.float32),
        in_specs=[VMEM] * 3 + [ANY] * len(after),
        out_specs=VMEM,
        cost_estimate=SMALL_COST,
        compiler_params=pltpu.CompilerParams(vmem_limit_bytes=KEY_VALUE_VMEM),
        name="join",
    )(rows, mine, theirs, *after)


def deliver_kernel(segments, spans, slots, *refs):
    fasts, refs = refs[:slots], refs[slots:]
    made, (out, own, out_held, own_held, arrivals, leavings) = refs[:-6], refs[-6:]
    share = own.shape[2]
    begin = pl.multiple_of(lax.axis_index("tok") * share, share)
    pairs = [(own_held.at[layer], own.at[layer]) for layer in range(slots)]
    pairs += [(out_held.at[span], out.at[span]) for span in range(spans)]
    for layer in range(slots):
        fetch(fasts[layer].at[:, pl.ds(begin, share)], own_held.at[layer], arrivals.at[layer])
    for span in range(spans):
        for index in range(segments):

            @pl.when(lax.axis_index("segment") == index)
            def _():
                fetch(made[index + span], out_held.at[span], arrivals.at[slots + span])

    copies = []
    for index, (held, target) in enumerate(pairs):
        pltpu.make_async_copy(held, held, arrivals.at[index]).wait()
        copies.append(fetch(held, target, leavings.at[index]))
    for copy in copies:
        copy.wait()


def deliver(fasts, made, segments, spans, share):
    kinds, _, width = fasts[0].shape
    out = (spans,) + made[0].shape
    own = (len(fasts), kinds, share, width)
    return pl.pallas_call(
        functools.partial(deliver_kernel, segments, spans, len(fasts)),
        out_shape=(
            jax.ShapeDtypeStruct(out, jnp.float32),
            jax.ShapeDtypeStruct(own, jnp.float32),
        ),
        in_specs=[ANY] * (len(fasts) + len(made)),
        out_specs=(ANY, ANY),
        scratch_shapes=[
            pltpu.VMEM(out, jnp.float32),
            pltpu.VMEM(own, jnp.float32),
            pltpu.SemaphoreType.DMA((len(fasts) + spans,)),
            pltpu.SemaphoreType.DMA((len(fasts) + spans,)),
        ],
        cost_estimate=SMALL_COST,
        compiler_params=pltpu.CompilerParams(vmem_limit_bytes=FORWARD_VMEM),
        name="deliver",
    )(*fasts, *made)


def update_kernel(layer, n_pieces, fast_all, *refs):
    pieces = refs[:n_pieces]
    fast_new, fast, keys, values, rounded, arrivals, leavings = refs[n_pieces:]
    source = fast_all.at[0, layer, 0] if len(fast_all.shape) == 6 else fast_all
    copies = [fetch(source.at[kind], fast.at[kind], arrivals.at[kind]) for kind in range(3)]
    head_size = keys.shape[1]
    head_scale = head_size**-0.5
    begin = 0
    for piece in pieces:
        at = slice(begin, begin + piece.shape[0])
        keys[at] = piece[:, :head_size].astype(jnp.bfloat16)
        values[at] = piece[:, head_size:].astype(jnp.bfloat16)
        begin += piece.shape[0]

    def ready(kind):
        copies[kind].wait()
        rounded[kind] = fast[kind].astype(jnp.bfloat16)

    total = keys.shape[0]
    chunk = min(total, CHUNK_TOKENS)
    made = ([], [], [])
    for begin in range(0, total, chunk):
        key_rows = keys[begin : begin + chunk]
        value_rows = values[begin : begin + chunk]
        if begin == 0:
            ready(0)
        gate = dot(key_rows, rounded[0]) * head_scale
        if begin == 0:
            ready(1)
        lift = dot(key_rows, rounded[1]) * head_scale
        logistic = jax.nn.sigmoid(gate)
        act = gate * logistic
        made[2].append((value_rows, (act * lift).astype(jnp.bfloat16)))
        if begin == 0:
            ready(2)
        up = dot(value_rows, rounded[2]) * -head_scale
        made[1].append((key_rows, (up * act).astype(jnp.bfloat16)))
        slope = logistic * (1.0 + gate * (1.0 - logistic))
        made[0].append((key_rows, (up * lift * slope).astype(jnp.bfloat16)))
    sums = [sum(dot_over_rows(left, right) for left, right in pairs) for pairs in made]
    out_copies = []
    for kind, sign in enumerate((head_scale, head_scale, -head_scale)):
        grad = sums[kind] * sign
        mean = jnp.mean(grad * grad)
        rate = STEP_RATE * lax.rsqrt(mean + TINY)
        fast[kind] = fast[kind] - grad * rate
        out_copies.append(fetch(fast.at[kind], fast_new.at[kind], leavings.at[kind]))
    for copy in out_copies:
        copy.wait()


def update(layer, pieces, fast):
    total = sum(piece.shape[0] for piece in pieces)
    shape = fast.shape[-3:]
    return pl.pallas_call(
        functools.partial(update_kernel, layer, len(pieces)),
        out_shape=jax.ShapeDtypeStruct(shape, jnp.float32),
        in_specs=[HBM] + [VMEM] * len(pieces),
        out_specs=HBM,
        scratch_shapes=[
            pltpu.VMEM(shape, jnp.float32),
            pltpu.VMEM((total, shape[1]), jnp.bfloat16),
            pltpu.VMEM((total, shape[1]), jnp.bfloat16),
            pltpu.VMEM(shape, jnp.bfloat16),
            pltpu.SemaphoreType.DMA((3,)),
            pltpu.SemaphoreType.DMA((3,)),
        ],
        cost_estimate=LARGE_COST,
        compiler_params=pltpu.CompilerParams(vmem_limit_bytes=UPDATE_VMEM),
        input_output_aliases={0: 0} if len(fast.shape) == 3 else {},
        name=f"update_l{layer}",
    )(fast, *pieces)


def make_send(sections):
    tok_size = lax.axis_size("tok")
    head_size = lax.axis_size("head")

    def flat(segment, tok, head):
        return (segment * tok_size + tok) * head_size + head

    def send(block, move):
        route = []
        for segment in sections:
            for tok in range(tok_size):
                for head in range(head_size):
                    target = move(segment, tok, head)
                    if target is not None:
                        route.append((flat(segment, tok, head), flat(*target)))
        return lax.ppermute(block, AXES, route)

    return send


def swap_head(send, block):
    return send(block, lambda s, k, h: (s, k, 1 - h))


def gather_near(send, block):
    if lax.axis_size("tok") != 4:
        return [lax.all_gather(block, "tok", axis=0, tiled=True)]
    first = send(block, lambda s, k, h: (s, k ^ 1, h))
    second = send(block, lambda s, k, h: (s, k ^ 2, h))
    return [block, first, second]


def gather_far(send, near):
    if len(near) == 1:
        return near
    cut = near[0].shape[0] // 2
    top = send(near[1][:cut], lambda s, k, h: (s, k ^ 2, h))
    low = send(near[2][cut:], lambda s, k, h: (s, k ^ 1, h))
    return near + [top, low]


def one_layer(fast, layer):
    return fast[0, layer, 0] if len(fast.shape) == 6 else fast


def body(stream, counts, norm_gain, w_qkv, w_out, fast_init):
    segments = lax.axis_size("segment")
    segment = lax.axis_index("segment")
    spans = stream.shape[0]
    slots = fast_init.shape[1]
    head_size = fast_init.shape[4]
    width = 2 * head_size
    fasts = [fast_init for layer in range(slots)]
    weights = [counts, norm_gain, w_qkv, w_out]
    steps = segments + spans - 1
    count = lax.dynamic_index_in_dim(counts, segment, 0, keepdims=False)

    def update_branch(step, depth, send):
        def run(block, norms, fasts):
            blocks = [block]
            for layer in range(1, depth):
                blocks.append(
                    key_value(step, layer, spans, counts, norms[layer - 1], w_qkv, width)
                )
            near = [gather_near(send, block) for block in blocks[:depth]]
            changed = [update(k, gather_far(send, near[k]), fasts[k]) for k in range(depth)]
            return changed + [one_layer(fasts[k], k) for k in range(depth, slots)]

        return run

    def last_branch(depth, send):
        def run(own, fasts, weights):
            if depth == 0:
                return jnp.zeros_like(own), fasts
            state = [own, swap_head(send, own)]
            near = []
            for layer in range(depth):
                last = layer > 0 and layer == depth - 1
                block = early_key_value(layer, state, weights, width)
                near.append(gather_near(send, block))
                made = forward(
                    steps - 1, layer, spans, last, state, weights, fasts[layer], [block]
                )
                rows = made[0]
                if layer > 0 and len(near[layer]) > 1:
                    *tied, rows = lax.optimization_barrier((*near[layer][1:], rows))
                    near[layer] = near[layer][:1] + tied
                state = [rows, made[2], swap_head(send, made[3] if last else made[2])]
            changed = [update(k, gather_far(send, near[k]), fasts[k]) for k in range(depth)]
            if depth == 1:
                grown = join(*state, changed[-1:])
            else:
                grown = finish(
                    steps - 1, spans, depth - 1, weights[0], *state, changed[-1:]
                )
            return grown, changed + fasts[depth:]

        return run

    grown_all = []
    own = stream[0]
    for step in range(steps - 1):
        send = make_send([s for s in range(segments) if 0 <= step - s < spans])
        active = (segment <= step) & (segment > step - spans)
        depth = jnp.where(active, count, 0)
        state = [own, swap_head(send, own)]
        blocks = []
        norms = []
        for layer in range(slots):
            last = layer == slots - 1
            made = forward(step, layer, spans, last, state, weights, fasts[layer], blocks)
            rows, normed = made[:2]
            got = swap_head(send, made[3] if last else made[2])
            state = [rows, made[2], got]
            if layer == 0:
                blocks.append(key_value(step, layer, spans, counts, normed, w_qkv, width))
            else:
                norms.append(normed)
        grown = finish(step, spans, slots - 1, counts, *state, blocks)
        grown_all.append(grown)
        arrived = send(grown, lambda s, k, h: (s + 1, k, h) if s + 1 < segments else None)
        branches = [update_branch(step, k, send) for k in range(slots + 1)]
        fasts = lax.switch(depth, branches, blocks[0], norms, fasts)
        own, fasts = lax.optimization_barrier((arrived, fasts))
        if step + 1 < spans:
            own = jnp.where(segment == 0, stream[step + 1], own)

    send = make_send([segments - 1])
    depth = jnp.where(segment == segments - 1, count, 0)
    branches = [last_branch(k, send) for k in range(slots + 1)]
    grown, fasts = lax.switch(depth, branches, own, fasts, weights)
    grown_all.append(grown)
    row_share = head_size // lax.axis_size("tok")
    results, rows = deliver(fasts, grown_all, segments, spans, row_share)
    return (results[None], rows[None, :, None])


def solution(mesh):
    in_specs = (
        P(None, "tok", "head"),
        P(),
        P("segment", None, None),
        P("segment", None, None, "head"),
        P("segment", None, "head", None),
        P("segment", None, "head", None, None, None),
    )
    out_specs = (P("segment", None, "tok", "head"), P("segment", None, "head", None, "tok", None))
    return jax.shard_map(body, mesh=mesh, in_specs=in_specs, out_specs=out_specs, check_vma=False)
```

```python
import functools

import jax
import jax.numpy as jnp
from jax import lax
from jax.experimental import pallas as pl
from jax.experimental.pallas import tpu as pltpu
from jax.sharding import PartitionSpec as P

STEP_RATE = 0.5
TINY = 1e-06
AXES = ("segment", "tok", "head")
MIB = 1024 * 1024
FORWARD_VMEM = 48 * MIB
KEY_VALUE_VMEM = 4 * MIB
UPDATE_VMEM = 28 * MIB
CHUNK_TOKENS = 512

VMEM = pl.BlockSpec(memory_space=pltpu.VMEM)
SMEM = pl.BlockSpec(memory_space=pltpu.SMEM)
ANY = pl.BlockSpec(memory_space=pl.ANY)
HBM = pl.BlockSpec(memory_space=pltpu.HBM)
LARGE_COST = pl.CostEstimate(flops=2**34, bytes_accessed=2**27, transcendentals=0)
SMALL_COST = pl.CostEstimate(flops=1024, bytes_accessed=1024, transcendentals=0)


def dot(left, right):
    return jnp.dot(left, right, preferred_element_type=jnp.float32)


def dot_over_rows(left, right):
    return lax.dot_general(
        left, right, (((0,), (0,)), ((), ())), preferred_element_type=jnp.float32
    )


def is_active(step, spans):
    segment = lax.axis_index("segment")
    return (segment <= step) & (segment > step - spans)


def fetch(source, target, arrival):
    copy = pltpu.make_async_copy(source, target, arrival)
    copy.start()
    return copy


def forward_kernel(step, layer, spans, last, n_after, *refs):
    counts, refs = refs[0], refs[1:]
    n_enter = 3 if layer > 0 else 2
    entering, refs = refs[:n_enter], refs[n_enter:]
    gains, w_qkv, w_out, fast = refs[:4]
    outs, scratch = refs[4 + n_after : -4], refs[-4:]
    w_query, w_mix, fast_here, arrivals = scratch
    rows, normed = outs[:2]
    head = lax.axis_index("head")
    active = is_active(step, spans)
    run = active & (layer < counts[lax.axis_index("segment")])
    half = rows.shape[2]
    head_size = w_mix.shape[0]

    def assemble():
        if layer == 0:
            rows[0] = entering[0][...]
            rows[1] = entering[1][...]
        else:
            held, mine, theirs = entering
            rows[0] = held[0] + (mine[0] + theirs[1])
            rows[1] = held[1] + (mine[1] + theirs[0])

    @pl.when(run)
    def _():
        keep_at = pl.multiple_of(head * half, half)
        send_at = pl.multiple_of((1 - head) * half, half)
        query_copies = [
            fetch(
                w_qkv.at[0, layer, pl.ds(at, half), pl.ds(0, head_size)],
                w_query.at[pl.ds(at, half)],
                arrivals.at[slot],
            )
            for at, slot in ((keep_at, 0), (send_at, 5))
        ]
        fast_from = fast.at[0, layer, 0] if len(fast.shape) == 6 else fast
        fast_copies = [
            fetch(fast_from.at[kind], fast_here.at[kind], arrivals.at[1 + kind])
            for kind in range(3)
        ]
        mix_copy = fetch(w_out.at[0, layer], w_mix, arrivals.at[4])
        assemble()
        squares = jnp.sum(rows[0] * rows[0], axis=-1, keepdims=True)
        squares = squares + jnp.sum(rows[1] * rows[1], axis=-1, keepdims=True)
        scale = lax.rsqrt(squares / (2 * half) + TINY)
        gain_keep = gains[0, layer : layer + 1, pl.ds(keep_at, half)]
        gain_send = gains[0, layer : layer + 1, pl.ds(send_at, half)]
        normed[0] = (rows[0] * scale * gain_keep).astype(jnp.bfloat16)
        normed[1] = (rows[1] * scale * gain_send).astype(jnp.bfloat16)
        query_copies[0].wait()
        query = dot(normed[0], w_query[pl.ds(keep_at, half)])
        query_copies[1].wait()
        query += dot(normed[1], w_query[pl.ds(send_at, half)])
        query = query.astype(jnp.bfloat16)
        head_scale = head_size**-0.5
        fast_copies[0].wait()
        gate = dot(query, fast_here[0].astype(jnp.bfloat16)) * head_scale
        fast_copies[1].wait()
        lift = dot(query, fast_here[1].astype(jnp.bfloat16)) * head_scale
        hidden = (gate * jax.nn.sigmoid(gate) * lift).astype(jnp.bfloat16)
        fast_copies[2].wait()
        answer = (
            lax.dot_general(
                hidden,
                fast_here[2].astype(jnp.bfloat16),
                (((1,), (1,)), ((), ())),
                preferred_element_type=jnp.float32,
            )
            * head_scale
        )
        mean = jnp.mean(answer * answer, axis=-1, keepdims=True)
        answer = (answer * lax.rsqrt(mean + TINY)).astype(jnp.bfloat16)
        mix_copy.wait()
        kept = dot(answer, w_mix[:, pl.ds(keep_at, half)])
        given = dot(answer, w_mix[:, pl.ds(send_at, half)])
        if last:
            outs[2][...] = kept
            outs[3][...] = given
        else:
            outs[2][0] = kept
            outs[2][1] = given

    @pl.when(active & jnp.logical_not(run))
    def _():
        assemble()


def forward(step, layer, spans, last, entering, weights, fast, after):
    counts, gains, w_qkv, w_out = weights
    tokens, half = entering[0].shape[-2:]
    head_size = w_out.shape[2]
    rows = jax.ShapeDtypeStruct((2, tokens, half), jnp.float32)
    normed = jax.ShapeDtypeStruct((2, tokens, half), jnp.bfloat16)
    part = jax.ShapeDtypeStruct((tokens, half), jnp.float32)
    return pl.pallas_call(
        functools.partial(forward_kernel, step, layer, spans, last, len(after)),
        out_shape=(rows, normed) + ((part, part) if last else (rows,)),
        in_specs=[SMEM] + [VMEM] * (len(entering) + 1) + [HBM] * 3 + [ANY] * len(after),
        out_specs=[VMEM] * (4 if last else 3),
        scratch_shapes=[
            pltpu.VMEM((2 * half, head_size), jnp.bfloat16),
            pltpu.VMEM((head_size, 2 * half), jnp.bfloat16),
            pltpu.VMEM(fast.shape[-3:], jnp.float32),
            pltpu.SemaphoreType.DMA((6,)),
        ],
        cost_estimate=SMALL_COST,
        compiler_params=pltpu.CompilerParams(vmem_limit_bytes=FORWARD_VMEM),
        name=f"forward_s{step}_l{layer}",
    )(counts, *entering, gains, w_qkv, w_out, fast, *after)


def key_value_kernel(step, layer, spans, counts, normed, w_qkv, out, held, arrivals):
    head = lax.axis_index("head")
    run = is_active(step, spans) & (layer < counts[lax.axis_index("segment")])

    @pl.when(run)
    def _():
        half = normed.shape[2]
        width = out.shape[1]
        begin = w_qkv.shape[3] - width
        pieces = arrivals.shape[0]
        depth = 2 * half // pieces
        source = w_qkv.at[0, layer, :, pl.ds(begin, width)]
        copies = []
        for index in range(pieces):
            side = head if index * depth < half else 1 - head
            at = pl.multiple_of(side * half + index * depth % half, depth)
            copies.append(
                fetch(source.at[pl.ds(at, depth)], held.at[index], arrivals.at[index])
            )
        made = 0.0
        for index in range(pieces):
            copies[index].wait()
            at = index * depth % half
            made += dot(normed[index * depth // half, :, at : at + depth], held[index])
        out[...] = made.astype(jnp.bfloat16).astype(jnp.float32)


def key_value(step, layer, spans, counts, normed, w_qkv, width):
    pieces = 8
    return pl.pallas_call(
        functools.partial(key_value_kernel, step, layer, spans),
        out_shape=jax.ShapeDtypeStruct((normed.shape[1], width), jnp.float32),
        in_specs=[SMEM, VMEM, HBM],
        out_specs=VMEM,
        scratch_shapes=[
            pltpu.VMEM((pieces, w_qkv.shape[2] // pieces, width), jnp.bfloat16),
            pltpu.SemaphoreType.DMA((pieces,)),
        ],
        cost_estimate=SMALL_COST,
        compiler_params=pltpu.CompilerParams(vmem_limit_bytes=FORWARD_VMEM),
        name=f"keyvalue_s{step}_l{layer}",
    )(counts, normed, w_qkv)


def early_kernel(layer, counts, *refs):
    entering, refs = refs[:-5], refs[-5:]
    gains, w_qkv, out, held, arrivals = refs
    segment = lax.axis_index("segment")
    head = lax.axis_index("head")

    @pl.when((segment == lax.axis_size("segment") - 1) & (layer < counts[segment]))
    def _():
        width = out.shape[1]
        pieces = arrivals.shape[0]
        half = w_qkv.shape[2] // 2
        depth = 2 * half // pieces
        source = w_qkv.at[0, layer, :, pl.ds(w_qkv.shape[3] - width, width)]
        copies = []
        for index in range(pieces):
            side = head if index * depth < half else 1 - head
            at = pl.multiple_of(side * half + index * depth % half, depth)
            copies.append(
                fetch(source.at[pl.ds(at, depth)], held.at[index], arrivals.at[index])
            )
        if len(entering) == 2:
            rows = [entering[0][...], entering[1][...]]
        else:
            before, mine, theirs = entering
            rows = [before[0] + (mine[0] + theirs[1]), before[1] + (mine[1] + theirs[0])]
        squares = jnp.sum(rows[0] * rows[0], axis=-1, keepdims=True)
        squares = squares + jnp.sum(rows[1] * rows[1], axis=-1, keepdims=True)
        scale = lax.rsqrt(squares / (2 * half) + TINY)
        normed = []
        for side, part in ((head, rows[0]), (1 - head, rows[1])):
            at = pl.multiple_of(side * half, half)
            gain = gains[0, layer : layer + 1, pl.ds(at, half)]
            normed.append((part * scale * gain).astype(jnp.bfloat16))
        made = 0.0
        for index in range(pieces):
            copies[index].wait()
            at = index * depth % half
            made += dot(normed[index * depth // half][:, at : at + depth], held[index])
        out[...] = made.astype(jnp.bfloat16).astype(jnp.float32)


def early_key_value(layer, entering, weights, width):
    counts, gains, w_qkv, _ = weights
    pieces = 8
    return pl.pallas_call(
        functools.partial(early_kernel, layer),
        out_shape=jax.ShapeDtypeStruct((entering[0].shape[-2], width), jnp.float32),
        in_specs=[SMEM] + [VMEM] * (len(entering) + 1) + [HBM],
        out_specs=VMEM,
        scratch_shapes=[
            pltpu.VMEM((pieces, w_qkv.shape[2] // pieces, width), jnp.bfloat16),
            pltpu.SemaphoreType.DMA((pieces,)),
        ],
        cost_estimate=SMALL_COST,
        compiler_params=pltpu.CompilerParams(vmem_limit_bytes=FORWARD_VMEM),
        name=f"early_l{layer}",
    )(counts, *entering, gains, w_qkv)


def finish_kernel(step, spans, layer, n_after, counts, rows, keep, got, *refs):
    grown = refs[n_after]
    segment = lax.axis_index("segment")
    active = is_active(step, spans)

    @pl.when(active & (layer < counts[segment]))
    def _():
        grown[...] = rows[0] + (keep[...] + got[...])

    @pl.when(active & (layer >= counts[segment]))
    def _():
        grown[...] = rows[0]


def finish(step, spans, layer, counts, rows, keep, got, after):
    return pl.pallas_call(
        functools.partial(finish_kernel, step, spans, layer, len(after)),
        out_shape=jax.ShapeDtypeStruct(keep.shape, jnp.float32),
        in_specs=[SMEM] + [VMEM] * 3 + [ANY] * len(after),
        out_specs=VMEM,
        cost_estimate=SMALL_COST,
        compiler_params=pltpu.CompilerParams(vmem_limit_bytes=KEY_VALUE_VMEM),
        name=f"finish_s{step}",
    )(counts, rows, keep, got, *after)


def join_kernel(n_after, rows, mine, theirs, *refs):
    refs[n_after][...] = rows[0] + (mine[0] + theirs[1])


def join(rows, mine, theirs, after):
    return pl.pallas_call(
        functools.partial(join_kernel, len(after)),
        out_shape=jax.ShapeDtypeStruct(rows.shape[1:], jnp.float32),
        in_specs=[VMEM] * 3 + [ANY] * len(after),
        out_specs=VMEM,
        cost_estimate=SMALL_COST,
        compiler_params=pltpu.CompilerParams(vmem_limit_bytes=KEY_VALUE_VMEM),
        name="join",
    )(rows, mine, theirs, *after)


def deliver_kernel(segments, spans, slots, *refs):
    fasts, refs = refs[:slots], refs[slots:]
    made, (out, own, out_held, own_held, arrivals, leavings) = refs[:-6], refs[-6:]
    share = own.shape[2]
    begin = pl.multiple_of(lax.axis_index("tok") * share, share)
    pairs = [(own_held.at[layer], own.at[layer]) for layer in range(slots)]
    pairs += [(out_held.at[span], out.at[span]) for span in range(spans)]
    for layer in range(slots):
        fetch(fasts[layer].at[:, pl.ds(begin, share)], own_held.at[layer], arrivals.at[layer])
    for span in range(spans):
        for index in range(segments):

            @pl.when(lax.axis_index("segment") == index)
            def _():
                fetch(made[index + span], out_held.at[span], arrivals.at[slots + span])

    copies = []
    for index, (held, target) in enumerate(pairs):
        pltpu.make_async_copy(held, held, arrivals.at[index]).wait()
        copies.append(fetch(held, target, leavings.at[index]))
    for copy in copies:
        copy.wait()


def deliver(fasts, made, segments, spans, share):
    kinds, _, width = fasts[0].shape
    out = (spans,) + made[0].shape
    own = (len(fasts), kinds, share, width)
    return pl.pallas_call(
        functools.partial(deliver_kernel, segments, spans, len(fasts)),
        out_shape=(
            jax.ShapeDtypeStruct(out, jnp.float32),
            jax.ShapeDtypeStruct(own, jnp.float32),
        ),
        in_specs=[ANY] * (len(fasts) + len(made)),
        out_specs=(ANY, ANY),
        scratch_shapes=[
            pltpu.VMEM(out, jnp.float32),
            pltpu.VMEM(own, jnp.float32),
            pltpu.SemaphoreType.DMA((len(fasts) + spans,)),
            pltpu.SemaphoreType.DMA((len(fasts) + spans,)),
        ],
        cost_estimate=SMALL_COST,
        compiler_params=pltpu.CompilerParams(vmem_limit_bytes=FORWARD_VMEM),
        name="deliver",
    )(*fasts, *made)


def update_kernel(layer, n_pieces, fast_all, *refs):
    pieces = refs[:n_pieces]
    fast_new, fast, keys, values, rounded, arrivals, leavings = refs[n_pieces:]
    source = fast_all.at[0, layer, 0] if len(fast_all.shape) == 6 else fast_all
    copies = [fetch(source.at[kind], fast.at[kind], arrivals.at[kind]) for kind in range(3)]
    head_size = keys.shape[1]
    head_scale = head_size**-0.5
    begin = 0
    for piece in pieces:
        at = slice(begin, begin + piece.shape[0])
        keys[at] = piece[:, :head_size].astype(jnp.bfloat16)
        values[at] = piece[:, head_size:].astype(jnp.bfloat16)
        begin += piece.shape[0]

    def ready(kind):
        copies[kind].wait()
        rounded[kind] = fast[kind].astype(jnp.bfloat16)

    total = keys.shape[0]
    chunk = min(total, CHUNK_TOKENS)
    made = ([], [], [])
    for begin in range(0, total, chunk):
        key_rows = keys[begin : begin + chunk]
        value_rows = values[begin : begin + chunk]
        if begin == 0:
            ready(0)
        gate = dot(key_rows, rounded[0]) * head_scale
        if begin == 0:
            ready(1)
        lift = dot(key_rows, rounded[1]) * head_scale
        logistic = jax.nn.sigmoid(gate)
        act = gate * logistic
        made[2].append((value_rows, (act * lift).astype(jnp.bfloat16)))
        if begin == 0:
            ready(2)
        up = dot(value_rows, rounded[2]) * -head_scale
        made[1].append((key_rows, (up * act).astype(jnp.bfloat16)))
        slope = logistic * (1.0 + gate * (1.0 - logistic))
        made[0].append((key_rows, (up * lift * slope).astype(jnp.bfloat16)))
    sums = [sum(dot_over_rows(left, right) for left, right in pairs) for pairs in made]
    out_copies = []
    for kind, sign in enumerate((head_scale, head_scale, -head_scale)):
        grad = sums[kind] * sign
        mean = jnp.mean(grad * grad)
        rate = STEP_RATE * lax.rsqrt(mean + TINY)
        fast[kind] = fast[kind] - grad * rate
        out_copies.append(fetch(fast.at[kind], fast_new.at[kind], leavings.at[kind]))
    for copy in out_copies:
        copy.wait()


def update(layer, pieces, fast):
    total = sum(piece.shape[0] for piece in pieces)
    shape = fast.shape[-3:]
    return pl.pallas_call(
        functools.partial(update_kernel, layer, len(pieces)),
        out_shape=jax.ShapeDtypeStruct(shape, jnp.float32),
        in_specs=[HBM] + [VMEM] * len(pieces),
        out_specs=HBM,
        scratch_shapes=[
            pltpu.VMEM(shape, jnp.float32),
            pltpu.VMEM((total, shape[1]), jnp.bfloat16),
            pltpu.VMEM((total, shape[1]), jnp.bfloat16),
            pltpu.VMEM(shape, jnp.bfloat16),
            pltpu.SemaphoreType.DMA((3,)),
            pltpu.SemaphoreType.DMA((3,)),
        ],
        cost_estimate=LARGE_COST,
        compiler_params=pltpu.CompilerParams(vmem_limit_bytes=UPDATE_VMEM),
        input_output_aliases={0: 0} if len(fast.shape) == 3 else {},
        name=f"update_l{layer}",
    )(fast, *pieces)


def make_send(sections):
    tok_size = lax.axis_size("tok")
    head_size = lax.axis_size("head")

    def flat(segment, tok, head):
        return (segment * tok_size + tok) * head_size + head

    def send(block, move):
        route = []
        for segment in sections:
            for tok in range(tok_size):
                for head in range(head_size):
                    target = move(segment, tok, head)
                    if target is not None:
                        route.append((flat(segment, tok, head), flat(*target)))
        return lax.ppermute(block, AXES, route)

    return send


def swap_head(send, block):
    return send(block, lambda s, k, h: (s, k, 1 - h))


def gather_near(send, block):
    if lax.axis_size("tok") != 4:
        return [lax.all_gather(block, "tok", axis=0, tiled=True)]
    first = send(block, lambda s, k, h: (s, k ^ 1, h))
    second = send(block, lambda s, k, h: (s, k ^ 2, h))
    return [block, first, second]


def gather_far(send, near):
    if len(near) == 1:
        return near
    cut = near[0].shape[0] // 2
    top = send(near[1][:cut], lambda s, k, h: (s, k ^ 2, h))
    low = send(near[2][cut:], lambda s, k, h: (s, k ^ 1, h))
    return near + [top, low]


def one_layer(fast, layer):
    return fast[0, layer, 0] if len(fast.shape) == 6 else fast


def body(stream, counts, norm_gain, w_qkv, w_out, fast_init):
    segments = lax.axis_size("segment")
    segment = lax.axis_index("segment")
    spans = stream.shape[0]
    slots = fast_init.shape[1]
    head_size = fast_init.shape[4]
    width = 2 * head_size
    fasts = [fast_init for layer in range(slots)]
    weights = [counts, norm_gain, w_qkv, w_out]
    steps = segments + spans - 1
    count = lax.dynamic_index_in_dim(counts, segment, 0, keepdims=False)

    def update_branch(step, depth, send):
        def run(block, norms, fasts):
            blocks = [block]
            for layer in range(1, depth):
                blocks.append(
                    key_value(step, layer, spans, counts, norms[layer - 1], w_qkv, width)
                )
            near = [gather_near(send, block) for block in blocks[:depth]]
            changed = [update(k, gather_far(send, near[k]), fasts[k]) for k in range(depth)]
            return changed + [one_layer(fasts[k], k) for k in range(depth, slots)]

        return run

    def last_branch(depth, send):
        def run(own, fasts, weights):
            if depth == 0:
                return jnp.zeros_like(own), fasts
            state = [own, swap_head(send, own)]
            near = []
            for layer in range(depth):
                last = layer > 0 and layer == depth - 1
                block = early_key_value(layer, state, weights, width)
                near.append(gather_near(send, block))
                made = forward(
                    steps - 1, layer, spans, last, state, weights, fasts[layer], [block]
                )
                rows = made[0]
                if layer > 0 and len(near[layer]) > 1:
                    *tied, rows = lax.optimization_barrier((*near[layer][1:], rows))
                    near[layer] = near[layer][:1] + tied
                state = [rows, made[2], swap_head(send, made[3] if last else made[2])]
            changed = [update(k, gather_far(send, near[k]), fasts[k]) for k in range(depth)]
            if depth == 1:
                grown = join(*state, changed[-1:])
            else:
                grown = finish(
                    steps - 1, spans, depth - 1, weights[0], *state, changed[-1:]
                )
            return grown, changed + fasts[depth:]

        return run

    grown_all = []
    own = stream[0]
    for step in range(steps - 1):
        send = make_send([s for s in range(segments) if 0 <= step - s < spans])
        active = (segment <= step) & (segment > step - spans)
        depth = jnp.where(active, count, 0)
        state = [own, swap_head(send, own)]
        blocks = []
        norms = []
        for layer in range(slots):
            last = layer == slots - 1
            made = forward(step, layer, spans, last, state, weights, fasts[layer], blocks)
            rows, normed = made[:2]
            got = swap_head(send, made[3] if last else made[2])
            state = [rows, made[2], got]
            if layer == 0:
                blocks.append(key_value(step, layer, spans, counts, normed, w_qkv, width))
            else:
                norms.append(normed)
        grown = finish(step, spans, slots - 1, counts, *state, blocks)
        grown_all.append(grown)
        arrived = send(grown, lambda s, k, h: (s + 1, k, h) if s + 1 < segments else None)
        branches = [update_branch(step, k, send) for k in range(slots + 1)]
        fasts = lax.switch(depth, branches, blocks[0], norms, fasts)
        own, fasts = lax.optimization_barrier((arrived, fasts))
        if step + 1 < spans:
            own = jnp.where(segment == 0, stream[step + 1], own)

    send = make_send([segments - 1])
    depth = jnp.where(segment == segments - 1, count, 0)
    branches = [last_branch(k, send) for k in range(slots + 1)]
    grown, fasts = lax.switch(depth, branches, own, fasts, weights)
    grown_all.append(grown)
    row_share = head_size // lax.axis_size("tok")
    results, rows = deliver(fasts, grown_all, segments, spans, row_share)
    return (results[None], rows[None, :, None])


def solution(mesh):
    in_specs = (
        P(None, "tok", "head"),
        P(),
        P("segment", None, None),
        P("segment", None, None, "head"),
        P("segment", None, "head", None),
        P("segment", None, "head", None, None, None),
    )
    out_specs = (P("segment", None, "tok", "head"), P("segment", None, "head", None, "tok", None))
    return jax.shard_map(body, mesh=mesh, in_specs=in_specs, out_specs=out_specs, check_vma=False)
```
